32 devices in a mesh: dp: 8 (over z, x), seq: 4 (over y, core).
Axes of the slice: x: 2, y: 2, z: 4, core: 2. Of those that a mesh axis runs over, the one named last changes fastest.
Arguments:
- qx: bfloat16 [4096, 1024], P(('dp', 'seq')), may hold values from -6 to 6
- queries: bfloat16 [4096, 1024], P(('dp', 'seq')), may hold values from -8 to 8
- keys: bfloat16 [1536, 1024], P('seq'), may hold values from -6 to 6
- values: bfloat16 [1536, 1024], P('seq'), may hold values from -6 to 6
- attn_out: bfloat16 [4096, 1024], P(('dp', 'seq')), may hold values from -3 to 3
- grad_out: bfloat16 [4096, 1024], P(('dp', 'seq')), may hold values from -24 to 24
- wq: bfloat16 [1024, 1024], replicated, may hold values from -0.1875 to 0.1875
Outputs:
- grad_input: bfloat16 [4096, 1024], P(('dp', 'seq'))
- grad_keys: bfloat16 [1536, 1024], P('seq')
- grad_values: bfloat16 [1536, 1024], P('seq')
- grad_weight: float32 [1024, 1024], P('dp', 'seq')
The draws below stay inside these ranges and needn't reach their ends.
All inputs are finite; a program needn't handle non-finite values.
Results may differ from the reference program's by a relative error of at most 0.014.
Values may be sent and summed in bfloat16 or wider, within the bound.
No kernel may reach another device: no remote copies, remote signals or barrier semaphores. Data moves between devices by JAX's collectives and lax.ppermute only.
A program may use at most 64 MiB of HBM per device.

```python
import math
import jax
import jax.numpy as jnp
from jax import lax

D = 1024
H = 16
HD = 64
SLAB = 512
QROWS = 4096
KEYS = 1536
N_DP = 8


def draw_queries(key, part):
    key = jax.random.fold_in(key, 1)
    base = jnp.clip(2.0 * jax.random.normal(key, (QROWS, D), jnp.float32), -8.0, 8.0)
    return base.astype(jnp.bfloat16)


def draw_keys(key, part):
    key = jax.random.fold_in(key, 2)
    base = jnp.clip(jax.random.normal(key, (KEYS, D), jnp.float32), -6.0, 6.0)
    return base.astype(jnp.bfloat16)


def block_scale(key, extent, cuts, low, largest):
    def one(position, blocks):
        heights = jax.random.uniform(jax.random.fold_in(jax.random.fold_in(key, 6), position), (blocks,), jnp.float32, low / len(cuts), largest / len(cuts))
        return jnp.repeat(jnp.exp(heights), extent[position] // blocks).reshape((-1,) + (1,) * (len(extent) - position - 1))

    factor_of = one(*cuts[0])
    for cut in cuts[1:]:
        factor_of = factor_of * one(*cut)
    return factor_of


def bell_draw(own_key, shape, spread, bound, cuts=(), kind=jnp.bfloat16):
    entries = jax.random.normal(own_key, shape, jnp.float32) * spread
    if len(cuts) > 0:
        entries = block_scale(own_key, shape, cuts, -0.22, 0.18) * entries
    return jnp.clip(entries, min=-bound, max=bound).astype(kind)


def setup_inputs(seed: int = 0) -> dict:
    streams_of = jax.random.split(jax.random.key(seed), 8)
    return {
        "qx": bell_draw(streams_of[0], (QROWS, D), 1.0, 6.0, ((0, 32),)),
        "queries": draw_queries(jax.random.fold_in(streams_of[7], 71), 0),
        "keys": draw_keys(jax.random.fold_in(streams_of[7], 71), 0),
        "values": bell_draw(streams_of[3], (KEYS, D), 1.0, 6.0, ((0, 4),)),
        "attn_out": bell_draw(streams_of[4], (QROWS, D), 0.5, 3.0, ((0, 32),)),
        "grad_out": bell_draw(streams_of[5], (QROWS, D), 4.0, 24.0, ((0, 32),)),
        "wq": bell_draw(streams_of[6], (D, D), D ** -0.5, 0.1875),
    }


def head_slab(query, grad, output, key_mat, val_mat, score_scale):
    scores = jnp.dot(query, key_mat.T) * score_scale
    top = lax.optimization_barrier(jnp.max(scores, axis=1, keepdims=True))
    lse = top + jnp.log(lax.optimization_barrier(jnp.sum(jnp.exp(scores - top), axis=1, keepdims=True)))
    probs = jnp.exp(scores - lse)
    probs_b = lax.optimization_barrier(probs.astype(jnp.bfloat16)).astype(jnp.float32)
    grad_probs = jnp.dot(grad, val_mat.T)
    delta = lax.optimization_barrier(jnp.sum(grad * output, axis=1, keepdims=True))
    grad_scores = (probs * (grad_probs - delta) * score_scale).astype(jnp.bfloat16)
    grad_scores = lax.optimization_barrier(grad_scores).astype(jnp.float32)
    grad_query = jnp.dot(grad_scores, key_mat).astype(jnp.bfloat16)
    value_part = jnp.dot(probs_b.T, grad).astype(jnp.bfloat16)
    key_part = jnp.dot(grad_scores.T, query).astype(jnp.bfloat16)
    return (grad_query, key_part, value_part)

def reference(qx, queries, keys, values, attn_out, grad_out, wq):
    score_scale = 1.0 / math.sqrt(HD)

    def split_rows(array):
        return array.astype(jnp.float32).reshape(N_DP, SLAB, H, HD).transpose(2, 0, 1, 3)

    def split_keys(array):
        return array.astype(jnp.float32).reshape(KEYS, H, HD).transpose(1, 0, 2)

    def one_head(items):
        query_h, grad_h, output_h, key_h, val_h = items

        def one_slab(inner):
            return head_slab(inner[0], inner[1], inner[2], key_h, val_h, score_scale)
        grad_query, key_parts, value_parts = lax.map(one_slab, (query_h, grad_h, output_h))
        key_total = lax.optimization_barrier(jnp.sum(key_parts.astype(jnp.float32), axis=0)).astype(jnp.bfloat16)
        value_total = lax.optimization_barrier(jnp.sum(value_parts.astype(jnp.float32), axis=0)).astype(jnp.bfloat16)
        return (grad_query, key_total, value_total)
    grad_query, grad_key_heads, grad_val_heads = lax.map(one_head, (split_rows(queries), split_rows(grad_out), split_rows(attn_out), split_keys(keys), split_keys(values)))
    grad_query = grad_query.transpose(1, 2, 0, 3).reshape(QROWS, D)
    grad_keys = grad_key_heads.transpose(1, 0, 2).reshape(KEYS, D)
    grad_values = grad_val_heads.transpose(1, 0, 2).reshape(KEYS, D)
    grad_input = jnp.dot(grad_query.astype(jnp.float32), wq.astype(jnp.float32).T).astype(jnp.bfloat16)
    grad_weight = jnp.dot(qx.astype(jnp.float32).T, grad_query.astype(jnp.float32))
    return (grad_input, grad_keys, grad_values, grad_weight)
```

```python
import functools
import math

import jax
import jax.numpy as jnp
from jax import lax
from jax.experimental import pallas as pl
from jax.experimental.pallas import tpu as pltpu
from jax.sharding import PartitionSpec as P

HD = 64
PAIR = 2 * HD
SCALE = 1.0 / math.sqrt(HD)
BF = jnp.bfloat16
F32 = jnp.float32
VMEM_LIMIT = 56 * 1024 * 1024


def dot(a, b, ca, cb):
    return lax.dot_general(a, b, (((ca,), (cb,)), ((), ())), preferred_element_type=F32)


def own_lanes(x, head):
    lane = lax.broadcasted_iota(jnp.int32, x.shape, 1)
    mine = lane < HD if head == 0 else lane >= HD
    return jnp.where(mine, x, jnp.zeros_like(x))


def delta_kernel(grad_ref, out_ref, delta_ref):
    prod = grad_ref[...].astype(F32) * out_ref[...].astype(F32)
    cols = prod.T
    heads = cols.shape[0] // HD
    for head in range(heads):
        part = jnp.sum(cols[head * HD : (head + 1) * HD], axis=0, keepdims=True)
        delta_ref[head // 2, head % 2] = part[0]


def delta_of(grad_out, attn_out):
    rows, cols = grad_out.shape
    return pl.pallas_call(
        delta_kernel,
        out_shape=jax.ShapeDtypeStruct((cols // PAIR, 2, rows), F32),
        compiler_params=pltpu.CompilerParams(vmem_limit_bytes=VMEM_LIMIT),
        cost_estimate=pl.CostEstimate(flops=4 * rows * cols, bytes_accessed=4 * rows * cols, transcendentals=0),
    )(grad_out, attn_out)


def probs_kernel(count, *refs):
    q_refs, k_ref = refs[:count], refs[count]
    p_ref, m_ref, lse_ref = refs[count + 1 :]
    q = jnp.concatenate([r[...] for r in q_refs], axis=0) * jnp.asarray(SCALE, BF)
    k = k_ref[...]
    for head in range(2):
        s = dot(own_lanes(k, head), q, 1, 1)
        top = jnp.max(s, axis=0, keepdims=True)
        p = jnp.exp(s - top)
        total = jnp.sum(p, axis=0, keepdims=True)
        p_ref[head] = p.astype(BF)
        m_ref[0, head] = top[0]
        lse_ref[0, head] = (top + jnp.log(total))[0]


def probs_of(q_pieces, keys):
    count = len(q_pieces)
    piece, cols = q_pieces[0].shape
    tokens = keys.shape[0]
    rows = piece * count
    pairs = cols // PAIR
    return pl.pallas_call(
        functools.partial(probs_kernel, count),
        grid=(pairs,),
        in_specs=[pl.BlockSpec((piece, PAIR), lambda i: (0, i))] * count
        + [pl.BlockSpec((tokens, PAIR), lambda i: (0, i))],
        out_specs=[
            pl.BlockSpec((2, tokens, rows), lambda i: (i, 0, 0)),
            pl.BlockSpec((1, 2, rows), lambda i: (i, 0, 0)),
            pl.BlockSpec((1, 2, rows), lambda i: (i, 0, 0)),
        ],
        out_shape=[
            jax.ShapeDtypeStruct((2 * pairs, tokens, rows), BF),
            jax.ShapeDtypeStruct((pairs, 2, rows), F32),
            jax.ShapeDtypeStruct((pairs, 2, rows), F32),
        ],
        compiler_params=pltpu.CompilerParams(vmem_limit_bytes=VMEM_LIMIT),
        cost_estimate=pl.CostEstimate(
            flops=2 * rows * tokens * cols,
            bytes_accessed=2 * rows * tokens * 2 * pairs,
            transcendentals=rows * tokens * 2 * pairs,
        ),
    )(*q_pieces, keys)


def grads_kernel(count, half_ref, *refs):
    q_refs, g_refs = refs[:count], refs[count : 2 * count]
    pa_ref, pb_ref, v_ref, kt_ref, w_ref, delta_ref, dkv_ref, dqt_ref = refs[2 * count :]
    rows = w_ref.shape[2]
    side = rows // 2
    w = w_ref[0]
    delta = delta_ref[0]
    v = v_ref[...]
    first = lax.broadcasted_iota(jnp.int32, (PAIR, rows), 0) < HD
    wide = jnp.where(first, w[0:1], w[1:2]).T
    q = jnp.concatenate([r[...] for r in q_refs], axis=0)
    g = jnp.concatenate([r[...] for r in g_refs], axis=0)
    qw = (q.astype(F32) * (wide * SCALE)).astype(BF)
    gw = (g.astype(F32) * wide).astype(BF)
    dk = jnp.zeros((v.shape[0], PAIR), F32)
    dv = jnp.zeros((v.shape[0], PAIR), F32)
    for half, p_ref in ((0, pa_ref), (1, pb_ref)):
        at = slice(half * side, (half + 1) * side)
        for head in range(2):
            p = p_ref[head]
            dp = dot(v, own_lanes(g[at], head), 1, 1)
            t = (p.astype(F32) * (dp - delta[head : head + 1, at])).astype(BF)
            dv = dv + dot(p, own_lanes(gw[at], head), 1, 0)
            dk = dk + dot(t, own_lanes(qw[at], head), 1, 0)
            dq = dot(kt_ref[head * HD : (head + 1) * HD], t, 1, 0)
            dq = dq * (w[head : head + 1, at] * SCALE)
            dqt_ref[head * HD : (head + 1) * HD, at] = dq.astype(BF)
    dkv_ref[0] = dk.astype(BF)
    dkv_ref[1] = dv.astype(BF)


def grads_of(half, q_pieces, g_pieces, pa, pb, values, keys_t, w, delta):
    count = len(q_pieces)
    piece, cols = q_pieces[0].shape
    tokens = values.shape[0]
    rows = piece * count
    steps = cols // PAIR // 2
    at = lambda i, h: h[0] * steps + i
    row_spec = pl.BlockSpec((piece, PAIR), lambda i, h: (0, at(i, h)))
    p_spec = pl.BlockSpec((2, tokens, rows // 2), lambda i, h: (at(i, h), 0, 0))
    stat_spec = pl.BlockSpec((1, 2, rows), lambda i, h: (at(i, h), 0, 0))
    return pl.pallas_call(
        functools.partial(grads_kernel, count),
        grid_spec=pltpu.PrefetchScalarGridSpec(
            num_scalar_prefetch=1,
            grid=(steps,),
            in_specs=[row_spec] * (2 * count)
            + [
                p_spec,
                p_spec,
                pl.BlockSpec((tokens, PAIR), lambda i, h: (0, at(i, h))),
                pl.BlockSpec((PAIR, tokens), lambda i, h: (at(i, h), 0)),
                stat_spec,
                stat_spec,
            ],
            out_specs=[
                pl.BlockSpec((2, tokens, PAIR), lambda i, h: (0, 0, i)),
                pl.BlockSpec((PAIR, rows), lambda i, h: (i, 0)),
            ],
        ),
        out_shape=[
            jax.ShapeDtypeStruct((2, tokens, cols // 2), BF),
            jax.ShapeDtypeStruct((cols // 2, rows), BF),
        ],
        compiler_params=pltpu.CompilerParams(vmem_limit_bytes=VMEM_LIMIT),
        cost_estimate=pl.CostEstimate(
            flops=4 * rows * tokens * cols,
            bytes_accessed=2 * rows * tokens * 2 * steps,
            transcendentals=0,
        ),
    )(half, *q_pieces, *g_pieces, pa, pb, values, keys_t, w, delta)


def weight_kernel(count, *refs):
    x = jnp.concatenate([r[...] for r in refs[:count]], axis=0)
    refs[count + 1][...] = dot(x, refs[count][...], 0, 1).astype(BF)


def weight_of(x_pieces, dq_cols):
    count = len(x_pieces)
    piece, cols = x_pieces[0].shape
    width, rows = dq_cols.shape
    step = min(cols, 256)
    return pl.pallas_call(
        functools.partial(weight_kernel, count),
        grid=(cols // step,),
        in_specs=[pl.BlockSpec((piece, step), lambda i: (0, i))] * count
        + [pl.BlockSpec((width, rows), lambda i: (0, 0))],
        out_specs=pl.BlockSpec((step, width), lambda i: (i, 0)),
        out_shape=jax.ShapeDtypeStruct((cols, width), BF),
        compiler_params=pltpu.CompilerParams(vmem_limit_bytes=VMEM_LIMIT),
        cost_estimate=pl.CostEstimate(
            flops=2 * rows * cols * width, bytes_accessed=2 * rows * cols, transcendentals=0
        ),
    )(*x_pieces, dq_cols)


def swap(x, axis, size, mask):
    return lax.ppermute(x, axis, [(i, i ^ mask) for i in range(size)])


def gather_pieces(x, axis, size):
    pieces = {0: x}
    bit = size // 2
    while bit:
        for k in list(pieces):
            pieces[k | bit] = swap(pieces[k], axis, size, bit)
        bit //= 2
    return [pieces[k] for k in range(size)]


def flip_pieces(x, count, bit):
    lead, piece = x.shape[:-1], x.shape[-1] // count
    y = x.reshape(lead + (count // (2 * bit), 2, bit * piece))
    return jnp.flip(y, axis=-2).reshape(x.shape)


def pick(blocks, index):
    return lax.dynamic_index_in_dim(blocks, index, 0, keepdims=False)


def exchange_sum(x, axis, size, stride, group, wide=False):
    me = (lax.axis_index(axis) // stride) % group
    total = pick(x, me).astype(F32)
    for k in range(1, group):
        total = total + swap(pick(x, me ^ k), axis, size, k * stride).astype(F32)
    return total if wide else total.astype(BF)


def exchange_gather(x, axis, size, stride, group):
    me = (lax.axis_index(axis) // stride) % group
    out = jnp.zeros((group,) + x.shape, x.dtype)
    for k in range(group):
        got = x if k == 0 else swap(x, axis, size, k * stride)
        out = lax.dynamic_update_index_in_dim(out, got, me ^ k, 0)
    return out


def local(n_dp, n_seq, qx, queries, keys, values, attn_out, grad_out, wq):
    low = max(n_dp // 4, 1)
    high = n_dp // low
    cols = queries.shape[1]
    me = lax.axis_index("seq")
    top = n_seq // 2
    q_pieces = gather_pieces(queries, "seq", n_seq)
    g_pieces = gather_pieces(grad_out, "seq", n_seq)
    x_pieces = gather_pieces(qx, "seq", n_seq)
    keys_t = keys.T
    delta = delta_of(grad_out, attn_out)
    pa, ma, la = probs_of(q_pieces[:top], keys)
    pb, mb, lb = probs_of(q_pieces[top:], keys)
    rows = 2 * la.shape[2]
    peak = jnp.concatenate([ma, mb], axis=2)
    lse = jnp.concatenate([la, lb], axis=2)
    bit = 1
    while bit < n_seq:
        got = swap(jnp.concatenate([lse, delta], axis=2), "seq", n_seq, bit)
        lse = jnp.logaddexp(lse, flip_pieces(got[:, :, :rows], n_seq, bit))
        delta = jnp.concatenate([delta, got[:, :, rows:]], axis=2)
        bit *= 2
    w = jnp.exp(peak - lse)

    mine = (me // top).astype(jnp.int32)
    shards, dqs = [], []
    for half in (1 - mine, mine):
        dkv, dqt = grads_of(half.reshape(1), q_pieces, g_pieces, pa, pb, values, keys_t, w, delta)
        tokens = dkv.shape[1]
        part = dkv.reshape(low, 2 * tokens // low, cols // 2)
        part = exchange_sum(part, "dp", n_dp, 1, low)
        part = part.reshape(high, part.shape[0] // high, cols // 2)
        shards.append(exchange_sum(part, "dp", n_dp, low, high))
        dqs.append(dqt)

    def narrow(dqt):
        blocks = dqt.reshape(top, dqt.shape[0] // top, rows)
        bit = 1
        base = me % top
        while bit < top:
            view = blocks.reshape((blocks.shape[0] // 2, 2) + blocks.shape[1:])
            own = (base // bit) % 2
            keep = lax.dynamic_index_in_dim(view, own, 1, keepdims=False)
            send = lax.dynamic_index_in_dim(view, 1 - own, 1, keepdims=False)
            got = swap(send, "seq", n_seq, bit)
            got = flip_pieces(got, n_seq, bit)
            blocks = (keep.astype(F32) + got.astype(F32)).astype(BF)
            bit *= 2
        return blocks[0]

    other, own = narrow(dqs[0]), narrow(dqs[1])
    got = flip_pieces(swap(other, "seq", n_seq, top), n_seq, top)
    dq_cols = (own.astype(F32) + got.astype(F32)).astype(BF)

    weight = weight_of(x_pieces, dq_cols)
    weight = weight.reshape(high, low, weight.shape[0] // n_dp, weight.shape[1])
    weight = exchange_sum(weight, "dp", n_dp, low, high)
    grad_weight = exchange_sum(weight, "dp", n_dp, 1, low, wide=True)

    piece = rows // n_seq
    width = cols // n_seq
    dq_rows = jnp.zeros((n_seq, width, piece), BF)
    for k in range(n_seq):
        block = dq_cols[:, k * piece : (k + 1) * piece]
        block = block if k == 0 else swap(block, "seq", n_seq, k)
        dq_rows = lax.dynamic_update_index_in_dim(dq_rows, block, me ^ k, 0)
    grad_input = dot(dq_rows.reshape(cols, piece), wq, 0, 1).astype(BF)

    halves = []
    for shard in shards:
        part = exchange_gather(shard, "dp", n_dp, low, high)
        part = part.reshape((-1,) + part.shape[2:])
        part = exchange_gather(part, "dp", n_dp, 1, low)
        halves.append(part.reshape(2, -1, cols // 2))
    other, own = halves
    left = jnp.where(mine == 0, own, other)
    right = jnp.where(mine == 0, other, own)
    both = jnp.concatenate([left, right], axis=2)
    return (grad_input, both[0], both[1], grad_weight)


def solution(mesh):
    n_dp, n_seq = mesh.shape["dp"], mesh.shape["seq"]
    return jax.shard_map(
        functools.partial(local, n_dp, n_seq),
        mesh=mesh,
        in_specs=(
            P(("dp", "seq"), None),
            P(("dp", "seq"), None),
            P("seq", None),
            P("seq", None),
            P(("dp", "seq"), None),
            P(("dp", "seq"), None),
            P(),
        ),
        out_specs=(P(("dp", "seq"), None), P("seq", None), P("seq", None), P("dp", "seq")),
        check_vma=False,
    )
```

```python
import functools
import math

import jax
import jax.numpy as jnp
from jax import lax
from jax.experimental import pallas as pl
from jax.experimental.pallas import tpu as pltpu
from jax.sharding import PartitionSpec as P

HD = 64
PAIR = 2 * HD
SCALE = 1.0 / math.sqrt(HD)
BF = jnp.bfloat16
F32 = jnp.float32
VMEM_LIMIT = 56 * 1024 * 1024


def dot(a, b, ca, cb):
    return lax.dot_general(a, b, (((ca,), (cb,)), ((), ())), preferred_element_type=F32)


def own_lanes(x, head):
    lane = lax.broadcasted_iota(jnp.int32, x.shape, 1)
    mine = lane < HD if head == 0 else lane >= HD
    return jnp.where(mine, x, jnp.zeros_like(x))


def delta_kernel(grad_ref, out_ref, delta_ref):
    prod = grad_ref[...].astype(F32) * out_ref[...].astype(F32)
    cols = prod.T
    heads = cols.shape[0] // HD
    for head in range(heads):
        part = jnp.sum(cols[head * HD : (head + 1) * HD], axis=0, keepdims=True)
        delta_ref[head // 2, head % 2] = part[0]


def delta_of(grad_out, attn_out):
    rows, cols = grad_out.shape
    return pl.pallas_call(
        delta_kernel,
        out_shape=jax.ShapeDtypeStruct((cols // PAIR, 2, rows), F32),
        compiler_params=pltpu.CompilerParams(vmem_limit_bytes=VMEM_LIMIT),
        cost_estimate=pl.CostEstimate(flops=4 * rows * cols, bytes_accessed=4 * rows * cols, transcendentals=0),
    )(grad_out, attn_out)


def probs_kernel(count, *refs):
    q_refs, k_ref = refs[:count], refs[count]
    p_ref, m_ref, lse_ref = refs[count + 1 :]
    q = jnp.concatenate([r[...] for r in q_refs], axis=0) * jnp.asarray(SCALE, BF)
    k = k_ref[...]
    for head in range(2):
        s = dot(own_lanes(k, head), q, 1, 1)
        top = jnp.max(s, axis=0, keepdims=True)
        p = jnp.exp(s - top)
        total = jnp.sum(p, axis=0, keepdims=True)
        p_ref[head] = p.astype(BF)
        m_ref[0, head] = top[0]
        lse_ref[0, head] = (top + jnp.log(total))[0]


def probs_of(q_pieces, keys):
    count = len(q_pieces)
    piece, cols = q_pieces[0].shape
    tokens = keys.shape[0]
    rows = piece * count
    pairs = cols // PAIR
    return pl.pallas_call(
        functools.partial(probs_kernel, count),
        grid=(pairs,),
        in_specs=[pl.BlockSpec((piece, PAIR), lambda i: (0, i))] * count
        + [pl.BlockSpec((tokens, PAIR), lambda i: (0, i))],
        out_specs=[
            pl.BlockSpec((2, tokens, rows), lambda i: (i, 0, 0)),
            pl.BlockSpec((1, 2, rows), lambda i: (i, 0, 0)),
            pl.BlockSpec((1, 2, rows), lambda i: (i, 0, 0)),
        ],
        out_shape=[
            jax.ShapeDtypeStruct((2 * pairs, tokens, rows), BF),
            jax.ShapeDtypeStruct((pairs, 2, rows), F32),
            jax.ShapeDtypeStruct((pairs, 2, rows), F32),
        ],
        compiler_params=pltpu.CompilerParams(vmem_limit_bytes=VMEM_LIMIT),
        cost_estimate=pl.CostEstimate(
            flops=2 * rows * tokens * cols,
            bytes_accessed=2 * rows * tokens * 2 * pairs,
            transcendentals=rows * tokens * 2 * pairs,
        ),
    )(*q_pieces, keys)


def grads_kernel(count, half_ref, *refs):
    q_refs, g_refs = refs[:count], refs[count : 2 * count]
    pa_ref, pb_ref, v_ref, kt_ref, w_ref, delta_ref, dkv_ref, dqt_ref = refs[2 * count :]
    rows = w_ref.shape[2]
    side = rows // 2
    w = w_ref[0]
    delta = delta_ref[0]
    v = v_ref[...]
    first = lax.broadcasted_iota(jnp.int32, (PAIR, rows), 0) < HD
    wide = jnp.where(first, w[0:1], w[1:2]).T
    q = jnp.concatenate([r[...] for r in q_refs], axis=0)
    g = jnp.concatenate([r[...] for r in g_refs], axis=0)
    qw = (q.astype(F32) * (wide * SCALE)).astype(BF)
    gw = (g.astype(F32) * wide).astype(BF)
    dk = jnp.zeros((v.shape[0], PAIR), F32)
    dv = jnp.zeros((v.shape[0], PAIR), F32)
    for half, p_ref in ((0, pa_ref), (1, pb_ref)):
        at = slice(half * side, (half + 1) * side)
        for head in range(2):
            p = p_ref[head]
            dp = dot(v, own_lanes(g[at], head), 1, 1)
            t = (p.astype(F32) * (dp - delta[head : head + 1, at])).astype(BF)
            dv = dv + dot(p, own_lanes(gw[at], head), 1, 0)
            dk = dk + dot(t, own_lanes(qw[at], head), 1, 0)
            dq = dot(kt_ref[head * HD : (head + 1) * HD], t, 1, 0)
            dq = dq * (w[head : head + 1, at] * SCALE)
            dqt_ref[head * HD : (head + 1) * HD, at] = dq.astype(BF)
    dkv_ref[0] = dk.astype(BF)
    dkv_ref[1] = dv.astype(BF)


def grads_of(half, q_pieces, g_pieces, pa, pb, values, keys_t, w, delta):
    count = len(q_pieces)
    piece, cols = q_pieces[0].shape
    tokens = values.shape[0]
    rows = piece * count
    steps = cols // PAIR // 2
    at = lambda i, h: h[0] * steps + i
    row_spec = pl.BlockSpec((piece, PAIR), lambda i, h: (0, at(i, h)))
    p_spec = pl.BlockSpec((2, tokens, rows // 2), lambda i, h: (at(i, h), 0, 0))
    stat_spec = pl.BlockSpec((1, 2, rows), lambda i, h: (at(i, h), 0, 0))
    return pl.pallas_call(
        functools.partial(grads_kernel, count),
        grid_spec=pltpu.PrefetchScalarGridSpec(
            num_scalar_prefetch=1,
            grid=(steps,),
            in_specs=[row_spec] * (2 * count)
            + [
                p_spec,
                p_spec,
                pl.BlockSpec((tokens, PAIR), lambda i, h: (0, at(i, h))),
                pl.BlockSpec((PAIR, tokens), lambda i, h: (at(i, h), 0)),
                stat_spec,
                stat_spec,
            ],
            out_specs=[
                pl.BlockSpec((2, tokens, PAIR), lambda i, h: (0, 0, i)),
                pl.BlockSpec((PAIR, rows), lambda i, h: (i, 0)),
            ],
        ),
        out_shape=[
            jax.ShapeDtypeStruct((2, tokens, cols // 2), BF),
            jax.ShapeDtypeStruct((cols // 2, rows), BF),
        ],
        compiler_params=pltpu.CompilerParams(vmem_limit_bytes=VMEM_LIMIT),
        cost_estimate=pl.CostEstimate(
            flops=4 * rows * tokens * cols,
            bytes_accessed=2 * rows * tokens * 2 * steps,
            transcendentals=0,
        ),
    )(half, *q_pieces, *g_pieces, pa, pb, values, keys_t, w, delta)


def weight_kernel(count, *refs):
    x = jnp.concatenate([r[...] for r in refs[:count]], axis=0)
    refs[count + 1][...] = dot(x, refs[count][...], 0, 1).astype(BF)


def weight_of(x_pieces, dq_cols):
    count = len(x_pieces)
    piece, cols = x_pieces[0].shape
    width, rows = dq_cols.shape
    step = min(cols, 256)
    return pl.pallas_call(
        functools.partial(weight_kernel, count),
        grid=(cols // step,),
        in_specs=[pl.BlockSpec((piece, step), lambda i: (0, i))] * count
        + [pl.BlockSpec((width, rows), lambda i: (0, 0))],
        out_specs=pl.BlockSpec((step, width), lambda i: (i, 0)),
        out_shape=jax.ShapeDtypeStruct((cols, width), BF),
        compiler_params=pltpu.CompilerParams(vmem_limit_bytes=VMEM_LIMIT),
        cost_estimate=pl.CostEstimate(
            flops=2 * rows * cols * width, bytes_accessed=2 * rows * cols, transcendentals=0
        ),
    )(*x_pieces, dq_cols)


def swap(x, axis, size, mask):
    return lax.ppermute(x, axis, [(i, i ^ mask) for i in range(size)])


def gather_pieces(x, axis, size):
    pieces = {0: x}
    bit = size // 2
    while bit:
        for k in list(pieces):
            pieces[k | bit] = swap(pieces[k], axis, size, bit)
        bit //= 2
    return [pieces[k] for k in range(size)]


def flip_pieces(x, count, bit):
    lead, piece = x.shape[:-1], x.shape[-1] // count
    y = x.reshape(lead + (count // (2 * bit), 2, bit * piece))
    return jnp.flip(y, axis=-2).reshape(x.shape)


def pick(blocks, index):
    return lax.dynamic_index_in_dim(blocks, index, 0, keepdims=False)


def exchange_sum(x, axis, size, stride, group, wide=False):
    me = (lax.axis_index(axis) // stride) % group
    total = pick(x, me).astype(F32)
    for k in range(1, group):
        total = total + swap(pick(x, me ^ k), axis, size, k * stride).astype(F32)
    return total if wide else total.astype(BF)


def exchange_gather(x, axis, size, stride, group):
    me = (lax.axis_index(axis) // stride) % group
    out = jnp.zeros((group,) + x.shape, x.dtype)
    for k in range(group):
        got = x if k == 0 else swap(x, axis, size, k * stride)
        out = lax.dynamic_update_index_in_dim(out, got, me ^ k, 0)
    return out


def local(n_dp, n_seq, qx, queries, keys, values, attn_out, grad_out, wq):
    low = max(n_dp // 4, 1)
    high = n_dp // low
    cols = queries.shape[1]
    me = lax.axis_index("seq")
    top = n_seq // 2
    q_pieces = gather_pieces(queries, "seq", n_seq)
    g_pieces = gather_pieces(grad_out, "seq", n_seq)
    x_pieces = gather_pieces(qx, "seq", n_seq)
    keys_t = keys.T
    delta = delta_of(grad_out, attn_out)
    pa, ma, la = probs_of(q_pieces[:top], keys)
    pb, mb, lb = probs_of(q_pieces[top:], keys)
    rows = 2 * la.shape[2]
    peak = jnp.concatenate([ma, mb], axis=2)
    lse = jnp.concatenate([la, lb], axis=2)
    bit = 1
    while bit < n_seq:
        got = swap(jnp.concatenate([lse, delta], axis=2), "seq", n_seq, bit)
        lse = jnp.logaddexp(lse, flip_pieces(got[:, :, :rows], n_seq, bit))
        delta = jnp.concatenate([delta, got[:, :, rows:]], axis=2)
        bit *= 2
    w = jnp.exp(peak - lse)

    mine = (me // top).astype(jnp.int32)
    shards, dqs = [], []
    for half in (1 - mine, mine):
        dkv, dqt = grads_of(half.reshape(1), q_pieces, g_pieces, pa, pb, values, keys_t, w, delta)
        tokens = dkv.shape[1]
        part = dkv.reshape(low, 2 * tokens // low, cols // 2)
        part = exchange_sum(part, "dp", n_dp, 1, low)
        part = part.reshape(high, part.shape[0] // high, cols // 2)
        shards.append(exchange_sum(part, "dp", n_dp, low, high))
        dqs.append(dqt)

    def narrow(dqt):
        blocks = dqt.reshape(top, dqt.shape[0] // top, rows)
        bit = 1
        base = me % top
        while bit < top:
            view = blocks.reshape((blocks.shape[0] // 2, 2) + blocks.shape[1:])
            own = (base // bit) % 2
            keep = lax.dynamic_index_in_dim(view, own, 1, keepdims=False)
            send = lax.dynamic_index_in_dim(view, 1 - own, 1, keepdims=False)
            got = swap(send, "seq", n_seq, bit)
            got = flip_pieces(got, n_seq, bit)
            blocks = (keep.astype(F32) + got.astype(F32)).astype(BF)
            bit *= 2
        return blocks[0]

    other, own = narrow(dqs[0]), narrow(dqs[1])
    got = flip_pieces(swap(other, "seq", n_seq, top), n_seq, top)
    dq_cols = (own.astype(F32) + got.astype(F32)).astype(BF)

    weight = weight_of(x_pieces, dq_cols)
    weight = weight.reshape(high, low, weight.shape[0] // n_dp, weight.shape[1])
    weight = exchange_sum(weight, "dp", n_dp, low, high)
    grad_weight = exchange_sum(weight, "dp", n_dp, 1, low, wide=True)

    piece = rows // n_seq
    width = cols // n_seq
    dq_rows = jnp.zeros((n_seq, width, piece), BF)
    for k in range(n_seq):
        block = dq_cols[:, k * piece : (k + 1) * piece]
        block = block if k == 0 else swap(block, "seq", n_seq, k)
        dq_rows = lax.dynamic_update_index_in_dim(dq_rows, block, me ^ k, 0)
    grad_input = dot(dq_rows.reshape(cols, piece), wq, 0, 1).astype(BF)

    halves = []
    for shard in shards:
        part = exchange_gather(shard, "dp", n_dp, low, high)
        part = part.reshape((-1,) + part.shape[2:])
        part = exchange_gather(part, "dp", n_dp, 1, low)
        halves.append(part.reshape(2, -1, cols // 2))
    other, own = halves
    left = jnp.where(mine == 0, own, other)
    right = jnp.where(mine == 0, other, own)
    both = jnp.concatenate([left, right], axis=2)
    return (grad_input, both[0], both[1], grad_weight)


def params(limit=24):
    return pltpu.CompilerParams(vmem_limit_bytes=limit * 1024 * 1024)


def cost(flops, nbytes, exps=0):
    return pl.CostEstimate(flops=flops, bytes_accessed=nbytes, transcendentals=exps)


def like(shape, dtype=BF):
    return jax.ShapeDtypeStruct(shape, dtype)


SMEM = pl.BlockSpec(memory_space=pltpu.SMEM)
VMEM = pl.BlockSpec(memory_space=pltpu.VMEM)


def span(i, size=PAIR):
    return slice(i * size, (i + 1) * size)


def flip_core(x):
    n = x.shape[-1] // PAIR
    return jnp.concatenate([x[..., span(i ^ 1)] for i in range(n)], axis=-1)


def pack_kernel(at_ref, q_ref, g_ref, o_ref, qk_ref, qs_ref, gk_ref, gs_ref, dk_ref, ds_ref):
    low = at_ref[0] == 0
    pairs = qk_ref.shape[1] // PAIR
    for ref, keep, send, scale in ((q_ref, qk_ref, qs_ref, SCALE), (g_ref, gk_ref, gs_ref, 1.0)):
        for p in range(pairs):
            a, b = ref[:, span(2 * p)], ref[:, span(2 * p + 1)]
            if scale != 1.0:
                a, b = a * jnp.asarray(scale, BF), b * jnp.asarray(scale, BF)
            keep[:, span(p)] = jnp.where(low, a, b)
            send[:, span(p)] = jnp.where(low, b, a)
    cols = (g_ref[...].astype(F32) * o_ref[...].astype(F32)).T
    for p in range(pairs):
        for h in range(2):
            a = jnp.sum(cols[span(4 * p + h, HD)], axis=0)
            b = jnp.sum(cols[span(4 * p + 2 + h, HD)], axis=0)
            dk_ref[p, h] = jnp.where(low, a, b)
            ds_ref[p, h] = jnp.where(low, b, a)


def pack(at, queries, grad_out, attn_out):
    rows, cols = queries.shape
    half, stat = like((rows, cols // 2)), like((cols // PAIR // 2, 2, rows), F32)
    return pl.pallas_call(
        pack_kernel,
        in_specs=[SMEM] + [VMEM] * 3,
        out_specs=[VMEM] * 6,
        out_shape=[half] * 4 + [stat] * 2,
        compiler_params=params(),
        cost_estimate=cost(4 * rows * cols, 10 * rows * cols),
    )(at, queries, grad_out, attn_out)


def pack_tokens_kernel(at_ref, k_ref, v_ref, kp_ref, vp_ref, kt_ref):
    low = at_ref[0] == 0
    for p in range(kp_ref.shape[1] // PAIR):
        k = jnp.where(low, k_ref[:, span(2 * p)], k_ref[:, span(2 * p + 1)])
        kp_ref[:, span(p)] = k
        kt_ref[span(p)] = k.T
        vp_ref[:, span(p)] = jnp.where(low, v_ref[:, span(2 * p)], v_ref[:, span(2 * p + 1)])


def pack_tokens(at, keys, values):
    tokens, cols = keys.shape
    return pl.pallas_call(
        pack_tokens_kernel,
        in_specs=[SMEM, VMEM, VMEM],
        out_specs=[VMEM] * 3,
        out_shape=[like((tokens, cols // 2))] * 2 + [like((cols // 2, tokens))],
        compiler_params=params(),
        cost_estimate=cost(tokens * cols, 7 * tokens * cols),
    )(at, keys, values)


def side_kernel(count, step, last, *refs):
    q_refs, k_ref = refs[:count], refs[count]
    if last:
        la_ref, own_ref, got_ref, p_ref, m_ref, lse_ref, send_ref = refs[count + 1 :]
    else:
        p_ref, m_ref, lse_ref = refs[count + 1 :]
    for j in range(step):
        q = jnp.concatenate([r[:, span(j)] for r in q_refs], axis=0)
        k = k_ref[:, span(j)]
        for head in range(2):
            s = dot(own_lanes(k, head), q, 1, 1)
            top = jnp.max(s, axis=0, keepdims=True)
            p = jnp.exp(s - top)
            total = jnp.sum(p, axis=0, keepdims=True)
            p_ref[2 * j + head] = p.astype(BF)
            m_ref[j, head] = top[0]
            lse_ref[j, head] = (top + jnp.log(total))[0]
    if last:
        send_ref[...] = jnp.concatenate(
            [flip_core(la_ref[...]), flip_core(lse_ref[...]), own_ref[...], got_ref[...]], axis=-1
        )


def side_of(pieces, keys, extra=None, step=2):
    count = len(pieces)
    piece, cols = pieces[0].shape
    tokens = keys.shape[0]
    rows, pairs = piece * count, cols // PAIR
    stat_spec = lambda n: pl.BlockSpec((step, 2, n), lambda i: (i, 0, 0))
    in_specs = [pl.BlockSpec((piece, step * PAIR), lambda i: (0, i))] * count
    in_specs += [pl.BlockSpec((tokens, step * PAIR), lambda i: (0, i))]
    out_specs = [pl.BlockSpec((2 * step, tokens, rows), lambda i: (i, 0, 0)), stat_spec(rows), stat_spec(rows)]
    out_shape = [like((2 * pairs, tokens, rows)), like((pairs, 2, rows), F32), like((pairs, 2, rows), F32)]
    args = [*pieces, keys]
    if extra is not None:
        in_specs += [stat_spec(rows), stat_spec(piece), stat_spec(piece)]
        out_specs += [stat_spec(2 * rows + 2 * piece)]
        out_shape += [like((pairs, 2, 2 * rows + 2 * piece), F32)]
        args += extra
    return pl.pallas_call(
        functools.partial(side_kernel, count, step, extra is not None),
        grid=(pairs // step,),
        in_specs=in_specs,
        out_specs=out_specs,
        out_shape=out_shape,
        compiler_params=params(),
        cost_estimate=cost(2 * rows * tokens * cols, 4 * rows * tokens * pairs, 2 * rows * tokens * pairs),
    )(*args)


def log_add(a, b):
    top = jnp.maximum(a, b)
    return top + jnp.log(jnp.exp(a - top) + jnp.exp(b - top))


def merge_kernel(la_ref, lb_ref, sent_ref, got_ref, send_ref):
    side = la_ref.shape[2]
    lb = log_add(lb_ref[...], got_ref[:, :, side : 2 * side])
    la = log_add(la_ref[...], got_ref[:, :, :side])
    own, other = sent_ref[:, :, 2 * side :], got_ref[:, :, 2 * side :]
    deltas = [own[..., span(0)], other[..., span(0)], own[..., span(1)], other[..., span(1)]]
    send_ref[...] = jnp.concatenate([lb, la] + deltas, axis=-1)


def merge(la, lb, sent, got):
    pairs, two, side = la.shape
    return pl.pallas_call(
        merge_kernel,
        in_specs=[VMEM] * 4,
        out_specs=VMEM,
        out_shape=like((pairs, two, 3 * side), F32),
        compiler_params=params(),
        cost_estimate=cost(1000, 100000),
    )(la, lb, sent, got)


def half_kernel(count, at_ref, *refs):
    q_refs, g_refs = refs[:count], refs[count : 2 * count]
    pa_ref, pb_ref, v_ref, kt_ref, ma_ref, mb_ref, sent_ref, got_ref = refs[2 * count : 2 * count + 8]
    kv_refs, dqs_ref, dqk_ref = refs[2 * count + 8 : -2], refs[-2], refs[-1]
    side = ma_ref.shape[2]
    z = at_ref[2]
    v = v_ref[...]
    tokens = v.shape[0]
    dk = jnp.zeros((tokens, PAIR), F32)
    dv = jnp.zeros((tokens, PAIR), F32)
    first = lax.broadcasted_iota(jnp.int32, (PAIR, side), 0) < HD
    halves = []
    for b, p_ref, m_ref in ((0, pa_ref, ma_ref), (1, pb_ref, mb_ref)):
        lse = log_add(sent_ref[0, :, span(1 - b, side)], got_ref[0, :, span(b, side)])
        w = jnp.exp(m_ref[0] - lse)
        delta = (got_ref if b else sent_ref)[0, :, 2 * side :]
        wide = jnp.where(first, w[0:1], w[1:2]).T
        at = slice(b * count // 2, (b + 1) * count // 2)
        q = jnp.concatenate([r[...] for r in q_refs[at]], axis=0)
        g = jnp.concatenate([r[...] for r in g_refs[at]], axis=0)
        qw = (q.astype(F32) * wide).astype(BF)
        gw = (g.astype(F32) * wide).astype(BF)
        parts = []
        for head in range(2):
            p = p_ref[head]
            dp = dot(v, own_lanes(g, head), 1, 1)
            t = (p.astype(F32) * (dp - delta[head : head + 1])).astype(BF)
            dv = dv + dot(p, own_lanes(gw, head), 1, 0)
            dk = dk + dot(t, own_lanes(qw, head), 1, 0)
            dq = dot(kt_ref[span(head, HD)], t, 1, 0)
            parts.append((dq * (w[head : head + 1] * SCALE)).astype(BF))
        halves.append(jnp.concatenate(parts, axis=0))
    dq = jnp.concatenate(halves, axis=1)

    @pl.when(pl.program_id(0) == 0)
    def _():
        dqs_ref[...] = flip_core(dq)

    @pl.when(pl.program_id(0) == 1)
    def _():
        dqk_ref[...] = dq

    both = jnp.concatenate([dk.astype(BF), dv.astype(BF)], axis=0)
    size = both.shape[0] // len(kv_refs)
    for k, ref in enumerate(kv_refs):
        out = both[:size]
        for j in range(1, len(kv_refs)):
            out = jnp.where((z ^ k) == j, both[span(j, size)], out)
        ref[...] = out


def half_of(at, high, q_pieces, g_pieces, pa, pb, vp, kt, ma, mb, sent, got):
    count = len(q_pieces)
    piece, cols = q_pieces[0].shape
    tokens = vp.shape[0]
    side = ma.shape[2]
    bit = lambda i, a: (i + 1 + a[1]) % 2
    pair = lambda i, a: 2 * a[0] + bit(i, a)
    row_spec = pl.BlockSpec((piece, PAIR), lambda i, a: (0, pair(i, a)))
    p_spec = pl.BlockSpec((2, tokens, side), lambda i, a: (pair(i, a), 0, 0))
    stat_spec = lambda n: pl.BlockSpec((1, 2, n), lambda i, a: (pair(i, a), 0, 0))
    block = 2 * tokens // high
    return pl.pallas_call(
        functools.partial(half_kernel, count),
        grid_spec=pltpu.PrefetchScalarGridSpec(
            num_scalar_prefetch=1,
            grid=(2,),
            in_specs=[row_spec] * (2 * count)
            + [
                p_spec,
                p_spec,
                pl.BlockSpec((tokens, PAIR), lambda i, a: (0, pair(i, a))),
                pl.BlockSpec((PAIR, tokens), lambda i, a: (pair(i, a), 0)),
                stat_spec(side),
                stat_spec(side),
                stat_spec(3 * side),
                stat_spec(3 * side),
            ],
            out_specs=[pl.BlockSpec((block, PAIR), lambda i, a: (0, bit(i, a)))] * high
            + [pl.BlockSpec((PAIR, 2 * side), lambda i, a: (0, 0))] * 2,
        ),
        out_shape=[like((block, 2 * PAIR))] * high + [like((PAIR, 2 * side))] * 2,
        compiler_params=params(),
        cost_estimate=cost(16 * side * tokens * 2 * PAIR * 2, 8 * side * tokens * 2, 0),
    )(at, *q_pieces, *g_pieces, pa, pb, vp, kt, ma, mb, sent, got)


def columns_kernel(count, high, at_ref, *refs):
    x_refs = refs[:count]
    keep_ref, core_ref, y_ref = refs[count : count + 3]
    w_refs, back_ref, send_ref, all_ref = refs[count + 3 : -3], refs[-3], refs[-2], refs[-1]
    side = keep_ref.shape[1] // 2
    far = jnp.concatenate([y_ref[:, side:], y_ref[:, :side]], axis=1)
    dq = (keep_ref[...].astype(F32) + core_ref[...].astype(F32) + far.astype(F32)).astype(BF)
    quarter = side // 2
    back_ref[...] = jnp.concatenate([dq[:, span(0, quarter)], dq[:, span(2, quarter)]], axis=1)
    send_ref[...] = jnp.concatenate([dq[:, span(1, quarter)], dq[:, span(3, quarter)]], axis=1)
    x = jnp.concatenate([r[...] for r in x_refs], axis=0)
    all_ref[...] = dot(dq, x, 1, 0)
    width = x.shape[1] // high
    for k, ref in enumerate(w_refs):
        start = pl.multiple_of((at_ref[0] ^ k) * width, PAIR)
        ref[...] = all_ref[:, pl.ds(start, width)].astype(BF)


def columns_of(at, high, x_pieces, keep, core, y):
    count = len(x_pieces)
    piece, cols = x_pieces[0].shape
    width, rows = keep.shape
    return pl.pallas_call(
        functools.partial(columns_kernel, count, high),
        in_specs=[SMEM] + [VMEM] * (count + 3),
        out_specs=[VMEM] * (high + 2),
        out_shape=[like((width, cols // high))] * high + [like((width, rows // 2))] * 2,
        scratch_shapes=[pltpu.VMEM((width, cols), F32)],
        compiler_params=params(),
        cost_estimate=cost(2 * rows * cols * width, 2 * rows * cols),
    )(at, *x_pieces, keep, core, y)


def input_kernel(at_ref, back_ref, x_ref, y_ref, core_ref, wq_ref, out_ref, dq_ref):
    me, x = at_ref[0], at_ref[1]
    size = back_ref.shape[0]

    def put(group, odd, block):
        row = pl.multiple_of((2 * group + (x ^ odd)) * size, PAIR)
        dq_ref[pl.ds(row, size), :] = block

    put(me, 0, back_ref[:, :size])
    put(me, 1, x_ref[:, :size])
    for odd in range(2):
        put(me ^ 2, odd, y_ref[span(odd, size), :size])
        put(me ^ 1, odd, core_ref[span(odd, size), :])
        put(me ^ 3, odd, core_ref[span(2 + odd, size), :])
    out_ref[...] = dot(dq_ref[...], wq_ref[...], 0, 1).astype(BF)


def input_of(at, back, x, y, core, wq):
    size, cols = back.shape[0], wq.shape[1]
    return pl.pallas_call(
        input_kernel,
        in_specs=[SMEM] + [VMEM] * 5,
        out_specs=VMEM,
        out_shape=like((size, cols)),
        scratch_shapes=[pltpu.VMEM((cols, size), BF)],
        compiler_params=params(),
        cost_estimate=cost(2 * size * cols * cols, 2 * cols * cols),
    )(at, back, x, y, core, wq)


def weight_sum_kernel(at_ref, *refs):
    total = refs[0][...].astype(F32)
    for r in refs[1:-2]:
        total = total + r[...].astype(F32)
    keep_ref, send_ref = refs[-2:]
    size = keep_ref.shape[1]
    a, b = total[:, :size], total[:, size:]
    low = at_ref[0] == 0
    keep_ref[...] = jnp.where(low, a, b)
    send_ref[...] = jnp.where(low, b, a).astype(BF)


def weight_sum(at, parts):
    rows, cols = parts[0].shape
    return pl.pallas_call(
        weight_sum_kernel,
        in_specs=[SMEM] + [VMEM] * len(parts),
        out_specs=[VMEM] * 2,
        out_shape=[like((rows, cols // 2), F32), like((rows, cols // 2))],
        compiler_params=params(),
        cost_estimate=cost(1000, 300000),
    )(at, *parts)


def weight_out_kernel(at_ref, keep_ref, got_ref, out_ref):
    size = keep_ref.shape[0]
    a, b = keep_ref[...].T, got_ref[...].astype(F32).T
    low = at_ref[0] == 0
    out_ref[:, :size] = jnp.where(low, a, b)
    out_ref[:, size:] = jnp.where(low, b, a)


def weight_out(at, keep, got):
    size, rows = keep.shape
    return pl.pallas_call(
        weight_out_kernel,
        in_specs=[SMEM, VMEM, VMEM],
        out_specs=VMEM,
        out_shape=like((rows, 2 * size), F32),
        compiler_params=params(),
        cost_estimate=cost(1000, 300000),
    )(at, keep, got)


def tokens_kernel(high, at_ref, *refs):
    y, x, z = at_ref[0], at_ref[1], at_ref[2]
    key_ref, val_ref = refs[-2:]
    size = refs[0].shape[0]
    each = high + 1
    for half in range(2):
        group = 2 * (y ^ (1 - half))
        own, got = refs[half * each : half * each + high], refs[half * each + high]
        for k in range(high):
            b = z ^ k
            row = pl.multiple_of((b % (high // 2)) * size, 16)
            for out_ref, which in ((key_ref, 0), (val_ref, 1)):

                @pl.when(b // (high // 2) == which)
                def _():
                    for c in range(2):
                        for odd, block in ((0, own[k][:, span(c)]), (1, got[span(k, size), span(c)])):
                            col = pl.multiple_of((2 * (group + c) + (x ^ odd)) * PAIR, PAIR)
                            out_ref[pl.ds(row, size), pl.ds(col, PAIR)] = block


def tokens_out(at, high, tokens, cols, parts):
    return pl.pallas_call(
        functools.partial(tokens_kernel, high),
        in_specs=[SMEM] + [VMEM] * len(parts),
        out_specs=[VMEM] * 2,
        out_shape=[like((tokens, cols))] * 2,
        compiler_params=params(),
        cost_estimate=cost(1000, 8 * tokens * cols),
    )(at, *parts)


def local_split(n_dp, n_seq, qx, queries, keys, values, attn_out, grad_out, wq):
    high = n_dp // 2
    dp, me = lax.axis_index("dp").astype(jnp.int32), lax.axis_index("seq").astype(jnp.int32)
    x, z, y, c = dp % 2, dp // 2, me // 2, me % 2
    over_x = lambda t: swap(t, "dp", n_dp, 1)
    over_y = lambda t: swap(t, "seq", n_seq, 2)
    over_core = lambda t: swap(t, "seq", n_seq, 1)
    over_z = lambda t, k: swap(t, "dp", n_dp, 2 * k)
    scalars = lambda *t: jnp.stack(t)

    def rows_of(own, from_x):
        from_y, from_xy = over_y(own), over_y(from_x)
        a = [own, over_core(own), from_x, over_core(from_x)]
        return a, [from_y, over_core(from_y), from_xy, over_core(from_xy)]

    qk, qs, gk, gs, delta, delta_s = pack(scalars(x), queries, grad_out, attn_out)
    kp, vp, kt = pack_tokens(scalars(x), keys, values)
    qa, qb = rows_of(qk, over_x(qs))
    ga, gb = rows_of(gk, over_x(gs))
    delta_x = over_x(delta_s)
    pa, ma, la = side_of(qa, kp)
    pb, mb, lb, sent = side_of(qb, kp, [la, delta, delta_x])
    send = merge(la, lb, sent, over_core(sent))
    got = over_y(send)

    sums, dqs = [], []
    for half in (1 - y, y):
        out = half_of(scalars(half, c, z), high, qa + qb, ga + gb, pa, pb, vp, kt, ma, mb, send, got)
        total = out[0].astype(F32)
        for k in range(1, high):
            total = total + over_z(out[k], k).astype(F32)
        sums.append(total.astype(BF))
        dqs.append((out[high + 1], over_core(out[high])))

    keep, core = dqs[0]
    far = over_y((keep.astype(F32) + core.astype(F32)).astype(BF))
    qx, got = lax.optimization_barrier((qx, got))
    xa, xb = rows_of(qx, over_x(qx))
    *parts, back, back_s = columns_of(scalars(z), high, xa + xb, *dqs[1], far)
    parts = parts[:1] + [over_z(parts[k], k) for k in range(1, high)]
    keep, send_w = weight_sum(scalars(x), parts)
    grad_weight = weight_out(scalars(x), keep, over_x(send_w))

    size = back.shape[0]
    from_x = over_x(back_s)
    from_y = over_y(jnp.concatenate([back[:, 2 * size :], from_x[:, 2 * size :]], axis=0))
    near = [back[:, size : 2 * size], from_x[:, size : 2 * size], from_y[:, size:]]
    from_core = over_core(jnp.concatenate(near, axis=0))
    grad_input = input_of(scalars(me, x), back, from_x, from_y, from_core, wq)

    parts = []
    for total in sums:
        blocks = [total] + [over_z(total, k) for k in range(1, high)]
        parts += blocks + [over_x(jnp.concatenate(blocks, axis=0))]
    grad_keys, grad_values = tokens_out(scalars(y, x, z), high, *keys.shape, parts)
    return (grad_input, grad_keys, grad_values, grad_weight)


def solution(mesh):
    n_dp, n_seq = mesh.shape["dp"], mesh.shape["seq"]

    def run(qx, queries, keys, *rest):
        pairs = queries.shape[1] == 2 * n_seq * PAIR and queries.shape[0] == n_dp * n_seq * PAIR
        split = n_seq == 4 and n_dp == 8 and pairs and (2 * keys.shape[0] // n_seq) % (16 * n_dp // 2) == 0
        return shard(local_split if split else local)(qx, queries, keys, *rest)

    def shard(f):
        return jax.shard_map(
            functools.partial(f, n_dp, n_seq),
            mesh=mesh,
            in_specs=(
                P(("dp", "seq"), None),
                P(("dp", "seq"), None),
                P("seq", None),
                P("seq", None),
                P(("dp", "seq"), None),
                P(("dp", "seq"), None),
                P(),
            ),
            out_specs=(P(("dp", "seq"), None), P("seq", None), P("seq", None), P("dp", "seq")),
            check_vma=False,
        )

    return run
```

```python
import functools
import math

import jax
import jax.numpy as jnp
from jax import lax
from jax.experimental import pallas as pl
from jax.experimental.pallas import tpu as pltpu
from jax.sharding import PartitionSpec as P

HD = 64
PAIR = 2 * HD
SCALE = 1.0 / math.sqrt(HD)
BF = jnp.bfloat16
F32 = jnp.float32
VMEM_LIMIT = 56 * 1024 * 1024


def dot(a, b, ca, cb):
    return lax.dot_general(a, b, (((ca,), (cb,)), ((), ())), preferred_element_type=F32)


def own_lanes(x, head):
    lane = lax.broadcasted_iota(jnp.int32, x.shape, 1)
    mine = lane < HD if head == 0 else lane >= HD
    return jnp.where(mine, x, jnp.zeros_like(x))


def delta_kernel(grad_ref, out_ref, delta_ref):
    prod = grad_ref[...].astype(F32) * out_ref[...].astype(F32)
    cols = prod.T
    heads = cols.shape[0] // HD
    for head in range(heads):
        part = jnp.sum(cols[head * HD : (head + 1) * HD], axis=0, keepdims=True)
        delta_ref[head // 2, head % 2] = part[0]


def delta_of(grad_out, attn_out):
    rows, cols = grad_out.shape
    return pl.pallas_call(
        delta_kernel,
        out_shape=jax.ShapeDtypeStruct((cols // PAIR, 2, rows), F32),
        compiler_params=pltpu.CompilerParams(vmem_limit_bytes=VMEM_LIMIT),
        cost_estimate=pl.CostEstimate(flops=4 * rows * cols, bytes_accessed=4 * rows * cols, transcendentals=0),
    )(grad_out, attn_out)


def probs_kernel(count, *refs):
    q_refs, k_ref = refs[:count], refs[count]
    p_ref, m_ref, lse_ref = refs[count + 1 :]
    q = jnp.concatenate([r[...] for r in q_refs], axis=0) * jnp.asarray(SCALE, BF)
    k = k_ref[...]
    for head in range(2):
        s = dot(own_lanes(k, head), q, 1, 1)
        top = jnp.max(s, axis=0, keepdims=True)
        p = jnp.exp(s - top)
        total = jnp.sum(p, axis=0, keepdims=True)
        p_ref[head] = p.astype(BF)
        m_ref[0, head] = top[0]
        lse_ref[0, head] = (top + jnp.log(total))[0]


def probs_of(q_pieces, keys):
    count = len(q_pieces)
    piece, cols = q_pieces[0].shape
    tokens = keys.shape[0]
    rows = piece * count
    pairs = cols // PAIR
    return pl.pallas_call(
        functools.partial(probs_kernel, count),
        grid=(pairs,),
        in_specs=[pl.BlockSpec((piece, PAIR), lambda i: (0, i))] * count
        + [pl.BlockSpec((tokens, PAIR), lambda i: (0, i))],
        out_specs=[
            pl.BlockSpec((2, tokens, rows), lambda i: (i, 0, 0)),
            pl.BlockSpec((1, 2, rows), lambda i: (i, 0, 0)),
            pl.BlockSpec((1, 2, rows), lambda i: (i, 0, 0)),
        ],
        out_shape=[
            jax.ShapeDtypeStruct((2 * pairs, tokens, rows), BF),
            jax.ShapeDtypeStruct((pairs, 2, rows), F32),
            jax.ShapeDtypeStruct((pairs, 2, rows), F32),
        ],
        compiler_params=pltpu.CompilerParams(vmem_limit_bytes=VMEM_LIMIT),
        cost_estimate=pl.CostEstimate(
            flops=2 * rows * tokens * cols,
            bytes_accessed=2 * rows * tokens * 2 * pairs,
            transcendentals=rows * tokens * 2 * pairs,
        ),
    )(*q_pieces, keys)


def grads_kernel(count, half_ref, *refs):
    q_refs, g_refs = refs[:count], refs[count : 2 * count]
    pa_ref, pb_ref, v_ref, kt_ref, w_ref, delta_ref, dkv_ref, dqt_ref = refs[2 * count :]
    rows = w_ref.shape[2]
    side = rows // 2
    w = w_ref[0]
    delta = delta_ref[0]
    v = v_ref[...]
    first = lax.broadcasted_iota(jnp.int32, (PAIR, rows), 0) < HD
    wide = jnp.where(first, w[0:1], w[1:2]).T
    q = jnp.concatenate([r[...] for r in q_refs], axis=0)
    g = jnp.concatenate([r[...] for r in g_refs], axis=0)
    qw = (q.astype(F32) * (wide * SCALE)).astype(BF)
    gw = (g.astype(F32) * wide).astype(BF)
    dk = jnp.zeros((v.shape[0], PAIR), F32)
    dv = jnp.zeros((v.shape[0], PAIR), F32)
    for half, p_ref in ((0, pa_ref), (1, pb_ref)):
        at = slice(half * side, (half + 1) * side)
        for head in range(2):
            p = p_ref[head]
            dp = dot(v, own_lanes(g[at], head), 1, 1)
            t = (p.astype(F32) * (dp - delta[head : head + 1, at])).astype(BF)
            dv = dv + dot(p, own_lanes(gw[at], head), 1, 0)
            dk = dk + dot(t, own_lanes(qw[at], head), 1, 0)
            dq = dot(kt_ref[head * HD : (head + 1) * HD], t, 1, 0)
            dq = dq * (w[head : head + 1, at] * SCALE)
            dqt_ref[head * HD : (head + 1) * HD, at] = dq.astype(BF)
    dkv_ref[0] = dk.astype(BF)
    dkv_ref[1] = dv.astype(BF)


def grads_of(half, q_pieces, g_pieces, pa, pb, values, keys_t, w, delta):
    count = len(q_pieces)
    piece, cols = q_pieces[0].shape
    tokens = values.shape[0]
    rows = piece * count
    steps = cols // PAIR // 2
    at = lambda i, h: h[0] * steps + i
    row_spec = pl.BlockSpec((piece, PAIR), lambda i, h: (0, at(i, h)))
    p_spec = pl.BlockSpec((2, tokens, rows // 2), lambda i, h: (at(i, h), 0, 0))
    stat_spec = pl.BlockSpec((1, 2, rows), lambda i, h: (at(i, h), 0, 0))
    return pl.pallas_call(
        functools.partial(grads_kernel, count),
        grid_spec=pltpu.PrefetchScalarGridSpec(
            num_scalar_prefetch=1,
            grid=(steps,),
            in_specs=[row_spec] * (2 * count)
            + [
                p_spec,
                p_spec,
                pl.BlockSpec((tokens, PAIR), lambda i, h: (0, at(i, h))),
                pl.BlockSpec((PAIR, tokens), lambda i, h: (at(i, h), 0)),
                stat_spec,
                stat_spec,
            ],
            out_specs=[
                pl.BlockSpec((2, tokens, PAIR), lambda i, h: (0, 0, i)),
                pl.BlockSpec((PAIR, rows), lambda i, h: (i, 0)),
            ],
        ),
        out_shape=[
            jax.ShapeDtypeStruct((2, tokens, cols // 2), BF),
            jax.ShapeDtypeStruct((cols // 2, rows), BF),
        ],
        compiler_params=pltpu.CompilerParams(vmem_limit_bytes=VMEM_LIMIT),
        cost_estimate=pl.CostEstimate(
            flops=4 * rows * tokens * cols,
            bytes_accessed=2 * rows * tokens * 2 * steps,
            transcendentals=0,
        ),
    )(half, *q_pieces, *g_pieces, pa, pb, values, keys_t, w, delta)


def weight_kernel(count, *refs):
    x = jnp.concatenate([r[...] for r in refs[:count]], axis=0)
    refs[count + 1][...] = dot(x, refs[count][...], 0, 1).astype(BF)


def weight_of(x_pieces, dq_cols):
    count = len(x_pieces)
    piece, cols = x_pieces[0].shape
    width, rows = dq_cols.shape
    step = min(cols, 256)
    return pl.pallas_call(
        functools.partial(weight_kernel, count),
        grid=(cols // step,),
        in_specs=[pl.BlockSpec((piece, step), lambda i: (0, i))] * count
        + [pl.BlockSpec((width, rows), lambda i: (0, 0))],
        out_specs=pl.BlockSpec((step, width), lambda i: (i, 0)),
        out_shape=jax.ShapeDtypeStruct((cols, width), BF),
        compiler_params=pltpu.CompilerParams(vmem_limit_bytes=VMEM_LIMIT),
        cost_estimate=pl.CostEstimate(
            flops=2 * rows * cols * width, bytes_accessed=2 * rows * cols, transcendentals=0
        ),
    )(*x_pieces, dq_cols)


def swap(x, axis, size, mask):
    return lax.ppermute(x, axis, [(i, i ^ mask) for i in range(size)])


def gather_pieces(x, axis, size):
    pieces = {0: x}
    bit = size // 2
    while bit:
        for k in list(pieces):
            pieces[k | bit] = swap(pieces[k], axis, size, bit)
        bit //= 2
    return [pieces[k] for k in range(size)]


def flip_pieces(x, count, bit):
    lead, piece = x.shape[:-1], x.shape[-1] // count
    y = x.reshape(lead + (count // (2 * bit), 2, bit * piece))
    return jnp.flip(y, axis=-2).reshape(x.shape)


def pick(blocks, index):
    return lax.dynamic_index_in_dim(blocks, index, 0, keepdims=False)


def exchange_sum(x, axis, size, stride, group, wide=False):
    me = (lax.axis_index(axis) // stride) % group
    total = pick(x, me).astype(F32)
    for k in range(1, group):
        total = total + swap(pick(x, me ^ k), axis, size, k * stride).astype(F32)
    return total if wide else total.astype(BF)


def exchange_gather(x, axis, size, stride, group):
    me = (lax.axis_index(axis) // stride) % group
    out = jnp.zeros((group,) + x.shape, x.dtype)
    for k in range(group):
        got = x if k == 0 else swap(x, axis, size, k * stride)
        out = lax.dynamic_update_index_in_dim(out, got, me ^ k, 0)
    return out


def local(n_dp, n_seq, qx, queries, keys, values, attn_out, grad_out, wq):
    low = max(n_dp // 4, 1)
    high = n_dp // low
    cols = queries.shape[1]
    me = lax.axis_index("seq")
    top = n_seq // 2
    q_pieces = gather_pieces(queries, "seq", n_seq)
    g_pieces = gather_pieces(grad_out, "seq", n_seq)
    x_pieces = gather_pieces(qx, "seq", n_seq)
    keys_t = keys.T
    delta = delta_of(grad_out, attn_out)
    pa, ma, la = probs_of(q_pieces[:top], keys)
    pb, mb, lb = probs_of(q_pieces[top:], keys)
    rows = 2 * la.shape[2]
    peak = jnp.concatenate([ma, mb], axis=2)
    lse = jnp.concatenate([la, lb], axis=2)
    bit = 1
    while bit < n_seq:
        got = swap(jnp.concatenate([lse, delta], axis=2), "seq", n_seq, bit)
        lse = jnp.logaddexp(lse, flip_pieces(got[:, :, :rows], n_seq, bit))
        delta = jnp.concatenate([delta, got[:, :, rows:]], axis=2)
        bit *= 2
    w = jnp.exp(peak - lse)

    mine = (me // top).astype(jnp.int32)
    shards, dqs = [], []
    for half in (1 - mine, mine):
        dkv, dqt = grads_of(half.reshape(1), q_pieces, g_pieces, pa, pb, values, keys_t, w, delta)
        tokens = dkv.shape[1]
        part = dkv.reshape(low, 2 * tokens // low, cols // 2)
        part = exchange_sum(part, "dp", n_dp, 1, low)
        part = part.reshape(high, part.shape[0] // high, cols // 2)
        shards.append(exchange_sum(part, "dp", n_dp, low, high))
        dqs.append(dqt)

    def narrow(dqt):
        blocks = dqt.reshape(top, dqt.shape[0] // top, rows)
        bit = 1
        base = me % top
        while bit < top:
            view = blocks.reshape((blocks.shape[0] // 2, 2) + blocks.shape[1:])
            own = (base // bit) % 2
            keep = lax.dynamic_index_in_dim(view, own, 1, keepdims=False)
            send = lax.dynamic_index_in_dim(view, 1 - own, 1, keepdims=False)
            got = swap(send, "seq", n_seq, bit)
            got = flip_pieces(got, n_seq, bit)
            blocks = (keep.astype(F32) + got.astype(F32)).astype(BF)
            bit *= 2
        return blocks[0]

    other, own = narrow(dqs[0]), narrow(dqs[1])
    got = flip_pieces(swap(other, "seq", n_seq, top), n_seq, top)
    dq_cols = (own.astype(F32) + got.astype(F32)).astype(BF)

    weight = weight_of(x_pieces, dq_cols)
    weight = weight.reshape(high, low, weight.shape[0] // n_dp, weight.shape[1])
    weight = exchange_sum(weight, "dp", n_dp, low, high)
    grad_weight = exchange_sum(weight, "dp", n_dp, 1, low, wide=True)

    piece = rows // n_seq
    width = cols // n_seq
    dq_rows = jnp.zeros((n_seq, width, piece), BF)
    for k in range(n_seq):
        block = dq_cols[:, k * piece : (k + 1) * piece]
        block = block if k == 0 else swap(block, "seq", n_seq, k)
        dq_rows = lax.dynamic_update_index_in_dim(dq_rows, block, me ^ k, 0)
    grad_input = dot(dq_rows.reshape(cols, piece), wq, 0, 1).astype(BF)

    halves = []
    for shard in shards:
        part = exchange_gather(shard, "dp", n_dp, low, high)
        part = part.reshape((-1,) + part.shape[2:])
        part = exchange_gather(part, "dp", n_dp, 1, low)
        halves.append(part.reshape(2, -1, cols // 2))
    other, own = halves
    left = jnp.where(mine == 0, own, other)
    right = jnp.where(mine == 0, other, own)
    both = jnp.concatenate([left, right], axis=2)
    return (grad_input, both[0], both[1], grad_weight)


def params(limit=24):
    return pltpu.CompilerParams(vmem_limit_bytes=limit * 1024 * 1024)


def cost(flops=0, nbytes=0, exps=0):
    return pl.CostEstimate(flops=1, bytes_accessed=1, transcendentals=0)


def like(shape, dtype=BF):
    return jax.ShapeDtypeStruct(shape, dtype)


SMEM = pl.BlockSpec(memory_space=pltpu.SMEM)
VMEM = pl.BlockSpec(memory_space=pltpu.VMEM)


def span(i, size=PAIR):
    return slice(i * size, (i + 1) * size)


def flip_core(x):
    n = x.shape[-1] // PAIR
    return jnp.concatenate([x[..., span(i ^ 1)] for i in range(n)], axis=-1)


def whole(shape):
    return pl.BlockSpec(shape, lambda i: (0,) * len(shape))


X, Y, Z, CORE, SEQ = range(5)
EXTRA = 16


def split_parts(d):
    high = d.astype(BF).astype(F32)
    mid = (d - high).astype(BF).astype(F32)
    return high, mid, d - high - mid


def pack_kernel(at_ref, q_ref, g_ref, o_ref, qk_ref, qs_ref, gk_ref, gs_ref):
    low = at_ref[X] == 0
    rows = q_ref.shape[0]
    pairs = qk_ref.shape[1] // PAIR
    for p in range(pairs):
        scale = jnp.asarray(SCALE, BF)
        a, b = q_ref[:, span(2 * p)] * scale, q_ref[:, span(2 * p + 1)] * scale
        qk_ref[:, span(p)] = jnp.where(low, a, b)
        qs_ref[:, span(p)] = jnp.where(low, b, a)
        a, b = g_ref[:, span(2 * p)], g_ref[:, span(2 * p + 1)]
        gk_ref[:rows, span(p)] = jnp.where(low, a, b)
        gs_ref[:rows, span(p)] = jnp.where(low, b, a)
    cols = (g_ref[...].astype(F32) * o_ref[...].astype(F32)).T
    for p in range(pairs):
        both = []
        for h in range(4):
            both.append(split_parts(jnp.sum(cols[span(4 * p + h, HD)], axis=0, keepdims=True)))
        pad = [jnp.zeros((EXTRA - 6, rows), F32)]
        a = jnp.concatenate([both[h][n] for n in range(3) for h in (0, 1)] + pad, axis=0).astype(BF)
        b = jnp.concatenate([both[h][n] for n in range(3) for h in (2, 3)] + pad, axis=0).astype(BF)
        gk_ref[rows:, span(p)] = jnp.where(low, a, b)
        gs_ref[rows:, span(p)] = jnp.where(low, b, a)


def pack(at, queries, grad_out, attn_out):
    rows, cols = queries.shape
    steps = 2
    block = pl.BlockSpec((rows, cols // steps), lambda i: (0, i))
    half = lambda n: pl.BlockSpec((n, cols // 2 // steps), lambda i: (0, i))
    return pl.pallas_call(
        pack_kernel,
        grid=(steps,),
        in_specs=[SMEM] + [block] * 3,
        out_specs=[half(rows)] * 2 + [half(rows + EXTRA)] * 2,
        out_shape=[like((rows, cols // 2))] * 2 + [like((rows + EXTRA, cols // 2))] * 2,
        compiler_params=params(),
        cost_estimate=cost(),
    )(at, queries, grad_out, attn_out)


def pack_tokens_kernel(at_ref, k_ref, v_ref, kp_ref, vp_ref, kt_ref):
    low = at_ref[X] == 0
    for p in range(kp_ref.shape[1] // PAIR):
        k = jnp.where(low, k_ref[:, span(2 * p)], k_ref[:, span(2 * p + 1)])
        kp_ref[:, span(p)] = k
        kt_ref[span(p)] = k.T
        vp_ref[:, span(p)] = jnp.where(low, v_ref[:, span(2 * p)], v_ref[:, span(2 * p + 1)])


def pack_tokens(at, keys, values):
    tokens, cols = keys.shape
    steps = 2
    block = pl.BlockSpec((tokens, cols // steps), lambda i: (0, i))
    half = pl.BlockSpec((tokens, cols // 2 // steps), lambda i: (0, i))
    return pl.pallas_call(
        pack_tokens_kernel,
        grid=(steps,),
        in_specs=[SMEM, block, block],
        out_specs=[half, half, pl.BlockSpec((cols // 2 // steps, tokens), lambda i: (i, 0))],
        out_shape=[like((tokens, cols // 2))] * 2 + [like((cols // 2, tokens))],
        compiler_params=params(),
        cost_estimate=cost(),
    )(at, keys, values)


def add_kernel(*refs):
    total = refs[0][...].astype(F32)
    for r in refs[1:-1]:
        total = total + r[...].astype(F32)
    refs[-1][...] = total.astype(BF)


def add(*parts):
    return pl.pallas_call(
        add_kernel,
        in_specs=[VMEM] * len(parts),
        out_specs=VMEM,
        out_shape=like(parts[0].shape),
        compiler_params=params(),
        cost_estimate=cost(),
    )(*parts)


def stack_kernel(cuts, *refs):
    out_ref, row = refs[-1], 0
    for r, cut in zip(refs[:-1], cuts, strict=True):
        block = r[...] if cut is None else r[:, cut]
        out_ref[row : row + block.shape[0], :] = block
        row += block.shape[0]


def stack(parts, cuts=None):
    cuts = cuts or [None] * len(parts)
    rows = sum(t.shape[0] for t in parts)
    width = parts[0].shape[1] if cuts[0] is None else cuts[0].stop - cuts[0].start
    return pl.pallas_call(
        functools.partial(stack_kernel, cuts),
        in_specs=[VMEM] * len(parts),
        out_specs=VMEM,
        out_shape=like((rows, width)),
        compiler_params=params(),
        cost_estimate=cost(),
    )(*parts)


def side_kernel(count, step, last, *refs):
    q_refs, k_ref = refs[:count], refs[count]
    if last:
        la_ref, p_ref, m_ref, lse_ref, send_ref = refs[count + 1 :]
    else:
        p_ref, m_ref, lse_ref = refs[count + 1 :]
    for j in range(step):
        q = jnp.concatenate([r[:, span(j)] for r in q_refs], axis=0)
        k = k_ref[:, span(j)]
        for head in range(2):
            s = dot(own_lanes(k, head), q, 1, 1)
            top = jnp.max(s, axis=0, keepdims=True)
            p = jnp.exp(s - top)
            total = jnp.sum(p, axis=0, keepdims=True)
            p_ref[2 * j + head] = p.astype(BF)
            m_ref[j, head] = top[0]
            lse_ref[j, head] = (top + jnp.log(total))[0]
    if last:
        send_ref[...] = jnp.concatenate([flip_core(la_ref[...]), flip_core(lse_ref[...])], axis=-1)


def side_of(pieces, keys, extra=None, step=2):
    count = len(pieces)
    piece, cols = pieces[0].shape
    tokens = keys.shape[0]
    rows, pairs = piece * count, cols // PAIR
    stat_spec = lambda n: pl.BlockSpec((step, 2, n), lambda i: (i, 0, 0))
    in_specs = [pl.BlockSpec((piece, step * PAIR), lambda i: (0, i))] * count
    in_specs += [pl.BlockSpec((tokens, step * PAIR), lambda i: (0, i))]
    out_specs = [pl.BlockSpec((2 * step, tokens, rows), lambda i: (i, 0, 0)), stat_spec(rows), stat_spec(rows)]
    out_shape = [like((2 * pairs, tokens, rows)), like((pairs, 2, rows), F32), like((pairs, 2, rows), F32)]
    args = [*pieces, keys]
    if extra is not None:
        in_specs += [stat_spec(rows)]
        out_specs += [stat_spec(2 * rows)]
        out_shape += [like((pairs, 2, 2 * rows), F32)]
        args += [extra]
    return pl.pallas_call(
        functools.partial(side_kernel, count, step, extra is not None),
        grid=(pairs // step,),
        in_specs=in_specs,
        out_specs=out_specs,
        out_shape=out_shape,
        compiler_params=params(),
        cost_estimate=cost(2 * rows * tokens * cols, 4 * rows * tokens * pairs, 2 * rows * tokens * pairs),
    )(*args)


def log_add(a, b):
    top = jnp.maximum(a, b)
    return top + jnp.log(jnp.exp(a - top) + jnp.exp(b - top))


def merge_kernel(la_ref, lb_ref, got_ref, send_ref):
    side = la_ref.shape[2]
    send_ref[:, :, :side] = log_add(lb_ref[...], got_ref[:, :, side:])
    send_ref[:, :, side:] = log_add(la_ref[...], got_ref[:, :, :side])


def merge(la, lb, got):
    pairs, two, side = la.shape
    return pl.pallas_call(
        merge_kernel,
        in_specs=[VMEM] * 3,
        out_specs=VMEM,
        out_shape=like((pairs, two, 2 * side), F32),
        compiler_params=params(),
        cost_estimate=cost(1000, 100000),
    )(la, lb, got)


def half_kernel(count, at_ref, *refs):
    q_refs, g_refs = refs[:count], refs[count : 2 * count]
    pa_ref, pb_ref, v_ref, kt_ref, ma_ref, mb_ref, sent_ref, got_ref = refs[2 * count : 2 * count + 8]
    kv_refs, dqs_ref, dqk_ref = refs[2 * count + 8 : -2], refs[-2], refs[-1]
    side = ma_ref.shape[2]
    z = at_ref[Z]
    v = v_ref[...]
    tokens = v.shape[0]
    dk = jnp.zeros((tokens, PAIR), F32)
    dv = jnp.zeros((tokens, PAIR), F32)
    first = lax.broadcasted_iota(jnp.int32, (PAIR, side), 0) < HD
    halves = []
    for b, p_ref, m_ref in ((0, pa_ref, ma_ref), (1, pb_ref, mb_ref)):
        lse = log_add(sent_ref[0, :, span(1 - b, side)], got_ref[0, :, span(b, side)])
        w = jnp.exp(m_ref[0] - lse)
        wide = jnp.where(first, w[0:1], w[1:2]).T
        at = slice(b * count // 2, (b + 1) * count // 2)
        q = jnp.concatenate([r[...] for r in q_refs[at]], axis=0)
        g = jnp.concatenate([r[: r.shape[0] - EXTRA] for r in g_refs[at]], axis=0)
        parts = [r[r.shape[0] - EXTRA :].astype(F32) for r in g_refs[at]]
        delta = jnp.concatenate([d[0:2] + d[2:4] + d[4:6] for d in parts], axis=1)
        qw = (q.astype(F32) * wide).astype(BF)
        gw = (g.astype(F32) * wide).astype(BF)
        parts = []
        for head in range(2):
            p = p_ref[head]
            dp = dot(v, own_lanes(g, head), 1, 1)
            t = (p.astype(F32) * (dp - delta[head : head + 1])).astype(BF)
            dv = dv + dot(p, own_lanes(gw, head), 1, 0)
            dk = dk + dot(t, own_lanes(qw, head), 1, 0)
            dq = dot(kt_ref[span(head, HD)], t, 1, 0)
            parts.append((dq * (w[head : head + 1] * SCALE)).astype(BF))
        halves.append(jnp.concatenate(parts, axis=0))
    dq = jnp.concatenate(halves, axis=1)

    @pl.when(pl.program_id(0) == 0)
    def _():
        dqs_ref[...] = flip_core(dq)

    @pl.when(pl.program_id(0) == 1)
    def _():
        dqk_ref[...] = dq

    both = jnp.concatenate([dk.astype(BF), dv.astype(BF)], axis=0)
    size = both.shape[0] // len(kv_refs)
    for k, ref in enumerate(kv_refs):
        out = both[:size]
        for j in range(1, len(kv_refs)):
            out = jnp.where((z ^ k) == j, both[span(j, size)], out)
        ref[...] = out


def half_of(at, own, high, q_pieces, g_pieces, pa, pb, vp, kt, ma, mb, sent, got):
    count = len(q_pieces)
    piece, cols = q_pieces[0].shape
    tokens = vp.shape[0]
    side = ma.shape[2]
    bit = lambda i, a: (i + 1 + a[CORE]) % 2
    pair = lambda i, a: 2 * (a[Y] if own else 1 - a[Y]) + bit(i, a)
    extra_spec = pl.BlockSpec((piece + EXTRA, PAIR), lambda i, a: (0, pair(i, a)))
    row_spec = pl.BlockSpec((piece, PAIR), lambda i, a: (0, pair(i, a)))
    p_spec = pl.BlockSpec((2, tokens, side), lambda i, a: (pair(i, a), 0, 0))
    stat_spec = lambda n: pl.BlockSpec((1, 2, n), lambda i, a: (pair(i, a), 0, 0))
    block = 2 * tokens // high
    return pl.pallas_call(
        functools.partial(half_kernel, count),
        grid_spec=pltpu.PrefetchScalarGridSpec(
            num_scalar_prefetch=1,
            grid=(2,),
            in_specs=[row_spec] * count
            + [extra_spec] * count
            + [
                p_spec,
                p_spec,
                pl.BlockSpec((tokens, PAIR), lambda i, a: (0, pair(i, a))),
                pl.BlockSpec((PAIR, tokens), lambda i, a: (pair(i, a), 0)),
                stat_spec(side),
                stat_spec(side),
                stat_spec(2 * side),
                stat_spec(2 * side),
            ],
            out_specs=[pl.BlockSpec((block, PAIR), lambda i, a: (0, bit(i, a)))] * high
            + [pl.BlockSpec((PAIR, 2 * side), lambda i, a: (0, 0))] * 2,
        ),
        out_shape=[like((block, 2 * PAIR))] * high + [like((PAIR, 2 * side))] * 2,
        compiler_params=params(),
        cost_estimate=cost(16 * side * tokens * 2 * PAIR * 2, 8 * side * tokens * 2, 0),
    )(at, *q_pieces, *g_pieces, pa, pb, vp, kt, ma, mb, sent, got)


def columns_kernel(count, high, at_ref, *refs):
    x_refs = refs[:count]
    keep_ref, core_ref, y_ref = refs[count : count + 3]
    w_refs, back_ref, send_ref, all_ref = refs[count + 3 : -3], refs[-3], refs[-2], refs[-1]
    side = keep_ref.shape[1] // 2
    far = jnp.concatenate([y_ref[:, side:], y_ref[:, :side]], axis=1)
    dq = (keep_ref[...].astype(F32) + core_ref[...].astype(F32) + far.astype(F32)).astype(BF)
    quarter = side // 2
    back_ref[...] = jnp.concatenate([dq[:, span(0, quarter)], dq[:, span(2, quarter)]], axis=1)
    send_ref[...] = jnp.concatenate([dq[:, span(1, quarter)], dq[:, span(3, quarter)]], axis=1)
    x = jnp.concatenate([r[...] for r in x_refs], axis=0)
    all_ref[...] = dot(dq, x, 1, 0)
    width = x.shape[1] // high
    for k, ref in enumerate(w_refs):
        start = pl.multiple_of((at_ref[Z] ^ k) * width, PAIR)
        ref[...] = all_ref[:, pl.ds(start, width)].astype(BF)


def columns_of(at, high, x_pieces, keep, core, y):
    count = len(x_pieces)
    piece, cols = x_pieces[0].shape
    width, rows = keep.shape
    return pl.pallas_call(
        functools.partial(columns_kernel, count, high),
        in_specs=[SMEM] + [VMEM] * (count + 3),
        out_specs=[VMEM] * (high + 2),
        out_shape=[like((width, cols // high))] * high + [like((width, rows // 2))] * 2,
        scratch_shapes=[pltpu.VMEM((width, cols), F32)],
        compiler_params=params(),
        cost_estimate=cost(2 * rows * cols * width, 2 * rows * cols),
    )(at, *x_pieces, keep, core, y)


def input_kernel(at_ref, back_ref, x_ref, y_ref, core_ref, wq_ref, out_ref, dq_ref):
    me, x = at_ref[SEQ], at_ref[X]
    size = back_ref.shape[0]

    def put(group, odd, block):
        row = pl.multiple_of((2 * group + (x ^ odd)) * size, PAIR)
        dq_ref[pl.ds(row, size), :] = block

    put(me, 0, back_ref[:, :size])
    put(me, 1, x_ref[:, :size])
    for odd in range(2):
        put(me ^ 2, odd, y_ref[span(odd, size), :size])
        put(me ^ 1, odd, core_ref[span(odd, size), :])
        put(me ^ 3, odd, core_ref[span(2 + odd, size), :])
    out_ref[...] = dot(dq_ref[...], wq_ref[...], 0, 1).astype(BF)


def input_of(at, back, x, y, core, wq):
    size, cols = back.shape[0], wq.shape[1]
    return pl.pallas_call(
        input_kernel,
        in_specs=[SMEM] + [VMEM] * 5,
        out_specs=VMEM,
        out_shape=like((size, cols)),
        scratch_shapes=[pltpu.VMEM((cols, size), BF)],
        compiler_params=params(),
        cost_estimate=cost(2 * size * cols * cols, 2 * cols * cols),
    )(at, back, x, y, core, wq)


def weight_sum_kernel(at_ref, *refs):
    total = refs[0][...].astype(F32)
    for r in refs[1:-2]:
        total = total + r[...].astype(F32)
    keep_ref, send_ref = refs[-2:]
    size = keep_ref.shape[1]
    a, b = total[:, :size], total[:, size:]
    low = at_ref[X] == 0
    keep_ref[...] = jnp.where(low, a, b)
    send_ref[...] = jnp.where(low, b, a).astype(BF)


def weight_sum(at, parts):
    rows, cols = parts[0].shape
    return pl.pallas_call(
        weight_sum_kernel,
        in_specs=[SMEM] + [VMEM] * len(parts),
        out_specs=[VMEM] * 2,
        out_shape=[like((rows, cols // 2), F32), like((rows, cols // 2))],
        compiler_params=params(),
        cost_estimate=cost(1000, 300000),
    )(at, *parts)


def weight_out_kernel(at_ref, keep_ref, got_ref, out_ref):
    size = keep_ref.shape[0]
    a, b = keep_ref[...].T, got_ref[...].astype(F32).T
    low = at_ref[X] == 0
    out_ref[:, :size] = jnp.where(low, a, b)
    out_ref[:, size:] = jnp.where(low, b, a)


def weight_out(at, keep, got):
    size, rows = keep.shape
    return pl.pallas_call(
        weight_out_kernel,
        in_specs=[SMEM, VMEM, VMEM],
        out_specs=VMEM,
        out_shape=like((rows, 2 * size), F32),
        compiler_params=params(),
        cost_estimate=cost(1000, 300000),
    )(at, keep, got)


def tokens_kernel(high, at_ref, *refs):
    y, x, z = at_ref[Y], at_ref[X], at_ref[Z]
    key_ref, val_ref = refs[-2:]
    size = refs[0].shape[0]
    each = high + 1
    for half in range(2):
        group = 2 * (y ^ (1 - half))
        own, got = refs[half * each : half * each + high], refs[half * each + high]
        for k in range(high):
            b = z ^ k
            row = pl.multiple_of((b % (high // 2)) * size, 16)
            for out_ref, which in ((key_ref, 0), (val_ref, 1)):

                @pl.when(b // (high // 2) == which)
                def _():
                    for c in range(2):
                        for odd, block in ((0, own[k][:, span(c)]), (1, got[span(k, size), span(c)])):
                            col = pl.multiple_of((2 * (group + c) + (x ^ odd)) * PAIR, PAIR)
                            out_ref[pl.ds(row, size), pl.ds(col, PAIR)] = block


def tokens_out(at, high, tokens, cols, parts):
    return pl.pallas_call(
        functools.partial(tokens_kernel, high),
        in_specs=[SMEM] + [VMEM] * len(parts),
        out_specs=[VMEM] * 2,
        out_shape=[like((tokens, cols))] * 2,
        compiler_params=params(),
        cost_estimate=cost(1000, 8 * tokens * cols),
    )(at, *parts)


def local_split(n_dp, n_seq, qx, queries, keys, values, attn_out, grad_out, wq):
    high = n_dp // 2
    dp, me = lax.axis_index("dp").astype(jnp.int32), lax.axis_index("seq").astype(jnp.int32)
    at = jnp.stack([dp % 2, me // 2, dp // 2, me % 2, me])
    over_x = lambda t: swap(t, "dp", n_dp, 1)
    over_y = lambda t: swap(t, "seq", n_seq, 2)
    over_core = lambda t: swap(t, "seq", n_seq, 1)
    over_z = lambda t, k: swap(t, "dp", n_dp, 2 * k)
    after = lambda t, *deps: lax.optimization_barrier((t, *deps))[0]

    def rows_of(own, from_x):
        from_y, from_xy = over_y(own), over_y(from_x)
        a = [own, over_core(own), from_x, over_core(from_x)]
        return a, [from_y, over_core(from_y), from_xy, over_core(from_xy)]

    qk, qs, gk, gs = pack(at, queries, grad_out, attn_out)
    kp, vp, kt = pack_tokens(at, keys, values)
    q_from_x = after(over_x(qs), kp)
    qa, qb = rows_of(qk, q_from_x)
    ga, gb = rows_of(after(gk, q_from_x), over_x(after(gs, q_from_x)))
    pa, ma, la = side_of(qa, kp)
    pb, mb, lb, sent = side_of(qb, kp, la)
    send = merge(la, lb, over_core(sent))
    got = over_y(send)

    sums, dqs = [], []
    for own in (False, True):
        out = half_of(at, own, high, qa + qb, ga + gb, pa, pb, vp, kt, ma, mb, send, got)
        sums.append(add(out[0], *[over_z(out[k], k) for k in range(1, high)]))
        dqs.append((out[high + 1], over_core(out[high])))

    far = over_y(add(*dqs[0]))
    qx_from_x = over_x(after(qx, la))
    xa, xb = rows_of(after(qx, got), after(qx_from_x, got))
    *parts, back, back_s = columns_of(at, high, xa + xb, *dqs[1], far)
    parts = parts[:1] + [over_z(parts[k], k) for k in range(1, high)]
    keep, send_w = weight_sum(at, parts)
    grad_weight = weight_out(at, keep, over_x(send_w))

    size = back.shape[0]
    from_x = over_x(back_s)
    far_cut = slice(2 * size, 4 * size)
    from_y = over_y(stack([back, from_x], [far_cut, far_cut]))
    near = slice(size, 2 * size)
    from_core = over_core(stack([back, from_x, from_y], [near, near, near]))
    grad_input = input_of(at, back, from_x, from_y, from_core, wq)

    parts = []
    for total in sums:
        blocks = [total] + [over_z(total, k) for k in range(1, high)]
        parts += blocks + [over_x(stack(blocks))]
    grad_keys, grad_values = tokens_out(at, high, *keys.shape, parts)
    return (grad_input, grad_keys, grad_values, grad_weight)


def solution(mesh):
    n_dp, n_seq = mesh.shape["dp"], mesh.shape["seq"]

    def run(qx, queries, keys, *rest):
        pairs = queries.shape[1] == 2 * n_seq * PAIR and queries.shape[0] == n_dp * n_seq * PAIR
        split = n_seq == 4 and n_dp == 8 and pairs and (2 * keys.shape[0] // n_seq) % (16 * n_dp // 2) == 0
        return shard(local_split if split else local)(qx, queries, keys, *rest)

    def shard(f):
        return jax.shard_map(
            functools.partial(f, n_dp, n_seq),
            mesh=mesh,
            in_specs=(
                P(("dp", "seq"), None),
                P(("dp", "seq"), None),
                P("seq", None),
                P("seq", None),
                P(("dp", "seq"), None),
                P(("dp", "seq"), None),
                P(),
            ),
            out_specs=(P(("dp", "seq"), None), P("seq", None), P("seq", None), P("dp", "seq")),
            check_vma=False,
        )

    return run
```

```python
import functools
import math

import jax
import jax.numpy as jnp
from jax import lax
from jax.experimental import pallas as pl
from jax.experimental.pallas import tpu as pltpu
from jax.sharding import PartitionSpec as P

HD = 64
PAIR = 2 * HD
SCALE = 1.0 / math.sqrt(HD)
BF = jnp.bfloat16
F32 = jnp.float32
VMEM_LIMIT = 56 * 1024 * 1024


def dot(a, b, ca, cb):
    return lax.dot_general(a, b, (((ca,), (cb,)), ((), ())), preferred_element_type=F32)


def own_lanes(x, head):
    lane = lax.broadcasted_iota(jnp.int32, x.shape, 1)
    mine = lane < HD if head == 0 else lane >= HD
    return jnp.where(mine, x, jnp.zeros_like(x))


def delta_kernel(grad_ref, out_ref, delta_ref):
    prod = grad_ref[...].astype(F32) * out_ref[...].astype(F32)
    cols = prod.T
    heads = cols.shape[0] // HD
    for head in range(heads):
        part = jnp.sum(cols[head * HD : (head + 1) * HD], axis=0, keepdims=True)
        delta_ref[head // 2, head % 2] = part[0]


def delta_of(grad_out, attn_out):
    rows, cols = grad_out.shape
    return pl.pallas_call(
        delta_kernel,
        out_shape=jax.ShapeDtypeStruct((cols // PAIR, 2, rows), F32),
        compiler_params=pltpu.CompilerParams(vmem_limit_bytes=VMEM_LIMIT),
        cost_estimate=pl.CostEstimate(flops=4 * rows * cols, bytes_accessed=4 * rows * cols, transcendentals=0),
    )(grad_out, attn_out)


def probs_kernel(count, *refs):
    q_refs, k_ref = refs[:count], refs[count]
    p_ref, m_ref, lse_ref = refs[count + 1 :]
    q = jnp.concatenate([r[...] for r in q_refs], axis=0) * jnp.asarray(SCALE, BF)
    k = k_ref[...]
    for head in range(2):
        s = dot(own_lanes(k, head), q, 1, 1)
        top = jnp.max(s, axis=0, keepdims=True)
        p = jnp.exp(s - top)
        total = jnp.sum(p, axis=0, keepdims=True)
        p_ref[head] = p.astype(BF)
        m_ref[0, head] = top[0]
        lse_ref[0, head] = (top + jnp.log(total))[0]


def probs_of(q_pieces, keys):
    count = len(q_pieces)
    piece, cols = q_pieces[0].shape
    tokens = keys.shape[0]
    rows = piece * count
    pairs = cols // PAIR
    return pl.pallas_call(
        functools.partial(probs_kernel, count),
        grid=(pairs,),
        in_specs=[pl.BlockSpec((piece, PAIR), lambda i: (0, i))] * count
        + [pl.BlockSpec((tokens, PAIR), lambda i: (0, i))],
        out_specs=[
            pl.BlockSpec((2, tokens, rows), lambda i: (i, 0, 0)),
            pl.BlockSpec((1, 2, rows), lambda i: (i, 0, 0)),
            pl.BlockSpec((1, 2, rows), lambda i: (i, 0, 0)),
        ],
        out_shape=[
            jax.ShapeDtypeStruct((2 * pairs, tokens, rows), BF),
            jax.ShapeDtypeStruct((pairs, 2, rows), F32),
            jax.ShapeDtypeStruct((pairs, 2, rows), F32),
        ],
        compiler_params=pltpu.CompilerParams(vmem_limit_bytes=VMEM_LIMIT),
        cost_estimate=pl.CostEstimate(
            flops=2 * rows * tokens * cols,
            bytes_accessed=2 * rows * tokens * 2 * pairs,
            transcendentals=rows * tokens * 2 * pairs,
        ),
    )(*q_pieces, keys)


def grads_kernel(count, half_ref, *refs):
    q_refs, g_refs = refs[:count], refs[count : 2 * count]
    pa_ref, pb_ref, v_ref, kt_ref, w_ref, delta_ref, dkv_ref, dqt_ref = refs[2 * count :]
    rows = w_ref.shape[2]
    side = rows // 2
    w = w_ref[0]
    delta = delta_ref[0]
    v = v_ref[...]
    first = lax.broadcasted_iota(jnp.int32, (PAIR, rows), 0) < HD
    wide = jnp.where(first, w[0:1], w[1:2]).T
    q = jnp.concatenate([r[...] for r in q_refs], axis=0)
    g = jnp.concatenate([r[...] for r in g_refs], axis=0)
    qw = (q.astype(F32) * (wide * SCALE)).astype(BF)
    gw = (g.astype(F32) * wide).astype(BF)
    dk = jnp.zeros((v.shape[0], PAIR), F32)
    dv = jnp.zeros((v.shape[0], PAIR), F32)
    for half, p_ref in ((0, pa_ref), (1, pb_ref)):
        at = slice(half * side, (half + 1) * side)
        for head in range(2):
            p = p_ref[head]
            dp = dot(v, own_lanes(g[at], head), 1, 1)
            t = (p.astype(F32) * (dp - delta[head : head + 1, at])).astype(BF)
            dv = dv + dot(p, own_lanes(gw[at], head), 1, 0)
            dk = dk + dot(t, own_lanes(qw[at], head), 1, 0)
            dq = dot(kt_ref[head * HD : (head + 1) * HD], t, 1, 0)
            dq = dq * (w[head : head + 1, at] * SCALE)
            dqt_ref[head * HD : (head + 1) * HD, at] = dq.astype(BF)
    dkv_ref[0] = dk.astype(BF)
    dkv_ref[1] = dv.astype(BF)


def grads_of(half, q_pieces, g_pieces, pa, pb, values, keys_t, w, delta):
    count = len(q_pieces)
    piece, cols = q_pieces[0].shape
    tokens = values.shape[0]
    rows = piece * count
    steps = cols // PAIR // 2
    at = lambda i, h: h[0] * steps + i
    row_spec = pl.BlockSpec((piece, PAIR), lambda i, h: (0, at(i, h)))
    p_spec = pl.BlockSpec((2, tokens, rows // 2), lambda i, h: (at(i, h), 0, 0))
    stat_spec = pl.BlockSpec((1, 2, rows), lambda i, h: (at(i, h), 0, 0))
    return pl.pallas_call(
        functools.partial(grads_kernel, count),
        grid_spec=pltpu.PrefetchScalarGridSpec(
            num_scalar_prefetch=1,
            grid=(steps,),
            in_specs=[row_spec] * (2 * count)
            + [
                p_spec,
                p_spec,
                pl.BlockSpec((tokens, PAIR), lambda i, h: (0, at(i, h))),
                pl.BlockSpec((PAIR, tokens), lambda i, h: (at(i, h), 0)),
                stat_spec,
                stat_spec,
            ],
            out_specs=[
                pl.BlockSpec((2, tokens, PAIR), lambda i, h: (0, 0, i)),
                pl.BlockSpec((PAIR, rows), lambda i, h: (i, 0)),
            ],
        ),
        out_shape=[
            jax.ShapeDtypeStruct((2, tokens, cols // 2), BF),
            jax.ShapeDtypeStruct((cols // 2, rows), BF),
        ],
        compiler_params=pltpu.CompilerParams(vmem_limit_bytes=VMEM_LIMIT),
        cost_estimate=pl.CostEstimate(
            flops=4 * rows * tokens * cols,
            bytes_accessed=2 * rows * tokens * 2 * steps,
            transcendentals=0,
        ),
    )(half, *q_pieces, *g_pieces, pa, pb, values, keys_t, w, delta)


def weight_kernel(count, *refs):
    x = jnp.concatenate([r[...] for r in refs[:count]], axis=0)
    refs[count + 1][...] = dot(x, refs[count][...], 0, 1).astype(BF)


def weight_of(x_pieces, dq_cols):
    count = len(x_pieces)
    piece, cols = x_pieces[0].shape
    width, rows = dq_cols.shape
    step = min(cols, 256)
    return pl.pallas_call(
        functools.partial(weight_kernel, count),
        grid=(cols // step,),
        in_specs=[pl.BlockSpec((piece, step), lambda i: (0, i))] * count
        + [pl.BlockSpec((width, rows), lambda i: (0, 0))],
        out_specs=pl.BlockSpec((step, width), lambda i: (i, 0)),
        out_shape=jax.ShapeDtypeStruct((cols, width), BF),
        compiler_params=pltpu.CompilerParams(vmem_limit_bytes=VMEM_LIMIT),
        cost_estimate=pl.CostEstimate(
            flops=2 * rows * cols * width, bytes_accessed=2 * rows * cols, transcendentals=0
        ),
    )(*x_pieces, dq_cols)


def swap(x, axis, size, mask):
    return lax.ppermute(x, axis, [(i, i ^ mask) for i in range(size)])


def gather_pieces(x, axis, size):
    pieces = {0: x}
    bit = size // 2
    while bit:
        for k in list(pieces):
            pieces[k | bit] = swap(pieces[k], axis, size, bit)
        bit //= 2
    return [pieces[k] for k in range(size)]


def flip_pieces(x, count, bit):
    lead, piece = x.shape[:-1], x.shape[-1] // count
    y = x.reshape(lead + (count // (2 * bit), 2, bit * piece))
    return jnp.flip(y, axis=-2).reshape(x.shape)


def pick(blocks, index):
    return lax.dynamic_index_in_dim(blocks, index, 0, keepdims=False)


def exchange_sum(x, axis, size, stride, group, wide=False):
    me = (lax.axis_index(axis) // stride) % group
    total = pick(x, me).astype(F32)
    for k in range(1, group):
        total = total + swap(pick(x, me ^ k), axis, size, k * stride).astype(F32)
    return total if wide else total.astype(BF)


def exchange_gather(x, axis, size, stride, group):
    me = (lax.axis_index(axis) // stride) % group
    out = jnp.zeros((group,) + x.shape, x.dtype)
    for k in range(group):
        got = x if k == 0 else swap(x, axis, size, k * stride)
        out = lax.dynamic_update_index_in_dim(out, got, me ^ k, 0)
    return out


def local(n_dp, n_seq, qx, queries, keys, values, attn_out, grad_out, wq):
    low = max(n_dp // 4, 1)
    high = n_dp // low
    cols = queries.shape[1]
    me = lax.axis_index("seq")
    top = n_seq // 2
    q_pieces = gather_pieces(queries, "seq", n_seq)
    g_pieces = gather_pieces(grad_out, "seq", n_seq)
    x_pieces = gather_pieces(qx, "seq", n_seq)
    keys_t = keys.T
    delta = delta_of(grad_out, attn_out)
    pa, ma, la = probs_of(q_pieces[:top], keys)
    pb, mb, lb = probs_of(q_pieces[top:], keys)
    rows = 2 * la.shape[2]
    peak = jnp.concatenate([ma, mb], axis=2)
    lse = jnp.concatenate([la, lb], axis=2)
    bit = 1
    while bit < n_seq:
        got = swap(jnp.concatenate([lse, delta], axis=2), "seq", n_seq, bit)
        lse = jnp.logaddexp(lse, flip_pieces(got[:, :, :rows], n_seq, bit))
        delta = jnp.concatenate([delta, got[:, :, rows:]], axis=2)
        bit *= 2
    w = jnp.exp(peak - lse)

    mine = (me // top).astype(jnp.int32)
    shards, dqs = [], []
    for half in (1 - mine, mine):
        dkv, dqt = grads_of(half.reshape(1), q_pieces, g_pieces, pa, pb, values, keys_t, w, delta)
        tokens = dkv.shape[1]
        part = dkv.reshape(low, 2 * tokens // low, cols // 2)
        part = exchange_sum(part, "dp", n_dp, 1, low)
        part = part.reshape(high, part.shape[0] // high, cols // 2)
        shards.append(exchange_sum(part, "dp", n_dp, low, high))
        dqs.append(dqt)

    def narrow(dqt):
        blocks = dqt.reshape(top, dqt.shape[0] // top, rows)
        bit = 1
        base = me % top
        while bit < top:
            view = blocks.reshape((blocks.shape[0] // 2, 2) + blocks.shape[1:])
            own = (base // bit) % 2
            keep = lax.dynamic_index_in_dim(view, own, 1, keepdims=False)
            send = lax.dynamic_index_in_dim(view, 1 - own, 1, keepdims=False)
            got = swap(send, "seq", n_seq, bit)
            got = flip_pieces(got, n_seq, bit)
            blocks = (keep.astype(F32) + got.astype(F32)).astype(BF)
            bit *= 2
        return blocks[0]

    other, own = narrow(dqs[0]), narrow(dqs[1])
    got = flip_pieces(swap(other, "seq", n_seq, top), n_seq, top)
    dq_cols = (own.astype(F32) + got.astype(F32)).astype(BF)

    weight = weight_of(x_pieces, dq_cols)
    weight = weight.reshape(high, low, weight.shape[0] // n_dp, weight.shape[1])
    weight = exchange_sum(weight, "dp", n_dp, low, high)
    grad_weight = exchange_sum(weight, "dp", n_dp, 1, low, wide=True)

    piece = rows // n_seq
    width = cols // n_seq
    dq_rows = jnp.zeros((n_seq, width, piece), BF)
    for k in range(n_seq):
        block = dq_cols[:, k * piece : (k + 1) * piece]
        block = block if k == 0 else swap(block, "seq", n_seq, k)
        dq_rows = lax.dynamic_update_index_in_dim(dq_rows, block, me ^ k, 0)
    grad_input = dot(dq_rows.reshape(cols, piece), wq, 0, 1).astype(BF)

    halves = []
    for shard in shards:
        part = exchange_gather(shard, "dp", n_dp, low, high)
        part = part.reshape((-1,) + part.shape[2:])
        part = exchange_gather(part, "dp", n_dp, 1, low)
        halves.append(part.reshape(2, -1, cols // 2))
    other, own = halves
    left = jnp.where(mine == 0, own, other)
    right = jnp.where(mine == 0, other, own)
    both = jnp.concatenate([left, right], axis=2)
    return (grad_input, both[0], both[1], grad_weight)


def params(limit=24):
    return pltpu.CompilerParams(vmem_limit_bytes=limit * 1024 * 1024)


def cost(flops=0, nbytes=0, exps=0):
    return pl.CostEstimate(flops=1, bytes_accessed=1, transcendentals=0)


def like(shape, dtype=BF):
    return jax.ShapeDtypeStruct(shape, dtype)


SMEM = pl.BlockSpec(memory_space=pltpu.SMEM)
VMEM = pl.BlockSpec(memory_space=pltpu.VMEM)


def span(i, size=PAIR):
    return slice(i * size, (i + 1) * size)


def flip_core(x):
    n = x.shape[-1] // PAIR
    return jnp.concatenate([x[..., span(i ^ 1)] for i in range(n)], axis=-1)


def whole(shape):
    return pl.BlockSpec(shape, lambda i: (0,) * len(shape))


X, Y, Z, CORE, SEQ = range(5)
EXTRA = 16
ORDERS = ((0, 2), (1, 3))


def split_parts(d):
    high = d.astype(BF).astype(F32)
    mid = (d - high).astype(BF).astype(F32)
    return high, mid, d - high - mid


def pack_kernel(at_ref, q_ref, g_ref, o_ref, qk_ref, qs_ref, gk_ref, gs_ref):
    low = at_ref[X] == 0
    rows = q_ref.shape[0]
    pairs = qk_ref.shape[1] // PAIR
    for p in range(pairs):
        scale = jnp.asarray(SCALE, BF)
        a, b = q_ref[:, span(2 * p)] * scale, q_ref[:, span(2 * p + 1)] * scale
        qk_ref[:, span(p)] = jnp.where(low, a, b)
        qs_ref[:, span(p)] = jnp.where(low, b, a)
        a, b = g_ref[:, span(2 * p)], g_ref[:, span(2 * p + 1)]
        gk_ref[:rows, span(p)] = jnp.where(low, a, b)
        gs_ref[:rows, span(p)] = jnp.where(low, b, a)
    cols = (g_ref[...].astype(F32) * o_ref[...].astype(F32)).T
    for p in range(pairs):
        both = []
        for h in range(4):
            both.append(split_parts(jnp.sum(cols[span(4 * p + h, HD)], axis=0, keepdims=True)))
        pad = [jnp.zeros((EXTRA - 6, rows), F32)]
        a = jnp.concatenate([both[h][n] for n in range(3) for h in (0, 1)] + pad, axis=0).astype(BF)
        b = jnp.concatenate([both[h][n] for n in range(3) for h in (2, 3)] + pad, axis=0).astype(BF)
        gk_ref[rows:, span(p)] = jnp.where(low, a, b)
        gs_ref[rows:, span(p)] = jnp.where(low, b, a)


def pack(at, queries, grad_out, attn_out):
    rows, cols = queries.shape
    steps = 2
    block = pl.BlockSpec((rows, cols // steps), lambda i: (0, i))
    half = lambda n: pl.BlockSpec((n, cols // 2 // steps), lambda i: (0, i))
    return pl.pallas_call(
        pack_kernel,
        grid=(steps,),
        in_specs=[SMEM] + [block] * 3,
        out_specs=[half(rows)] * 2 + [half(rows + EXTRA)] * 2,
        out_shape=[like((rows, cols // 2))] * 2 + [like((rows + EXTRA, cols // 2))] * 2,
        compiler_params=params(60),
        cost_estimate=cost(),
    )(at, queries, grad_out, attn_out)


def pack_tokens_kernel(at_ref, k_ref, v_ref, kp_ref, vp_ref, kt_ref):
    low = at_ref[X] == 0
    for p in range(kp_ref.shape[1] // PAIR):
        k = jnp.where(low, k_ref[:, span(2 * p)], k_ref[:, span(2 * p + 1)])
        kp_ref[:, span(p)] = k
        kt_ref[span(p)] = k.T
        vp_ref[:, span(p)] = jnp.where(low, v_ref[:, span(2 * p)], v_ref[:, span(2 * p + 1)])


def pack_tokens(at, keys, values):
    tokens, cols = keys.shape
    steps = 2
    block = pl.BlockSpec((tokens, cols // steps), lambda i: (0, i))
    half = pl.BlockSpec((tokens, cols // 2 // steps), lambda i: (0, i))
    return pl.pallas_call(
        pack_tokens_kernel,
        grid=(steps,),
        in_specs=[SMEM, block, block],
        out_specs=[half, half, pl.BlockSpec((cols // 2 // steps, tokens), lambda i: (i, 0))],
        out_shape=[like((tokens, cols // 2))] * 2 + [like((cols // 2, tokens))],
        compiler_params=params(),
        cost_estimate=cost(),
    )(at, keys, values)


def add_kernel(*refs):
    total = refs[0][...].astype(F32)
    for r in refs[1:-1]:
        total = total + r[...].astype(F32)
    refs[-1][...] = total.astype(BF)


def add(*parts):
    return pl.pallas_call(
        add_kernel,
        in_specs=[VMEM] * len(parts),
        out_specs=VMEM,
        out_shape=like(parts[0].shape),
        compiler_params=params(),
        cost_estimate=cost(),
    )(*parts)


def add_turned_kernel(own_ref, got_ref, out_ref):
    rows = own_ref.shape[0] // 2
    for n in range(2):
        total = own_ref[span(n, rows)].astype(F32) + got_ref[span(1 - n, rows)].astype(F32)
        out_ref[span(n, rows)] = total.astype(BF)


def add_turned(own, got):
    return pl.pallas_call(
        add_turned_kernel,
        in_specs=[VMEM] * 2,
        out_specs=VMEM,
        out_shape=like(own.shape),
        compiler_params=params(),
        cost_estimate=cost(),
    )(own, got)


def stack_kernel(cuts, *refs):
    out_ref, row = refs[-1], 0
    for r, cut in zip(refs[:-1], cuts, strict=True):
        block = r[...] if cut is None else r[cut]
        out_ref[row : row + block.shape[0], :] = block
        row += block.shape[0]


def stack(parts, cuts=None):
    cuts = cuts or [None] * len(parts)
    shapes = [jax.eval_shape(lambda t, c=c: t if c is None else t[c], t).shape for t, c in zip(parts, cuts, strict=True)]
    rows, width = sum(t[0] for t in shapes), shapes[0][1]
    return pl.pallas_call(
        functools.partial(stack_kernel, cuts),
        in_specs=[VMEM] * len(parts),
        out_specs=VMEM,
        out_shape=like((rows, width)),
        compiler_params=params(),
        cost_estimate=cost(),
    )(*parts)


def side_kernel(count, step, last, *refs):
    q_refs, k_ref = refs[:count], refs[count]
    if last:
        la_ref, p_ref, m_ref, lse_ref, send_ref = refs[count + 1 :]
    else:
        p_ref, m_ref, lse_ref = refs[count + 1 :]
    for j in range(step):
        q = jnp.concatenate([r[:, span(j)] for r in q_refs], axis=0)
        k = k_ref[:, span(j)]
        for head in range(2):
            s = dot(own_lanes(k, head), q, 1, 1)
            top = jnp.max(s, axis=0, keepdims=True)
            p = jnp.exp(s - top)
            total = jnp.sum(p, axis=0, keepdims=True)
            p_ref[2 * j + head] = p.astype(BF)
            m_ref[j, head] = top[0]
            lse_ref[j, head] = (top + jnp.log(total))[0]
    if last:
        send_ref[...] = jnp.concatenate([flip_core(la_ref[...]), flip_core(lse_ref[...])], axis=-1)


def side_of(pieces, keys, extra=None, step=2):
    count = len(pieces)
    piece, cols = pieces[0].shape
    tokens = keys.shape[0]
    rows, pairs = piece * count, cols // PAIR
    stat_spec = lambda n: pl.BlockSpec((step, 2, n), lambda i: (i, 0, 0))
    in_specs = [pl.BlockSpec((piece, step * PAIR), lambda i: (0, i))] * count
    in_specs += [pl.BlockSpec((tokens, step * PAIR), lambda i: (0, i))]
    out_specs = [pl.BlockSpec((2 * step, tokens, rows), lambda i: (i, 0, 0)), stat_spec(rows), stat_spec(rows)]
    out_shape = [like((2 * pairs, tokens, rows)), like((pairs, 2, rows), F32), like((pairs, 2, rows), F32)]
    args = [*pieces, keys]
    if extra is not None:
        in_specs += [stat_spec(rows)]
        out_specs += [stat_spec(2 * rows)]
        out_shape += [like((pairs, 2, 2 * rows), F32)]
        args += [extra]
    return pl.pallas_call(
        functools.partial(side_kernel, count, step, extra is not None),
        grid=(pairs // step,),
        in_specs=in_specs,
        out_specs=out_specs,
        out_shape=out_shape,
        compiler_params=params(),
        cost_estimate=cost(2 * rows * tokens * cols, 4 * rows * tokens * pairs, 2 * rows * tokens * pairs),
    )(*args)


def log_add(a, b):
    top = jnp.maximum(a, b)
    return top + jnp.log(jnp.exp(a - top) + jnp.exp(b - top))


def merge_kernel(la_ref, lb_ref, got_ref, send_ref):
    side = la_ref.shape[2]
    send_ref[:, :, :side] = log_add(lb_ref[...], got_ref[:, :, side:])
    send_ref[:, :, side:] = log_add(la_ref[...], got_ref[:, :, :side])


def merge(la, lb, got):
    pairs, two, side = la.shape
    return pl.pallas_call(
        merge_kernel,
        in_specs=[VMEM] * 3,
        out_specs=VMEM,
        out_shape=like((pairs, two, 2 * side), F32),
        compiler_params=params(),
        cost_estimate=cost(1000, 100000),
    )(la, lb, got)


def half_kernel(count, at_ref, *refs):
    q_refs, g_refs = refs[:count], refs[count : 2 * count]
    pa_ref, pb_ref, v_ref, kt_ref, ma_ref, mb_ref, sent_ref, got_ref = refs[2 * count : 2 * count + 8]
    kv_refs, dqs_ref, dqk_ref = refs[2 * count + 8 : -2], refs[-2], refs[-1]
    side = ma_ref.shape[2]
    z = at_ref[Z]
    v = v_ref[...]
    tokens = v.shape[0]
    dk = jnp.zeros((tokens, PAIR), F32)
    dv = jnp.zeros((tokens, PAIR), F32)
    first = lax.broadcasted_iota(jnp.int32, (PAIR, side), 0) < HD
    halves = []
    for b, p_ref, m_ref in ((0, pa_ref, ma_ref), (1, pb_ref, mb_ref)):
        lse = log_add(sent_ref[0, :, span(1 - b, side)], got_ref[0, :, span(b, side)])
        w = jnp.exp(m_ref[0] - lse)
        wide = jnp.where(first, w[0:1], w[1:2]).T
        at = slice(b * count // 2, (b + 1) * count // 2)
        q = jnp.concatenate([r[...] for r in q_refs[at]], axis=0)
        g = jnp.concatenate([r[: r.shape[0] - EXTRA] for r in g_refs[at]], axis=0)
        parts = [r[r.shape[0] - EXTRA :].astype(F32) for r in g_refs[at]]
        delta = jnp.concatenate([d[0:2] + d[2:4] + d[4:6] for d in parts], axis=1)
        qw = (q.astype(F32) * wide).astype(BF)
        gw = (g.astype(F32) * wide).astype(BF)
        parts = []
        for head in range(2):
            p = p_ref[head]
            dp = dot(v, own_lanes(g, head), 1, 1)
            t = (p.astype(F32) * (dp - delta[head : head + 1])).astype(BF)
            dv = dv + dot(p, own_lanes(gw, head), 1, 0)
            dk = dk + dot(t, own_lanes(qw, head), 1, 0)
            dq = dot(kt_ref[span(head, HD)], t, 1, 0)
            parts.append((dq * (w[head : head + 1] * SCALE)).astype(BF))
        halves.append(jnp.concatenate(parts, axis=0))
    dq = jnp.concatenate(halves, axis=1)

    @pl.when(pl.program_id(0) == 0)
    def _():
        dqs_ref[...] = flip_core(dq)

    @pl.when(pl.program_id(0) == 1)
    def _():
        dqk_ref[...] = dq

    both = jnp.concatenate([dk.astype(BF), dv.astype(BF)], axis=0)
    size = both.shape[0] // 4
    for ref, order in zip(kv_refs, ORDERS, strict=True):
        for n, k in enumerate(order):
            out = both[:size]
            for j in range(1, 4):
                out = jnp.where((z ^ k) == j, both[span(j, size)], out)
            ref[span(n, size)] = out


def half_of(at, own, q_pieces, g_pieces, pa, pb, vp, kt, ma, mb, sent, got):
    count = len(q_pieces)
    piece, cols = q_pieces[0].shape
    tokens = vp.shape[0]
    side = ma.shape[2]
    bit = lambda i, a: (i + 1 + a[CORE]) % 2
    pair = lambda i, a: 2 * (a[Y] if own else 1 - a[Y]) + bit(i, a)
    extra_spec = pl.BlockSpec((piece + EXTRA, PAIR), lambda i, a: (0, pair(i, a)))
    row_spec = pl.BlockSpec((piece, PAIR), lambda i, a: (0, pair(i, a)))
    p_spec = pl.BlockSpec((2, tokens, side), lambda i, a: (pair(i, a), 0, 0))
    stat_spec = lambda n: pl.BlockSpec((1, 2, n), lambda i, a: (pair(i, a), 0, 0))
    block = tokens
    return pl.pallas_call(
        functools.partial(half_kernel, count),
        grid_spec=pltpu.PrefetchScalarGridSpec(
            num_scalar_prefetch=1,
            grid=(2,),
            in_specs=[row_spec] * count
            + [extra_spec] * count
            + [
                p_spec,
                p_spec,
                pl.BlockSpec((tokens, PAIR), lambda i, a: (0, pair(i, a))),
                pl.BlockSpec((PAIR, tokens), lambda i, a: (pair(i, a), 0)),
                stat_spec(side),
                stat_spec(side),
                stat_spec(2 * side),
                stat_spec(2 * side),
            ],
            out_specs=[pl.BlockSpec((block, PAIR), lambda i, a: (0, bit(i, a)))] * 2
            + [pl.BlockSpec((PAIR, 2 * side), lambda i, a: (0, 0))] * 2,
        ),
        out_shape=[like((block, 2 * PAIR))] * 2 + [like((PAIR, 2 * side))] * 2,
        compiler_params=params(),
        cost_estimate=cost(16 * side * tokens * 2 * PAIR * 2, 8 * side * tokens * 2, 0),
    )(at, *q_pieces, *g_pieces, pa, pb, vp, kt, ma, mb, sent, got)


def columns_kernel(count, high, at_ref, *refs):
    x_refs = refs[:count]
    keep_ref, core_ref, y_ref = refs[count : count + 3]
    w_refs, back_ref, send_ref, all_ref = refs[count + 3 : -3], refs[-3], refs[-2], refs[-1]
    side = keep_ref.shape[1] // 2
    far = jnp.concatenate([y_ref[:, side:], y_ref[:, :side]], axis=1)
    dq = (keep_ref[...].astype(F32) + core_ref[...].astype(F32) + far.astype(F32)).astype(BF)
    quarter = side // 2
    back_ref[...] = jnp.concatenate([dq[:, span(0, quarter)], dq[:, span(2, quarter)]], axis=1)
    send_ref[...] = jnp.concatenate([dq[:, span(1, quarter)], dq[:, span(3, quarter)]], axis=1)
    x = jnp.concatenate([r[...] for r in x_refs], axis=0)
    all_ref[...] = dot(dq, x, 1, 0)
    width = x.shape[1] // high
    for ref, order in zip(w_refs, ORDERS, strict=True):
        for n, k in enumerate(order):
            start = pl.multiple_of((at_ref[Z] ^ k) * width, PAIR)
            ref[span(n, ref.shape[0] // 2)] = all_ref[:, pl.ds(start, width)].astype(BF)


def columns_of(at, high, x_pieces, keep, core, y):
    count = len(x_pieces)
    piece, cols = x_pieces[0].shape
    width, rows = keep.shape
    return pl.pallas_call(
        functools.partial(columns_kernel, count, high),
        in_specs=[SMEM] + [VMEM] * (count + 3),
        out_specs=[VMEM] * 4,
        out_shape=[like((2 * width, cols // high))] * 2 + [like((width, rows // 2))] * 2,
        scratch_shapes=[pltpu.VMEM((width, cols), F32)],
        compiler_params=params(),
        cost_estimate=cost(2 * rows * cols * width, 2 * rows * cols),
    )(at, *x_pieces, keep, core, y)


def input_kernel(at_ref, back_ref, x_ref, y_ref, core_ref, wq_ref, out_ref, dq_ref):
    me, x = at_ref[SEQ], at_ref[X]
    size = back_ref.shape[0]

    def put(group, odd, block):
        row = pl.multiple_of((2 * group + (x ^ odd)) * size, PAIR)
        dq_ref[pl.ds(row, size), :] = block

    put(me, 0, back_ref[:, :size])
    put(me, 1, x_ref[:, :size])
    for odd in range(2):
        put(me ^ 2, odd, y_ref[span(odd, size), :size])
        put(me ^ 1, odd, core_ref[span(odd, size), :])
        put(me ^ 3, odd, core_ref[span(2 + odd, size), :])
    out_ref[...] = dot(dq_ref[...], wq_ref[...], 0, 1).astype(BF)


def input_of(at, back, x, y, core, wq):
    size, cols = back.shape[0], wq.shape[1]
    return pl.pallas_call(
        input_kernel,
        in_specs=[SMEM] + [VMEM] * 5,
        out_specs=VMEM,
        out_shape=like((size, cols)),
        scratch_shapes=[pltpu.VMEM((cols, size), BF)],
        compiler_params=params(),
        cost_estimate=cost(2 * size * cols * cols, 2 * cols * cols),
    )(at, back, x, y, core, wq)


def weight_near_kernel(own_ref, got_ref, keep_ref, send_ref):
    rows = keep_ref.shape[0]
    keep_ref[...] = own_ref[:rows].astype(F32) + got_ref[:rows].astype(F32)
    send_ref[...] = (own_ref[rows:].astype(F32) + got_ref[rows:].astype(F32)).astype(BF)


def weight_near(own, got):
    rows, cols = own.shape[0] // 2, own.shape[1]
    return pl.pallas_call(
        weight_near_kernel,
        in_specs=[VMEM] * 2,
        out_specs=[VMEM] * 2,
        out_shape=[like((rows, cols), F32), like((rows, cols))],
        compiler_params=params(),
        cost_estimate=cost(),
    )(own, got)


def weight_sum_kernel(at_ref, own_ref, got_ref, keep_ref, send_ref):
    total = own_ref[...] + got_ref[...].astype(F32)
    size = keep_ref.shape[1]
    a, b = total[:, :size], total[:, size:]
    low = at_ref[X] == 0
    keep_ref[...] = jnp.where(low, a, b)
    send_ref[...] = jnp.where(low, b, a).astype(BF)


def weight_sum(at, own, got):
    rows, cols = own.shape
    return pl.pallas_call(
        weight_sum_kernel,
        in_specs=[SMEM, VMEM, VMEM],
        out_specs=[VMEM] * 2,
        out_shape=[like((rows, cols // 2), F32), like((rows, cols // 2))],
        compiler_params=params(),
        cost_estimate=cost(),
    )(at, own, got)


def weight_out_kernel(at_ref, keep_ref, got_ref, out_ref):
    size = keep_ref.shape[0]
    a, b = keep_ref[...].T, got_ref[...].astype(F32).T
    low = at_ref[X] == 0
    out_ref[:, :size] = jnp.where(low, a, b)
    out_ref[:, size:] = jnp.where(low, b, a)


def weight_out(at, keep, got):
    size, rows = keep.shape
    return pl.pallas_call(
        weight_out_kernel,
        in_specs=[SMEM, VMEM, VMEM],
        out_specs=VMEM,
        out_shape=like((rows, 2 * size), F32),
        compiler_params=params(),
        cost_estimate=cost(1000, 300000),
    )(at, keep, got)


def tokens_kernel(at_ref, *refs):
    y, x, z = at_ref[Y], at_ref[X], at_ref[Z]
    key_ref, val_ref = refs[-2:]
    size = refs[0].shape[0] // 2
    for half in range(2):
        group = 2 * (y ^ (1 - half))
        keep, near, got = refs[3 * half : 3 * half + 3]
        for i, k in enumerate(ORDERS[0] + ORDERS[1]):
            b = z ^ k
            row = pl.multiple_of((b % 2) * size, 16)
            own = (keep if i < 2 else near)[span(i % 2, size)]
            for out_ref, which in ((key_ref, 0), (val_ref, 1)):

                @pl.when(b // 2 == which)
                def _():
                    for c in range(2):
                        for odd, block in ((0, own[:, span(c)]), (1, got[span(i, size), span(c)])):
                            col = pl.multiple_of((2 * (group + c) + (x ^ odd)) * PAIR, PAIR)
                            out_ref[pl.ds(row, size), pl.ds(col, PAIR)] = block


def tokens_out(at, tokens, cols, parts):
    return pl.pallas_call(
        tokens_kernel,
        in_specs=[SMEM] + [VMEM] * len(parts),
        out_specs=[VMEM] * 2,
        out_shape=[like((tokens, cols))] * 2,
        compiler_params=params(),
        cost_estimate=cost(),
    )(at, *parts)


def local_split(n_dp, n_seq, qx, queries, keys, values, attn_out, grad_out, wq):
    high = n_dp // 2
    dp, me = lax.axis_index("dp").astype(jnp.int32), lax.axis_index("seq").astype(jnp.int32)
    at = jnp.stack([dp % 2, me // 2, dp // 2, me % 2, me])
    over_x = lambda t: swap(t, "dp", n_dp, 1)
    over_y = lambda t: swap(t, "seq", n_seq, 2)
    over_core = lambda t: swap(t, "seq", n_seq, 1)
    over_z = lambda t, k: swap(t, "dp", n_dp, 2 * k)
    after = lambda t, *deps: lax.optimization_barrier((t, *deps))[0]

    def rows_of(own, from_x):
        from_y, from_xy = over_y(own), over_y(from_x)
        a = [own, over_core(own), from_x, over_core(from_x)]
        return a, from_y, from_xy

    def far_rows(from_y, from_xy):
        return [from_y, over_core(from_y), from_xy, over_core(from_xy)]

    qk, qs, gk, gs = pack(at, queries, grad_out, attn_out)
    kp, vp, kt = pack_tokens(at, keys, values)
    q_from_x = after(over_x(qs), kp)
    qa, q_y, q_xy = rows_of(qk, q_from_x)
    g_from_x = over_x(after(gs, q_from_x))
    ga, g_y, g_xy = rows_of(after(gk, q_from_x), g_from_x)
    gb = far_rows(g_y, g_xy)
    pa, ma, la = side_of(qa, kp)
    qb = far_rows(q_y, after(q_xy, la))
    pb, mb, lb, sent = side_of(qb, kp, la)
    send = merge(la, lb, over_core(sent))
    got = over_y(send)
    x_from_x = over_x(after(qx, la))
    xa, x_y, x_xy = rows_of(after(qx, got), after(x_from_x, got))

    def half(own, pa):
        return half_of(at, own, qa + qb, ga + gb, pa, pb, vp, kt, ma, mb, send, got)

    def sum_near(keep, send):
        return add(keep, over_z(send, 1))

    def sum_far(near):
        return add_turned(near, over_z(near, 2))

    def spread(total):
        near = over_z(total, 1)
        return [total, near, over_x(stack([total, near]))]

    kv_keep, kv_send, dq_send, dq_keep = half(False, pa)
    first = sum_near(kv_keep, kv_send)
    far = add(dq_keep, over_core(dq_send))
    kv_keep, kv_send, dq_send, dq_keep = half(True, after(pa, far, x_y, x_from_x))
    far = over_y(far)
    second = sum_near(kv_keep, kv_send)
    x_y, x_xy = after(x_y, dq_keep), after(x_xy, dq_keep)
    w_keep, w_send, back, back_s = columns_of(
        at, high, xa + far_rows(x_y, x_xy), dq_keep, over_core(dq_send), far
    )
    first, second = sum_far(first), sum_far(second)
    w_keep, w_send = weight_near(w_keep, over_z(w_send, 1))
    w_keep, w_send = weight_sum(at, w_keep, over_z(w_send, 2))
    grad_weight = weight_out(at, w_keep, over_x(w_send))

    from_x = over_x(back_s)
    size = back.shape[0]
    part = lambda i, n: (slice(None), slice(i * size, (i + n) * size))
    from_y = over_y(stack([back, from_x], [part(2, 2)] * 2))
    from_core = over_core(stack([back, from_x, from_y], [part(1, 1)] * 3))
    grad_input = input_of(at, back, from_x, from_y, from_core, wq)
    grad_keys, grad_values = tokens_out(at, *keys.shape, spread(first) + spread(second))
    return (grad_input, grad_keys, grad_values, grad_weight)


def solution(mesh):
    n_dp, n_seq = mesh.shape["dp"], mesh.shape["seq"]

    def run(qx, queries, keys, *rest):
        pairs = queries.shape[1] == 2 * n_seq * PAIR and queries.shape[0] == n_dp * n_seq * PAIR
        split = n_seq == 4 and n_dp == 8 and pairs and (2 * keys.shape[0] // n_seq) % (16 * n_dp // 2) == 0
        return shard(local_split if split else local)(qx, queries, keys, *rest)

    def shard(f):
        return jax.shard_map(
            functools.partial(f, n_dp, n_seq),
            mesh=mesh,
            in_specs=(
                P(("dp", "seq"), None),
                P(("dp", "seq"), None),
                P("seq", None),
                P("seq", None),
                P(("dp", "seq"), None),
                P(("dp", "seq"), None),
                P(),
            ),
            out_specs=(P(("dp", "seq"), None), P("seq", None), P("seq", None), P("dp", "seq")),
            check_vma=False,
        )

    return run
```

```python
import functools
import math

import jax
import jax.numpy as jnp
from jax import lax
from jax.experimental import pallas as pl
from jax.experimental.pallas import tpu as pltpu
from jax.sharding import PartitionSpec as P

HD = 64
PAIR = 2 * HD
SCALE = 1.0 / math.sqrt(HD)
BF = jnp.bfloat16
F32 = jnp.float32
VMEM_LIMIT = 56 * 1024 * 1024


def dot(a, b, ca, cb):
    return lax.dot_general(a, b, (((ca,), (cb,)), ((), ())), preferred_element_type=F32)


def own_lanes(x, head):
    lane = lax.broadcasted_iota(jnp.int32, x.shape, 1)
    mine = lane < HD if head == 0 else lane >= HD
    return jnp.where(mine, x, jnp.zeros_like(x))


def delta_kernel(grad_ref, out_ref, delta_ref):
    prod = grad_ref[...].astype(F32) * out_ref[...].astype(F32)
    cols = prod.T
    heads = cols.shape[0] // HD
    for head in range(heads):
        part = jnp.sum(cols[head * HD : (head + 1) * HD], axis=0, keepdims=True)
        delta_ref[head // 2, head % 2] = part[0]


def delta_of(grad_out, attn_out):
    rows, cols = grad_out.shape
    return pl.pallas_call(
        delta_kernel,
        out_shape=jax.ShapeDtypeStruct((cols // PAIR, 2, rows), F32),
        compiler_params=pltpu.CompilerParams(vmem_limit_bytes=VMEM_LIMIT),
        cost_estimate=pl.CostEstimate(flops=4 * rows * cols, bytes_accessed=4 * rows * cols, transcendentals=0),
    )(grad_out, attn_out)


def probs_kernel(count, *refs):
    q_refs, k_ref = refs[:count], refs[count]
    p_ref, m_ref, lse_ref = refs[count + 1 :]
    q = jnp.concatenate([r[...] for r in q_refs], axis=0) * jnp.asarray(SCALE, BF)
    k = k_ref[...]
    for head in range(2):
        s = dot(own_lanes(k, head), q, 1, 1)
        top = jnp.max(s, axis=0, keepdims=True)
        p = jnp.exp(s - top)
        total = jnp.sum(p, axis=0, keepdims=True)
        p_ref[head] = p.astype(BF)
        m_ref[0, head] = top[0]
        lse_ref[0, head] = (top + jnp.log(total))[0]


def probs_of(q_pieces, keys):
    count = len(q_pieces)
    piece, cols = q_pieces[0].shape
    tokens = keys.shape[0]
    rows = piece * count
    pairs = cols // PAIR
    return pl.pallas_call(
        functools.partial(probs_kernel, count),
        grid=(pairs,),
        in_specs=[pl.BlockSpec((piece, PAIR), lambda i: (0, i))] * count
        + [pl.BlockSpec((tokens, PAIR), lambda i: (0, i))],
        out_specs=[
            pl.BlockSpec((2, tokens, rows), lambda i: (i, 0, 0)),
            pl.BlockSpec((1, 2, rows), lambda i: (i, 0, 0)),
            pl.BlockSpec((1, 2, rows), lambda i: (i, 0, 0)),
        ],
        out_shape=[
            jax.ShapeDtypeStruct((2 * pairs, tokens, rows), BF),
            jax.ShapeDtypeStruct((pairs, 2, rows), F32),
            jax.ShapeDtypeStruct((pairs, 2, rows), F32),
        ],
        compiler_params=pltpu.CompilerParams(vmem_limit_bytes=VMEM_LIMIT),
        cost_estimate=pl.CostEstimate(
            flops=2 * rows * tokens * cols,
            bytes_accessed=2 * rows * tokens * 2 * pairs,
            transcendentals=rows * tokens * 2 * pairs,
        ),
    )(*q_pieces, keys)


def grads_kernel(count, half_ref, *refs):
    q_refs, g_refs = refs[:count], refs[count : 2 * count]
    pa_ref, pb_ref, v_ref, kt_ref, w_ref, delta_ref, dkv_ref, dqt_ref = refs[2 * count :]
    rows = w_ref.shape[2]
    side = rows // 2
    w = w_ref[0]
    delta = delta_ref[0]
    v = v_ref[...]
    first = lax.broadcasted_iota(jnp.int32, (PAIR, rows), 0) < HD
    wide = jnp.where(first, w[0:1], w[1:2]).T
    q = jnp.concatenate([r[...] for r in q_refs], axis=0)
    g = jnp.concatenate([r[...] for r in g_refs], axis=0)
    qw = (q.astype(F32) * (wide * SCALE)).astype(BF)
    gw = (g.astype(F32) * wide).astype(BF)
    dk = jnp.zeros((v.shape[0], PAIR), F32)
    dv = jnp.zeros((v.shape[0], PAIR), F32)
    for half, p_ref in ((0, pa_ref), (1, pb_ref)):
        at = slice(half * side, (half + 1) * side)
        for head in range(2):
            p = p_ref[head]
            dp = dot(v, own_lanes(g[at], head), 1, 1)
            t = (p.astype(F32) * (dp - delta[head : head + 1, at])).astype(BF)
            dv = dv + dot(p, own_lanes(gw[at], head), 1, 0)
            dk = dk + dot(t, own_lanes(qw[at], head), 1, 0)
            dq = dot(kt_ref[head * HD : (head + 1) * HD], t, 1, 0)
            dq = dq * (w[head : head + 1, at] * SCALE)
            dqt_ref[head * HD : (head + 1) * HD, at] = dq.astype(BF)
    dkv_ref[0] = dk.astype(BF)
    dkv_ref[1] = dv.astype(BF)


def grads_of(half, q_pieces, g_pieces, pa, pb, values, keys_t, w, delta):
    count = len(q_pieces)
    piece, cols = q_pieces[0].shape
    tokens = values.shape[0]
    rows = piece * count
    steps = cols // PAIR // 2
    at = lambda i, h: h[0] * steps + i
    row_spec = pl.BlockSpec((piece, PAIR), lambda i, h: (0, at(i, h)))
    p_spec = pl.BlockSpec((2, tokens, rows // 2), lambda i, h: (at(i, h), 0, 0))
    stat_spec = pl.BlockSpec((1, 2, rows), lambda i, h: (at(i, h), 0, 0))
    return pl.pallas_call(
        functools.partial(grads_kernel, count),
        grid_spec=pltpu.PrefetchScalarGridSpec(
            num_scalar_prefetch=1,
            grid=(steps,),
            in_specs=[row_spec] * (2 * count)
            + [
                p_spec,
                p_spec,
                pl.BlockSpec((tokens, PAIR), lambda i, h: (0, at(i, h))),
                pl.BlockSpec((PAIR, tokens), lambda i, h: (at(i, h), 0)),
                stat_spec,
                stat_spec,
            ],
            out_specs=[
                pl.BlockSpec((2, tokens, PAIR), lambda i, h: (0, 0, i)),
                pl.BlockSpec((PAIR, rows), lambda i, h: (i, 0)),
            ],
        ),
        out_shape=[
            jax.ShapeDtypeStruct((2, tokens, cols // 2), BF),
            jax.ShapeDtypeStruct((cols // 2, rows), BF),
        ],
        compiler_params=pltpu.CompilerParams(vmem_limit_bytes=VMEM_LIMIT),
        cost_estimate=pl.CostEstimate(
            flops=4 * rows * tokens * cols,
            bytes_accessed=2 * rows * tokens * 2 * steps,
            transcendentals=0,
        ),
    )(half, *q_pieces, *g_pieces, pa, pb, values, keys_t, w, delta)


def weight_kernel(count, *refs):
    x = jnp.concatenate([r[...] for r in refs[:count]], axis=0)
    refs[count + 1][...] = dot(x, refs[count][...], 0, 1).astype(BF)


def weight_of(x_pieces, dq_cols):
    count = len(x_pieces)
    piece, cols = x_pieces[0].shape
    width, rows = dq_cols.shape
    step = min(cols, 256)
    return pl.pallas_call(
        functools.partial(weight_kernel, count),
        grid=(cols // step,),
        in_specs=[pl.BlockSpec((piece, step), lambda i: (0, i))] * count
        + [pl.BlockSpec((width, rows), lambda i: (0, 0))],
        out_specs=pl.BlockSpec((step, width), lambda i: (i, 0)),
        out_shape=jax.ShapeDtypeStruct((cols, width), BF),
        compiler_params=pltpu.CompilerParams(vmem_limit_bytes=VMEM_LIMIT),
        cost_estimate=pl.CostEstimate(
            flops=2 * rows * cols * width, bytes_accessed=2 * rows * cols, transcendentals=0
        ),
    )(*x_pieces, dq_cols)


def swap(x, axis, size, mask):
    return lax.ppermute(x, axis, [(i, i ^ mask) for i in range(size)])


def gather_pieces(x, axis, size):
    pieces = {0: x}
    bit = size // 2
    while bit:
        for k in list(pieces):
            pieces[k | bit] = swap(pieces[k], axis, size, bit)
        bit //= 2
    return [pieces[k] for k in range(size)]


def flip_pieces(x, count, bit):
    lead, piece = x.shape[:-1], x.shape[-1] // count
    y = x.reshape(lead + (count // (2 * bit), 2, bit * piece))
    return jnp.flip(y, axis=-2).reshape(x.shape)


def pick(blocks, index):
    return lax.dynamic_index_in_dim(blocks, index, 0, keepdims=False)


def exchange_sum(x, axis, size, stride, group, wide=False):
    me = (lax.axis_index(axis) // stride) % group
    total = pick(x, me).astype(F32)
    for k in range(1, group):
        total = total + swap(pick(x, me ^ k), axis, size, k * stride).astype(F32)
    return total if wide else total.astype(BF)


def exchange_gather(x, axis, size, stride, group):
    me = (lax.axis_index(axis) // stride) % group
    out = jnp.zeros((group,) + x.shape, x.dtype)
    for k in range(group):
        got = x if k == 0 else swap(x, axis, size, k * stride)
        out = lax.dynamic_update_index_in_dim(out, got, me ^ k, 0)
    return out


def local(n_dp, n_seq, qx, queries, keys, values, attn_out, grad_out, wq):
    low = max(n_dp // 4, 1)
    high = n_dp // low
    cols = queries.shape[1]
    me = lax.axis_index("seq")
    top = n_seq // 2
    q_pieces = gather_pieces(queries, "seq", n_seq)
    g_pieces = gather_pieces(grad_out, "seq", n_seq)
    x_pieces = gather_pieces(qx, "seq", n_seq)
    keys_t = keys.T
    delta = delta_of(grad_out, attn_out)
    pa, ma, la = probs_of(q_pieces[:top], keys)
    pb, mb, lb = probs_of(q_pieces[top:], keys)
    rows = 2 * la.shape[2]
    peak = jnp.concatenate([ma, mb], axis=2)
    lse = jnp.concatenate([la, lb], axis=2)
    bit = 1
    while bit < n_seq:
        got = swap(jnp.concatenate([lse, delta], axis=2), "seq", n_seq, bit)
        lse = jnp.logaddexp(lse, flip_pieces(got[:, :, :rows], n_seq, bit))
        delta = jnp.concatenate([delta, got[:, :, rows:]], axis=2)
        bit *= 2
    w = jnp.exp(peak - lse)

    mine = (me // top).astype(jnp.int32)
    shards, dqs = [], []
    for half in (1 - mine, mine):
        dkv, dqt = grads_of(half.reshape(1), q_pieces, g_pieces, pa, pb, values, keys_t, w, delta)
        tokens = dkv.shape[1]
        part = dkv.reshape(low, 2 * tokens // low, cols // 2)
        part = exchange_sum(part, "dp", n_dp, 1, low)
        part = part.reshape(high, part.shape[0] // high, cols // 2)
        shards.append(exchange_sum(part, "dp", n_dp, low, high))
        dqs.append(dqt)

    def narrow(dqt):
        blocks = dqt.reshape(top, dqt.shape[0] // top, rows)
        bit = 1
        base = me % top
        while bit < top:
            view = blocks.reshape((blocks.shape[0] // 2, 2) + blocks.shape[1:])
            own = (base // bit) % 2
            keep = lax.dynamic_index_in_dim(view, own, 1, keepdims=False)
            send = lax.dynamic_index_in_dim(view, 1 - own, 1, keepdims=False)
            got = swap(send, "seq", n_seq, bit)
            got = flip_pieces(got, n_seq, bit)
            blocks = (keep.astype(F32) + got.astype(F32)).astype(BF)
            bit *= 2
        return blocks[0]

    other, own = narrow(dqs[0]), narrow(dqs[1])
    got = flip_pieces(swap(other, "seq", n_seq, top), n_seq, top)
    dq_cols = (own.astype(F32) + got.astype(F32)).astype(BF)

    weight = weight_of(x_pieces, dq_cols)
    weight = weight.reshape(high, low, weight.shape[0] // n_dp, weight.shape[1])
    weight = exchange_sum(weight, "dp", n_dp, low, high)
    grad_weight = exchange_sum(weight, "dp", n_dp, 1, low, wide=True)

    piece = rows // n_seq
    width = cols // n_seq
    dq_rows = jnp.zeros((n_seq, width, piece), BF)
    for k in range(n_seq):
        block = dq_cols[:, k * piece : (k + 1) * piece]
        block = block if k == 0 else swap(block, "seq", n_seq, k)
        dq_rows = lax.dynamic_update_index_in_dim(dq_rows, block, me ^ k, 0)
    grad_input = dot(dq_rows.reshape(cols, piece), wq, 0, 1).astype(BF)

    halves = []
    for shard in shards:
        part = exchange_gather(shard, "dp", n_dp, low, high)
        part = part.reshape((-1,) + part.shape[2:])
        part = exchange_gather(part, "dp", n_dp, 1, low)
        halves.append(part.reshape(2, -1, cols // 2))
    other, own = halves
    left = jnp.where(mine == 0, own, other)
    right = jnp.where(mine == 0, other, own)
    both = jnp.concatenate([left, right], axis=2)
    return (grad_input, both[0], both[1], grad_weight)


def params(limit=24):
    return pltpu.CompilerParams(vmem_limit_bytes=limit * 1024 * 1024)


def cost(flops=0, nbytes=0, exps=0):
    return pl.CostEstimate(flops=1, bytes_accessed=1, transcendentals=0)


def like(shape, dtype=BF):
    return jax.ShapeDtypeStruct(shape, dtype)


SMEM = pl.BlockSpec(memory_space=pltpu.SMEM)
VMEM = pl.BlockSpec(memory_space=pltpu.VMEM)


def span(i, size=PAIR):
    return slice(i * size, (i + 1) * size)


def flip_core(x):
    n = x.shape[-1] // PAIR
    return jnp.concatenate([x[..., span(i ^ 1)] for i in range(n)], axis=-1)


def whole(shape):
    return pl.BlockSpec(shape, lambda i: (0,) * len(shape))


X, Y, Z, CORE, SEQ = range(5)
EXTRA = 16
ORDERS = ((0, 2), (1, 3))


def split_parts(d):
    high = d.astype(BF).astype(F32)
    mid = (d - high).astype(BF).astype(F32)
    return high, mid, d - high - mid


def pack_kernel(q_ref, g_ref, o_ref, keep_ref, send_ref):
    low = lax.axis_index("dp") % 2 == 0
    rows = q_ref.shape[0]
    pairs = keep_ref.shape[1] // PAIR
    for p in range(pairs):
        scale = jnp.asarray(SCALE, BF)
        a, b = q_ref[:, span(2 * p)] * scale, q_ref[:, span(2 * p + 1)] * scale
        keep_ref[:rows, span(p)] = jnp.where(low, a, b)
        send_ref[:rows, span(p)] = jnp.where(low, b, a)
        a, b = g_ref[:, span(2 * p)], g_ref[:, span(2 * p + 1)]
        keep_ref[rows : 2 * rows, span(p)] = jnp.where(low, a, b)
        send_ref[rows : 2 * rows, span(p)] = jnp.where(low, b, a)
    cols = (g_ref[...].astype(F32) * o_ref[...].astype(F32)).T
    for p in range(pairs):
        both = []
        for h in range(4):
            both.append(split_parts(jnp.sum(cols[span(4 * p + h, HD)], axis=0, keepdims=True)))
        pad = [jnp.zeros((EXTRA - 6, rows), F32)]
        a = jnp.concatenate([both[h][n] for n in range(3) for h in (0, 1)] + pad, axis=0).astype(BF)
        b = jnp.concatenate([both[h][n] for n in range(3) for h in (2, 3)] + pad, axis=0).astype(BF)
        keep_ref[2 * rows :, span(p)] = jnp.where(low, a, b)
        send_ref[2 * rows :, span(p)] = jnp.where(low, b, a)


def pack(queries, grad_out, attn_out):
    rows, cols = queries.shape
    steps = 2
    block = pl.BlockSpec((rows, cols // steps), lambda i: (0, i))
    total = 2 * rows + EXTRA
    half = pl.BlockSpec((total, cols // 2 // steps), lambda i: (0, i))
    return pl.pallas_call(
        pack_kernel,
        grid=(steps,),
        in_specs=[block] * 3,
        out_specs=[half] * 2,
        out_shape=[like((total, cols // 2))] * 2,
        compiler_params=params(60),
        cost_estimate=cost(),
    )(queries, grad_out, attn_out)


def pack_tokens_kernel(at_ref, k_ref, v_ref, kp_ref, vp_ref, kt_ref):
    low = at_ref[X] == 0
    for p in range(kp_ref.shape[1] // PAIR):
        k = jnp.where(low, k_ref[:, span(2 * p)], k_ref[:, span(2 * p + 1)])
        kp_ref[:, span(p)] = k
        kt_ref[span(p)] = k.T
        vp_ref[:, span(p)] = jnp.where(low, v_ref[:, span(2 * p)], v_ref[:, span(2 * p + 1)])


def pack_tokens(at, keys, values):
    tokens, cols = keys.shape
    steps = 2
    block = pl.BlockSpec((tokens, cols // steps), lambda i: (0, i))
    half = pl.BlockSpec((tokens, cols // 2 // steps), lambda i: (0, i))
    return pl.pallas_call(
        pack_tokens_kernel,
        grid=(steps,),
        in_specs=[SMEM, block, block],
        out_specs=[half, half, pl.BlockSpec((cols // 2 // steps, tokens), lambda i: (i, 0))],
        out_shape=[like((tokens, cols // 2))] * 2 + [like((cols // 2, tokens))],
        compiler_params=params(),
        cost_estimate=cost(),
    )(at, keys, values)


def add_kernel(*refs):
    total = refs[0][...].astype(F32)
    for r in refs[1:-1]:
        total = total + r[...].astype(F32)
    refs[-1][...] = total.astype(BF)


def add(*parts):
    return pl.pallas_call(
        add_kernel,
        in_specs=[VMEM] * len(parts),
        out_specs=VMEM,
        out_shape=like(parts[0].shape),
        compiler_params=params(),
        cost_estimate=cost(),
    )(*parts)


def add_turned_kernel(own_ref, got_ref, out_ref):
    rows = own_ref.shape[0] // 2
    for n in range(2):
        total = own_ref[span(n, rows)].astype(F32) + got_ref[span(1 - n, rows)].astype(F32)
        out_ref[span(n, rows)] = total.astype(BF)


def add_turned(own, got):
    return pl.pallas_call(
        add_turned_kernel,
        in_specs=[VMEM] * 2,
        out_specs=VMEM,
        out_shape=like(own.shape),
        compiler_params=params(),
        cost_estimate=cost(),
    )(own, got)


def stack_kernel(cuts, *refs):
    out_ref, row = refs[-1], 0
    for r, cut in zip(refs[:-1], cuts, strict=True):
        block = r[...] if cut is None else r[cut]
        out_ref[row : row + block.shape[0], :] = block
        row += block.shape[0]


def stack(parts, cuts=None):
    cuts = cuts or [None] * len(parts)
    shapes = [jax.eval_shape(lambda t, c=c: t if c is None else t[c], t).shape for t, c in zip(parts, cuts, strict=True)]
    rows, width = sum(t[0] for t in shapes), shapes[0][1]
    return pl.pallas_call(
        functools.partial(stack_kernel, cuts),
        in_specs=[VMEM] * len(parts),
        out_specs=VMEM,
        out_shape=like((rows, width)),
        compiler_params=params(),
        cost_estimate=cost(),
    )(*parts)


def side_kernel(count, step, last, *refs):
    q_refs, k_ref = refs[:count], refs[count]
    if last:
        la_ref, p_ref, m_ref, lse_ref, send_ref = refs[count + 1 :]
    else:
        p_ref, m_ref, lse_ref = refs[count + 1 :]
    for j in range(step):
        q = jnp.concatenate([r[:, span(j)] for r in q_refs], axis=0)
        k = k_ref[:, span(j)]
        for head in range(2):
            s = dot(own_lanes(k, head), q, 1, 1)
            top = jnp.max(s, axis=0, keepdims=True)
            p = jnp.exp(s - top)
            total = jnp.sum(p, axis=0, keepdims=True)
            p_ref[2 * j + head] = p.astype(BF)
            m_ref[j, head] = top[0]
            lse_ref[j, head] = (top + jnp.log(total))[0]
    if last:
        send_ref[...] = jnp.concatenate([flip_core(la_ref[...]), flip_core(lse_ref[...])], axis=-1)


def side_of(pieces, keys, extra=None, step=2):
    count = len(pieces)
    cols = pieces[0].shape[1]
    tokens = keys.shape[0]
    piece = (pieces[0].shape[0] - EXTRA) // 2
    rows, pairs = piece * count, cols // PAIR
    stat_spec = lambda n: pl.BlockSpec((step, 2, n), lambda i: (i, 0, 0))
    in_specs = [pl.BlockSpec((piece, step * PAIR), lambda i: (0, i))] * count
    in_specs += [pl.BlockSpec((tokens, step * PAIR), lambda i: (0, i))]
    out_specs = [pl.BlockSpec((2 * step, tokens, rows), lambda i: (i, 0, 0)), stat_spec(rows), stat_spec(rows)]
    out_shape = [like((2 * pairs, tokens, rows)), like((pairs, 2, rows), F32), like((pairs, 2, rows), F32)]
    args = [*pieces, keys]
    if extra is not None:
        in_specs += [stat_spec(rows)]
        out_specs += [stat_spec(2 * rows)]
        out_shape += [like((pairs, 2, 2 * rows), F32)]
        args += [extra]
    return pl.pallas_call(
        functools.partial(side_kernel, count, step, extra is not None),
        grid=(pairs // step,),
        in_specs=in_specs,
        out_specs=out_specs,
        out_shape=out_shape,
        compiler_params=params(),
        cost_estimate=cost(2 * rows * tokens * cols, 4 * rows * tokens * pairs, 2 * rows * tokens * pairs),
    )(*args)


def log_add(a, b):
    top = jnp.maximum(a, b)
    return top + jnp.log(jnp.exp(a - top) + jnp.exp(b - top))


def merge_kernel(la_ref, lb_ref, got_ref, send_ref):
    side = la_ref.shape[2]
    send_ref[:, :, :side] = log_add(lb_ref[...], got_ref[:, :, side:])
    send_ref[:, :, side:] = log_add(la_ref[...], got_ref[:, :, :side])


def merge(la, lb, got):
    pairs, two, side = la.shape
    return pl.pallas_call(
        merge_kernel,
        in_specs=[VMEM] * 3,
        out_specs=VMEM,
        out_shape=like((pairs, two, 2 * side), F32),
        compiler_params=params(),
        cost_estimate=cost(1000, 100000),
    )(la, lb, got)


def half_kernel(count, at_ref, *refs):
    row_refs = refs[:count]
    piece = (row_refs[0].shape[0] - EXTRA) // 2
    pa_ref, pb_ref, v_ref, kt_ref, ma_ref, mb_ref, sent_ref, got_ref = refs[count : count + 8]
    kv_refs, dqs_ref, dqk_ref = refs[count + 8 : -2], refs[-2], refs[-1]
    side = ma_ref.shape[2]
    z = at_ref[Z]
    v = v_ref[...]
    tokens = v.shape[0]
    dk = jnp.zeros((tokens, PAIR), F32)
    dv = jnp.zeros((tokens, PAIR), F32)
    first = lax.broadcasted_iota(jnp.int32, (PAIR, side), 0) < HD
    halves = []
    for b, p_ref, m_ref in ((0, pa_ref, ma_ref), (1, pb_ref, mb_ref)):
        lse = log_add(sent_ref[0, :, span(1 - b, side)], got_ref[0, :, span(b, side)])
        w = jnp.exp(m_ref[0] - lse)
        wide = jnp.where(first, w[0:1], w[1:2]).T
        at = slice(b * count // 2, (b + 1) * count // 2)
        q = jnp.concatenate([r[:piece] for r in row_refs[at]], axis=0)
        g = jnp.concatenate([r[piece : 2 * piece] for r in row_refs[at]], axis=0)
        parts = [r[2 * piece :].astype(F32) for r in row_refs[at]]
        delta = jnp.concatenate([d[0:2] + d[2:4] + d[4:6] for d in parts], axis=1)
        qw = (q.astype(F32) * wide).astype(BF)
        gw = (g.astype(F32) * wide).astype(BF)
        parts = []
        for head in range(2):
            p = p_ref[head]
            dp = dot(v, own_lanes(g, head), 1, 1)
            t = (p.astype(F32) * (dp - delta[head : head + 1])).astype(BF)
            dv = dv + dot(p, own_lanes(gw, head), 1, 0)
            dk = dk + dot(t, own_lanes(qw, head), 1, 0)
            dq = dot(kt_ref[span(head, HD)], t, 1, 0)
            parts.append((dq * (w[head : head + 1] * SCALE)).astype(BF))
        halves.append(jnp.concatenate(parts, axis=0))
    dq = jnp.concatenate(halves, axis=1)

    @pl.when(pl.program_id(0) == 0)
    def _():
        dqs_ref[...] = flip_core(dq)

    @pl.when(pl.program_id(0) == 1)
    def _():
        dqk_ref[...] = dq

    both = jnp.concatenate([dk.astype(BF), dv.astype(BF)], axis=0)
    size = both.shape[0] // 4
    for ref, order in zip(kv_refs, ORDERS, strict=True):
        for n, k in enumerate(order):
            out = both[:size]
            for j in range(1, 4):
                out = jnp.where((z ^ k) == j, both[span(j, size)], out)
            ref[span(n, size)] = out


def half_of(at, own, pieces, pa, pb, vp, kt, ma, mb, sent, got):
    count = len(pieces)
    tokens = vp.shape[0]
    side = ma.shape[2]
    bit = lambda i, a: (i + 1 + a[CORE]) % 2
    pair = lambda i, a: 2 * (a[Y] if own else 1 - a[Y]) + bit(i, a)
    row_spec = pl.BlockSpec((pieces[0].shape[0], PAIR), lambda i, a: (0, pair(i, a)))
    p_spec = pl.BlockSpec((2, tokens, side), lambda i, a: (pair(i, a), 0, 0))
    stat_spec = lambda n: pl.BlockSpec((1, 2, n), lambda i, a: (pair(i, a), 0, 0))
    block = tokens
    return pl.pallas_call(
        functools.partial(half_kernel, count),
        grid_spec=pltpu.PrefetchScalarGridSpec(
            num_scalar_prefetch=1,
            grid=(2,),
            in_specs=[row_spec] * count
            + [
                p_spec,
                p_spec,
                pl.BlockSpec((tokens, PAIR), lambda i, a: (0, pair(i, a))),
                pl.BlockSpec((PAIR, tokens), lambda i, a: (pair(i, a), 0)),
                stat_spec(side),
                stat_spec(side),
                stat_spec(2 * side),
                stat_spec(2 * side),
            ],
            out_specs=[pl.BlockSpec((block, PAIR), lambda i, a: (0, bit(i, a)))] * 2
            + [pl.BlockSpec((PAIR, 2 * side), lambda i, a: (0, 0))] * 2,
        ),
        out_shape=[like((block, 2 * PAIR))] * 2 + [like((PAIR, 2 * side))] * 2,
        compiler_params=params(),
        cost_estimate=cost(16 * side * tokens * 2 * PAIR * 2, 8 * side * tokens * 2, 0),
    )(at, *pieces, pa, pb, vp, kt, ma, mb, sent, got)


def columns_kernel(count, high, at_ref, *refs):
    x_refs = refs[:count]
    keep_ref, core_ref, y_ref = refs[count : count + 3]
    w_refs, back_ref, send_ref, all_ref = refs[count + 3 : -3], refs[-3], refs[-2], refs[-1]
    side = keep_ref.shape[1] // 2
    far = jnp.concatenate([y_ref[:, side:], y_ref[:, :side]], axis=1)
    dq = (keep_ref[...].astype(F32) + core_ref[...].astype(F32) + far.astype(F32)).astype(BF)
    quarter = side // 2
    back_ref[...] = jnp.concatenate([dq[:, span(0, quarter)], dq[:, span(2, quarter)]], axis=1)
    send_ref[...] = jnp.concatenate([dq[:, span(1, quarter)], dq[:, span(3, quarter)]], axis=1)
    x = jnp.concatenate([r[...] for r in x_refs], axis=0)
    all_ref[...] = dot(dq, x, 1, 0)
    width = x.shape[1] // high
    for ref, order in zip(w_refs, ORDERS, strict=True):
        for n, k in enumerate(order):
            start = pl.multiple_of((at_ref[Z] ^ k) * width, PAIR)
            ref[span(n, ref.shape[0] // 2)] = all_ref[:, pl.ds(start, width)].astype(BF)


def columns_of(at, high, x_pieces, keep, core, y):
    count = len(x_pieces)
    piece, cols = x_pieces[0].shape
    width, rows = keep.shape
    return pl.pallas_call(
        functools.partial(columns_kernel, count, high),
        in_specs=[SMEM] + [VMEM] * (count + 3),
        out_specs=[VMEM] * 4,
        out_shape=[like((2 * width, cols // high))] * 2 + [like((width, rows // 2))] * 2,
        scratch_shapes=[pltpu.VMEM((width, cols), F32)],
        compiler_params=params(),
        cost_estimate=cost(2 * rows * cols * width, 2 * rows * cols),
    )(at, *x_pieces, keep, core, y)


def input_kernel(at_ref, back_ref, x_ref, y_ref, core_ref, wq_ref, out_ref, dq_ref):
    me, x = at_ref[SEQ], at_ref[X]
    size = back_ref.shape[0]

    def put(group, odd, block):
        row = pl.multiple_of((2 * group + (x ^ odd)) * size, PAIR)
        dq_ref[pl.ds(row, size), :] = block

    put(me, 0, back_ref[:, :size])
    put(me, 1, x_ref[:, :size])
    for odd in range(2):
        put(me ^ 2, odd, y_ref[span(odd, size), :size])
        put(me ^ 1, odd, core_ref[span(odd, size), :])
        put(me ^ 3, odd, core_ref[span(2 + odd, size), :])
    out_ref[...] = dot(dq_ref[...], wq_ref[...], 0, 1).astype(BF)


def input_of(at, back, x, y, core, wq):
    size, cols = back.shape[0], wq.shape[1]
    return pl.pallas_call(
        input_kernel,
        in_specs=[SMEM] + [VMEM] * 5,
        out_specs=VMEM,
        out_shape=like((size, cols)),
        scratch_shapes=[pltpu.VMEM((cols, size), BF)],
        compiler_params=params(),
        cost_estimate=cost(2 * size * cols * cols, 2 * cols * cols),
    )(at, back, x, y, core, wq)


def weight_near_kernel(own_ref, got_ref, keep_ref, send_ref):
    rows = keep_ref.shape[0]
    keep_ref[...] = own_ref[:rows].astype(F32) + got_ref[:rows].astype(F32)
    send_ref[...] = (own_ref[rows:].astype(F32) + got_ref[rows:].astype(F32)).astype(BF)


def weight_near(own, got):
    rows, cols = own.shape[0] // 2, own.shape[1]
    return pl.pallas_call(
        weight_near_kernel,
        in_specs=[VMEM] * 2,
        out_specs=[VMEM] * 2,
        out_shape=[like((rows, cols), F32), like((rows, cols))],
        compiler_params=params(),
        cost_estimate=cost(),
    )(own, got)


def weight_sum_kernel(at_ref, own_ref, got_ref, keep_ref, send_ref):
    total = own_ref[...] + got_ref[...].astype(F32)
    size = keep_ref.shape[1]
    a, b = total[:, :size], total[:, size:]
    low = at_ref[X] == 0
    keep_ref[...] = jnp.where(low, a, b)
    send_ref[...] = jnp.where(low, b, a).astype(BF)


def weight_sum(at, own, got):
    rows, cols = own.shape
    return pl.pallas_call(
        weight_sum_kernel,
        in_specs=[SMEM, VMEM, VMEM],
        out_specs=[VMEM] * 2,
        out_shape=[like((rows, cols // 2), F32), like((rows, cols // 2))],
        compiler_params=params(),
        cost_estimate=cost(),
    )(at, own, got)


def weight_out_kernel(at_ref, keep_ref, got_ref, out_ref):
    size = keep_ref.shape[0]
    a, b = keep_ref[...].T, got_ref[...].astype(F32).T
    low = at_ref[X] == 0
    out_ref[:, :size] = jnp.where(low, a, b)
    out_ref[:, size:] = jnp.where(low, b, a)


def weight_out(at, keep, got):
    size, rows = keep.shape
    return pl.pallas_call(
        weight_out_kernel,
        in_specs=[SMEM, VMEM, VMEM],
        out_specs=VMEM,
        out_shape=like((rows, 2 * size), F32),
        compiler_params=params(),
        cost_estimate=cost(1000, 300000),
    )(at, keep, got)


def tokens_kernel(at_ref, *refs):
    y, x, z = at_ref[Y], at_ref[X], at_ref[Z]
    key_ref, val_ref = refs[-2:]
    size = refs[0].shape[0] // 2
    for half in range(2):
        group = 2 * (y ^ (1 - half))
        keep, near, got = refs[3 * half : 3 * half + 3]
        for i, k in enumerate(ORDERS[0] + ORDERS[1]):
            b = z ^ k
            row = pl.multiple_of((b % 2) * size, 16)
            own = (keep if i < 2 else near)[span(i % 2, size)]
            for out_ref, which in ((key_ref, 0), (val_ref, 1)):

                @pl.when(b // 2 == which)
                def _():
                    for c in range(2):
                        for odd, block in ((0, own[:, span(c)]), (1, got[span(i, size), span(c)])):
                            col = pl.multiple_of((2 * (group + c) + (x ^ odd)) * PAIR, PAIR)
                            out_ref[pl.ds(row, size), pl.ds(col, PAIR)] = block


def tokens_out(at, tokens, cols, parts):
    return pl.pallas_call(
        tokens_kernel,
        in_specs=[SMEM] + [VMEM] * len(parts),
        out_specs=[VMEM] * 2,
        out_shape=[like((tokens, cols))] * 2,
        compiler_params=params(),
        cost_estimate=cost(),
    )(at, *parts)


def local_split(n_dp, n_seq, qx, queries, keys, values, attn_out, grad_out, wq):
    high = n_dp // 2
    dp, me = lax.axis_index("dp").astype(jnp.int32), lax.axis_index("seq").astype(jnp.int32)
    at = jnp.stack([dp % 2, me // 2, dp // 2, me % 2, me])
    over_x = lambda t: swap(t, "dp", n_dp, 1)
    over_y = lambda t: swap(t, "seq", n_seq, 2)
    over_core = lambda t: swap(t, "seq", n_seq, 1)
    over_z = lambda t, k: swap(t, "dp", n_dp, 2 * k)
    after = lambda t, *deps: lax.optimization_barrier((t, *deps))[0]

    def rows_of(own, from_x):
        from_y, from_xy = over_y(own), over_y(from_x)
        a = [own, over_core(own), from_x, over_core(from_x)]
        return a, from_y, from_xy

    def far_rows(from_y, from_xy):
        return [from_y, over_core(from_y), from_xy, over_core(from_xy)]

    own, send = pack(queries, grad_out, attn_out)
    kp, vp, kt = pack_tokens(at, keys, values)
    from_x = after(over_x(send), kp)
    ra, r_y, r_xy = rows_of(own, from_x)
    x_from_x = over_x(after(qx, from_x))
    pa, ma, la = side_of(ra, kp)
    rb = far_rows(r_y, after(r_xy, la))
    x_y = over_y(after(qx, r_xy))
    pb, mb, lb, sent = side_of(rb, kp, la)
    send = merge(la, lb, over_core(sent))
    got = over_y(send)
    x_xy = over_y(after(x_from_x, got))
    xa = [qx, over_core(after(qx, got)), x_from_x, over_core(after(x_from_x, got))]

    def half(own, pa):
        return half_of(at, own, ra + rb, pa, pb, vp, kt, ma, mb, send, got)

    def sum_near(keep, send):
        return add(keep, over_z(send, 1))

    def sum_far(near):
        return add_turned(near, over_z(near, 2))

    def spread(total):
        near = over_z(total, 1)
        return [total, near, over_x(stack([total, near]))]

    kv_keep, kv_send, dq_send, dq_keep = half(False, after(pa, x_from_x, x_y))
    first = sum_near(kv_keep, kv_send)
    far = add(dq_keep, over_core(dq_send))
    kv_keep, kv_send, dq_send, dq_keep = half(True, after(pa, far))
    far = over_y(far)
    second = sum_near(kv_keep, kv_send)
    x_y, x_xy = after(x_y, dq_keep), after(x_xy, dq_keep)
    w_keep, w_send, back, back_s = columns_of(
        at, high, xa + far_rows(x_y, x_xy), dq_keep, over_core(dq_send), far
    )
    first, second = sum_far(first), sum_far(second)
    w_keep, w_send = weight_near(w_keep, over_z(w_send, 1))
    w_keep, w_send = weight_sum(at, w_keep, over_z(w_send, 2))
    grad_weight = weight_out(at, w_keep, over_x(w_send))

    from_x = over_x(back_s)
    size = back.shape[0]
    part = lambda i, n: (slice(None), slice(i * size, (i + n) * size))
    from_y = over_y(stack([back, from_x], [part(2, 2)] * 2))
    from_core = over_core(stack([back, from_x, from_y], [part(1, 1)] * 3))
    grad_input = input_of(at, back, from_x, from_y, from_core, wq)
    grad_keys, grad_values = tokens_out(at, *keys.shape, spread(first) + spread(second))
    return (grad_input, grad_keys, grad_values, grad_weight)


def solution(mesh):
    n_dp, n_seq = mesh.shape["dp"], mesh.shape["seq"]

    def run(qx, queries, keys, *rest):
        pairs = queries.shape[1] == 2 * n_seq * PAIR and queries.shape[0] == n_dp * n_seq * PAIR
        split = n_seq == 4 and n_dp == 8 and pairs and (2 * keys.shape[0] // n_seq) % (16 * n_dp // 2) == 0
        return shard(local_split if split else local)(qx, queries, keys, *rest)

    def shard(f):
        return jax.shard_map(
            functools.partial(f, n_dp, n_seq),
            mesh=mesh,
            in_specs=(
                P(("dp", "seq"), None),
                P(("dp", "seq"), None),
                P("seq", None),
                P("seq", None),
                P(("dp", "seq"), None),
                P(("dp", "seq"), None),
                P(),
            ),
            out_specs=(P(("dp", "seq"), None), P("seq", None), P("seq", None), P("dp", "seq")),
            check_vma=False,
        )

    return run
```

```python
import functools
import math

import jax
import jax.numpy as jnp
from jax import lax
from jax.experimental import pallas as pl
from jax.experimental.pallas import tpu as pltpu
from jax.sharding import PartitionSpec as P

HD = 64
PAIR = 2 * HD
SCALE = 1.0 / math.sqrt(HD)
BF = jnp.bfloat16
F32 = jnp.float32
VMEM_LIMIT = 56 * 1024 * 1024


def dot(a, b, ca, cb):
    return lax.dot_general(a, b, (((ca,), (cb,)), ((), ())), preferred_element_type=F32)


def own_lanes(x, head):
    lane = lax.broadcasted_iota(jnp.int32, x.shape, 1)
    mine = lane < HD if head == 0 else lane >= HD
    return jnp.where(mine, x, jnp.zeros_like(x))


def delta_kernel(grad_ref, out_ref, delta_ref):
    prod = grad_ref[...].astype(F32) * out_ref[...].astype(F32)
    cols = prod.T
    heads = cols.shape[0] // HD
    for head in range(heads):
        part = jnp.sum(cols[head * HD : (head + 1) * HD], axis=0, keepdims=True)
        delta_ref[head // 2, head % 2] = part[0]


def delta_of(grad_out, attn_out):
    rows, cols = grad_out.shape
    return pl.pallas_call(
        delta_kernel,
        out_shape=jax.ShapeDtypeStruct((cols // PAIR, 2, rows), F32),
        compiler_params=pltpu.CompilerParams(vmem_limit_bytes=VMEM_LIMIT),
        cost_estimate=pl.CostEstimate(flops=4 * rows * cols, bytes_accessed=4 * rows * cols, transcendentals=0),
    )(grad_out, attn_out)


def probs_kernel(count, *refs):
    q_refs, k_ref = refs[:count], refs[count]
    p_ref, m_ref, lse_ref = refs[count + 1 :]
    q = jnp.concatenate([r[...] for r in q_refs], axis=0) * jnp.asarray(SCALE, BF)
    k = k_ref[...]
    for head in range(2):
        s = dot(own_lanes(k, head), q, 1, 1)
        top = jnp.max(s, axis=0, keepdims=True)
        p = jnp.exp(s - top)
        total = jnp.sum(p, axis=0, keepdims=True)
        p_ref[head] = p.astype(BF)
        m_ref[0, head] = top[0]
        lse_ref[0, head] = (top + jnp.log(total))[0]


def probs_of(q_pieces, keys):
    count = len(q_pieces)
    piece, cols = q_pieces[0].shape
    tokens = keys.shape[0]
    rows = piece * count
    pairs = cols // PAIR
    return pl.pallas_call(
        functools.partial(probs_kernel, count),
        grid=(pairs,),
        in_specs=[pl.BlockSpec((piece, PAIR), lambda i: (0, i))] * count
        + [pl.BlockSpec((tokens, PAIR), lambda i: (0, i))],
        out_specs=[
            pl.BlockSpec((2, tokens, rows), lambda i: (i, 0, 0)),
            pl.BlockSpec((1, 2, rows), lambda i: (i, 0, 0)),
            pl.BlockSpec((1, 2, rows), lambda i: (i, 0, 0)),
        ],
        out_shape=[
            jax.ShapeDtypeStruct((2 * pairs, tokens, rows), BF),
            jax.ShapeDtypeStruct((pairs, 2, rows), F32),
            jax.ShapeDtypeStruct((pairs, 2, rows), F32),
        ],
        compiler_params=pltpu.CompilerParams(vmem_limit_bytes=VMEM_LIMIT),
        cost_estimate=pl.CostEstimate(
            flops=2 * rows * tokens * cols,
            bytes_accessed=2 * rows * tokens * 2 * pairs,
            transcendentals=rows * tokens * 2 * pairs,
        ),
    )(*q_pieces, keys)


def grads_kernel(count, half_ref, *refs):
    q_refs, g_refs = refs[:count], refs[count : 2 * count]
    pa_ref, pb_ref, v_ref, kt_ref, w_ref, delta_ref, dkv_ref, dqt_ref = refs[2 * count :]
    rows = w_ref.shape[2]
    side = rows // 2
    w = w_ref[0]
    delta = delta_ref[0]
    v = v_ref[...]
    first = lax.broadcasted_iota(jnp.int32, (PAIR, rows), 0) < HD
    wide = jnp.where(first, w[0:1], w[1:2]).T
    q = jnp.concatenate([r[...] for r in q_refs], axis=0)
    g = jnp.concatenate([r[...] for r in g_refs], axis=0)
    qw = (q.astype(F32) * (wide * SCALE)).astype(BF)
    gw = (g.astype(F32) * wide).astype(BF)
    dk = jnp.zeros((v.shape[0], PAIR), F32)
    dv = jnp.zeros((v.shape[0], PAIR), F32)
    for half, p_ref in ((0, pa_ref), (1, pb_ref)):
        at = slice(half * side, (half + 1) * side)
        for head in range(2):
            p = p_ref[head]
            dp = dot(v, own_lanes(g[at], head), 1, 1)
            t = (p.astype(F32) * (dp - delta[head : head + 1, at])).astype(BF)
            dv = dv + dot(p, own_lanes(gw[at], head), 1, 0)
            dk = dk + dot(t, own_lanes(qw[at], head), 1, 0)
            dq = dot(kt_ref[head * HD : (head + 1) * HD], t, 1, 0)
            dq = dq * (w[head : head + 1, at] * SCALE)
            dqt_ref[head * HD : (head + 1) * HD, at] = dq.astype(BF)
    dkv_ref[0] = dk.astype(BF)
    dkv_ref[1] = dv.astype(BF)


def grads_of(half, q_pieces, g_pieces, pa, pb, values, keys_t, w, delta):
    count = len(q_pieces)
    piece, cols = q_pieces[0].shape
    tokens = values.shape[0]
    rows = piece * count
    steps = cols // PAIR // 2
    at = lambda i, h: h[0] * steps + i
    row_spec = pl.BlockSpec((piece, PAIR), lambda i, h: (0, at(i, h)))
    p_spec = pl.BlockSpec((2, tokens, rows // 2), lambda i, h: (at(i, h), 0, 0))
    stat_spec = pl.BlockSpec((1, 2, rows), lambda i, h: (at(i, h), 0, 0))
    return pl.pallas_call(
        functools.partial(grads_kernel, count),
        grid_spec=pltpu.PrefetchScalarGridSpec(
            num_scalar_prefetch=1,
            grid=(steps,),
            in_specs=[row_spec] * (2 * count)
            + [
                p_spec,
                p_spec,
                pl.BlockSpec((tokens, PAIR), lambda i, h: (0, at(i, h))),
                pl.BlockSpec((PAIR, tokens), lambda i, h: (at(i, h), 0)),
                stat_spec,
                stat_spec,
            ],
            out_specs=[
                pl.BlockSpec((2, tokens, PAIR), lambda i, h: (0, 0, i)),
                pl.BlockSpec((PAIR, rows), lambda i, h: (i, 0)),
            ],
        ),
        out_shape=[
            jax.ShapeDtypeStruct((2, tokens, cols // 2), BF),
            jax.ShapeDtypeStruct((cols // 2, rows), BF),
        ],
        compiler_params=pltpu.CompilerParams(vmem_limit_bytes=VMEM_LIMIT),
        cost_estimate=pl.CostEstimate(
            flops=4 * rows * tokens * cols,
            bytes_accessed=2 * rows * tokens * 2 * steps,
            transcendentals=0,
        ),
    )(half, *q_pieces, *g_pieces, pa, pb, values, keys_t, w, delta)


def weight_kernel(count, *refs):
    x = jnp.concatenate([r[...] for r in refs[:count]], axis=0)
    refs[count + 1][...] = dot(x, refs[count][...], 0, 1).astype(BF)


def weight_of(x_pieces, dq_cols):
    count = len(x_pieces)
    piece, cols = x_pieces[0].shape
    width, rows = dq_cols.shape
    step = min(cols, 256)
    return pl.pallas_call(
        functools.partial(weight_kernel, count),
        grid=(cols // step,),
        in_specs=[pl.BlockSpec((piece, step), lambda i: (0, i))] * count
        + [pl.BlockSpec((width, rows), lambda i: (0, 0))],
        out_specs=pl.BlockSpec((step, width), lambda i: (i, 0)),
        out_shape=jax.ShapeDtypeStruct((cols, width), BF),
        compiler_params=pltpu.CompilerParams(vmem_limit_bytes=VMEM_LIMIT),
        cost_estimate=pl.CostEstimate(
            flops=2 * rows * cols * width, bytes_accessed=2 * rows * cols, transcendentals=0
        ),
    )(*x_pieces, dq_cols)


def swap(x, axis, size, mask):
    return lax.ppermute(x, axis, [(i, i ^ mask) for i in range(size)])


def gather_pieces(x, axis, size):
    pieces = {0: x}
    bit = size // 2
    while bit:
        for k in list(pieces):
            pieces[k | bit] = swap(pieces[k], axis, size, bit)
        bit //= 2
    return [pieces[k] for k in range(size)]


def flip_pieces(x, count, bit):
    lead, piece = x.shape[:-1], x.shape[-1] // count
    y = x.reshape(lead + (count // (2 * bit), 2, bit * piece))
    return jnp.flip(y, axis=-2).reshape(x.shape)


def pick(blocks, index):
    return lax.dynamic_index_in_dim(blocks, index, 0, keepdims=False)


def exchange_sum(x, axis, size, stride, group, wide=False):
    me = (lax.axis_index(axis) // stride) % group
    total = pick(x, me).astype(F32)
    for k in range(1, group):
        total = total + swap(pick(x, me ^ k), axis, size, k * stride).astype(F32)
    return total if wide else total.astype(BF)


def exchange_gather(x, axis, size, stride, group):
    me = (lax.axis_index(axis) // stride) % group
    out = jnp.zeros((group,) + x.shape, x.dtype)
    for k in range(group):
        got = x if k == 0 else swap(x, axis, size, k * stride)
        out = lax.dynamic_update_index_in_dim(out, got, me ^ k, 0)
    return out


def local(n_dp, n_seq, qx, queries, keys, values, attn_out, grad_out, wq):
    low = max(n_dp // 4, 1)
    high = n_dp // low
    cols = queries.shape[1]
    me = lax.axis_index("seq")
    top = n_seq // 2
    q_pieces = gather_pieces(queries, "seq", n_seq)
    g_pieces = gather_pieces(grad_out, "seq", n_seq)
    x_pieces = gather_pieces(qx, "seq", n_seq)
    keys_t = keys.T
    delta = delta_of(grad_out, attn_out)
    pa, ma, la = probs_of(q_pieces[:top], keys)
    pb, mb, lb = probs_of(q_pieces[top:], keys)
    rows = 2 * la.shape[2]
    peak = jnp.concatenate([ma, mb], axis=2)
    lse = jnp.concatenate([la, lb], axis=2)
    bit = 1
    while bit < n_seq:
        got = swap(jnp.concatenate([lse, delta], axis=2), "seq", n_seq, bit)
        lse = jnp.logaddexp(lse, flip_pieces(got[:, :, :rows], n_seq, bit))
        delta = jnp.concatenate([delta, got[:, :, rows:]], axis=2)
        bit *= 2
    w = jnp.exp(peak - lse)

    mine = (me // top).astype(jnp.int32)
    shards, dqs = [], []
    for half in (1 - mine, mine):
        dkv, dqt = grads_of(half.reshape(1), q_pieces, g_pieces, pa, pb, values, keys_t, w, delta)
        tokens = dkv.shape[1]
        part = dkv.reshape(low, 2 * tokens // low, cols // 2)
        part = exchange_sum(part, "dp", n_dp, 1, low)
        part = part.reshape(high, part.shape[0] // high, cols // 2)
        shards.append(exchange_sum(part, "dp", n_dp, low, high))
        dqs.append(dqt)

    def narrow(dqt):
        blocks = dqt.reshape(top, dqt.shape[0] // top, rows)
        bit = 1
        base = me % top
        while bit < top:
            view = blocks.reshape((blocks.shape[0] // 2, 2) + blocks.shape[1:])
            own = (base // bit) % 2
            keep = lax.dynamic_index_in_dim(view, own, 1, keepdims=False)
            send = lax.dynamic_index_in_dim(view, 1 - own, 1, keepdims=False)
            got = swap(send, "seq", n_seq, bit)
            got = flip_pieces(got, n_seq, bit)
            blocks = (keep.astype(F32) + got.astype(F32)).astype(BF)
            bit *= 2
        return blocks[0]

    other, own = narrow(dqs[0]), narrow(dqs[1])
    got = flip_pieces(swap(other, "seq", n_seq, top), n_seq, top)
    dq_cols = (own.astype(F32) + got.astype(F32)).astype(BF)

    weight = weight_of(x_pieces, dq_cols)
    weight = weight.reshape(high, low, weight.shape[0] // n_dp, weight.shape[1])
    weight = exchange_sum(weight, "dp", n_dp, low, high)
    grad_weight = exchange_sum(weight, "dp", n_dp, 1, low, wide=True)

    piece = rows // n_seq
    width = cols // n_seq
    dq_rows = jnp.zeros((n_seq, width, piece), BF)
    for k in range(n_seq):
        block = dq_cols[:, k * piece : (k + 1) * piece]
        block = block if k == 0 else swap(block, "seq", n_seq, k)
        dq_rows = lax.dynamic_update_index_in_dim(dq_rows, block, me ^ k, 0)
    grad_input = dot(dq_rows.reshape(cols, piece), wq, 0, 1).astype(BF)

    halves = []
    for shard in shards:
        part = exchange_gather(shard, "dp", n_dp, low, high)
        part = part.reshape((-1,) + part.shape[2:])
        part = exchange_gather(part, "dp", n_dp, 1, low)
        halves.append(part.reshape(2, -1, cols // 2))
    other, own = halves
    left = jnp.where(mine == 0, own, other)
    right = jnp.where(mine == 0, other, own)
    both = jnp.concatenate([left, right], axis=2)
    return (grad_input, both[0], both[1], grad_weight)


def params(limit=24):
    return pltpu.CompilerParams(vmem_limit_bytes=limit * 1024 * 1024)


def cost(flops=0, nbytes=0, exps=0):
    return pl.CostEstimate(flops=1, bytes_accessed=1, transcendentals=0)


def like(shape, dtype=BF):
    return jax.ShapeDtypeStruct(shape, dtype)


SMEM = pl.BlockSpec(memory_space=pltpu.SMEM)
VMEM = pl.BlockSpec(memory_space=pltpu.VMEM)


def span(i, size=PAIR):
    return slice(i * size, (i + 1) * size)


def flip_core(x):
    n = x.shape[-1] // PAIR
    return jnp.concatenate([x[..., span(i ^ 1)] for i in range(n)], axis=-1)


def whole(shape):
    return pl.BlockSpec(shape, lambda i: (0,) * len(shape))


X, Y, Z, CORE, SEQ = range(5)
EXTRA = 16
ORDERS = ((0, 2), (1, 3))


def split_parts(d):
    high = d.astype(BF).astype(F32)
    mid = (d - high).astype(BF).astype(F32)
    return high, mid, d - high - mid


def pack_kernel(q_ref, g_ref, o_ref, keep_ref, send_ref):
    low = lax.axis_index("dp") % 2 == 0
    rows = q_ref.shape[0]
    pairs = keep_ref.shape[1] // PAIR
    for p in range(pairs):
        scale = jnp.asarray(SCALE, BF)
        a, b = q_ref[:, span(2 * p)] * scale, q_ref[:, span(2 * p + 1)] * scale
        keep_ref[:rows, span(p)] = jnp.where(low, a, b)
        send_ref[:rows, span(p)] = jnp.where(low, b, a)
        a, b = g_ref[:, span(2 * p)], g_ref[:, span(2 * p + 1)]
        keep_ref[rows : 2 * rows, span(p)] = jnp.where(low, a, b)
        send_ref[rows : 2 * rows, span(p)] = jnp.where(low, b, a)
    cols = (g_ref[...].astype(F32) * o_ref[...].astype(F32)).T
    for p in range(pairs):
        both = []
        for h in range(4):
            both.append(split_parts(jnp.sum(cols[span(4 * p + h, HD)], axis=0, keepdims=True)))
        pad = [jnp.zeros((EXTRA - 6, rows), F32)]
        a = jnp.concatenate([both[h][n] for n in range(3) for h in (0, 1)] + pad, axis=0).astype(BF)
        b = jnp.concatenate([both[h][n] for n in range(3) for h in (2, 3)] + pad, axis=0).astype(BF)
        keep_ref[2 * rows :, span(p)] = jnp.where(low, a, b)
        send_ref[2 * rows :, span(p)] = jnp.where(low, b, a)


def pack(queries, grad_out, attn_out):
    rows, cols = queries.shape
    steps = 2
    block = pl.BlockSpec((rows, cols // steps), lambda i: (0, i))
    total = 2 * rows + EXTRA
    half = pl.BlockSpec((total, cols // 2 // steps), lambda i: (0, i))
    return pl.pallas_call(
        pack_kernel,
        grid=(steps,),
        in_specs=[block] * 3,
        out_specs=[half] * 2,
        out_shape=[like((total, cols // 2))] * 2,
        compiler_params=params(60),
        cost_estimate=cost(),
    )(queries, grad_out, attn_out)


def pack_tokens_kernel(at_ref, k_ref, v_ref, kp_ref, vp_ref, kt_ref):
    low = at_ref[X] == 0
    for p in range(kp_ref.shape[1] // PAIR):
        k = jnp.where(low, k_ref[:, span(2 * p)], k_ref[:, span(2 * p + 1)])
        kp_ref[:, span(p)] = k
        kt_ref[span(p)] = k.T
        vp_ref[:, span(p)] = jnp.where(low, v_ref[:, span(2 * p)], v_ref[:, span(2 * p + 1)])


def pack_tokens(at, keys, values):
    tokens, cols = keys.shape
    steps = 2
    block = pl.BlockSpec((tokens, cols // steps), lambda i: (0, i))
    half = pl.BlockSpec((tokens, cols // 2 // steps), lambda i: (0, i))
    return pl.pallas_call(
        pack_tokens_kernel,
        grid=(steps,),
        in_specs=[SMEM, block, block],
        out_specs=[half, half, pl.BlockSpec((cols // 2 // steps, tokens), lambda i: (i, 0))],
        out_shape=[like((tokens, cols // 2))] * 2 + [like((cols // 2, tokens))],
        compiler_params=params(),
        cost_estimate=cost(),
    )(at, keys, values)


def add_kernel(*refs):
    total = refs[0][...].astype(F32)
    for r in refs[1:-1]:
        total = total + r[...].astype(F32)
    refs[-1][...] = total.astype(BF)


def add(*parts):
    return pl.pallas_call(
        add_kernel,
        in_specs=[VMEM] * len(parts),
        out_specs=VMEM,
        out_shape=like(parts[0].shape),
        compiler_params=params(),
        cost_estimate=cost(),
    )(*parts)


def add_turned_kernel(own_ref, got_ref, out_ref):
    rows = own_ref.shape[0] // 2
    for n in range(2):
        total = own_ref[span(n, rows)].astype(F32) + got_ref[span(1 - n, rows)].astype(F32)
        out_ref[span(n, rows)] = total.astype(BF)


def add_turned(own, got):
    return pl.pallas_call(
        add_turned_kernel,
        in_specs=[VMEM] * 2,
        out_specs=VMEM,
        out_shape=like(own.shape),
        compiler_params=params(),
        cost_estimate=cost(),
    )(own, got)


def stack_kernel(cuts, *refs):
    out_ref, row = refs[-1], 0
    for r, cut in zip(refs[:-1], cuts, strict=True):
        block = r[...] if cut is None else r[cut]
        out_ref[row : row + block.shape[0], :] = block
        row += block.shape[0]


def stack(parts, cuts=None):
    cuts = cuts or [None] * len(parts)
    shapes = [jax.eval_shape(lambda t, c=c: t if c is None else t[c], t).shape for t, c in zip(parts, cuts, strict=True)]
    rows, width = sum(t[0] for t in shapes), shapes[0][1]
    return pl.pallas_call(
        functools.partial(stack_kernel, cuts),
        in_specs=[VMEM] * len(parts),
        out_specs=VMEM,
        out_shape=like((rows, width)),
        compiler_params=params(),
        cost_estimate=cost(),
    )(*parts)


def side_kernel(count, step, last, *refs):
    q_refs, k_ref = refs[:count], refs[count]
    if last:
        la_ref, p_ref, m_ref, lse_ref, send_ref = refs[count + 1 :]
    else:
        p_ref, m_ref, lse_ref = refs[count + 1 :]
    for j in range(step):
        q = jnp.concatenate([r[:, span(j)] for r in q_refs], axis=0)
        k = k_ref[:, span(j)]
        for head in range(2):
            s = dot(own_lanes(k, head), q, 1, 1)
            top = jnp.max(s, axis=0, keepdims=True)
            p = jnp.exp(s - top)
            total = jnp.sum(p, axis=0, keepdims=True)
            p_ref[2 * j + head] = p.astype(BF)
            m_ref[j, head] = top[0]
            lse_ref[j, head] = (top + jnp.log(total))[0]
    if last:
        send_ref[...] = jnp.concatenate([flip_core(la_ref[...]), flip_core(lse_ref[...])], axis=-1)


def side_of(pieces, keys, extra=None, step=2):
    count = len(pieces)
    cols = pieces[0].shape[1]
    tokens = keys.shape[0]
    piece = (pieces[0].shape[0] - EXTRA) // 2
    rows, pairs = piece * count, cols // PAIR
    stat_spec = lambda n: pl.BlockSpec((step, 2, n), lambda i: (i, 0, 0))
    in_specs = [pl.BlockSpec((piece, step * PAIR), lambda i: (0, i))] * count
    in_specs += [pl.BlockSpec((tokens, step * PAIR), lambda i: (0, i))]
    out_specs = [pl.BlockSpec((2 * step, tokens, rows), lambda i: (i, 0, 0)), stat_spec(rows), stat_spec(rows)]
    out_shape = [like((2 * pairs, tokens, rows)), like((pairs, 2, rows), F32), like((pairs, 2, rows), F32)]
    args = [*pieces, keys]
    if extra is not None:
        in_specs += [stat_spec(rows)]
        out_specs += [stat_spec(2 * rows)]
        out_shape += [like((pairs, 2, 2 * rows), F32)]
        args += [extra]
    return pl.pallas_call(
        functools.partial(side_kernel, count, step, extra is not None),
        grid=(pairs // step,),
        in_specs=in_specs,
        out_specs=out_specs,
        out_shape=out_shape,
        compiler_params=params(),
        cost_estimate=cost(2 * rows * tokens * cols, 4 * rows * tokens * pairs, 2 * rows * tokens * pairs),
    )(*args)


def log_add(a, b):
    top = jnp.maximum(a, b)
    return top + jnp.log(jnp.exp(a - top) + jnp.exp(b - top))


def merge_kernel(la_ref, lb_ref, got_ref, send_ref):
    side = la_ref.shape[2]
    send_ref[:, :, :side] = log_add(lb_ref[...], got_ref[:, :, side:])
    send_ref[:, :, side:] = log_add(la_ref[...], got_ref[:, :, :side])


def merge(la, lb, got):
    pairs, two, side = la.shape
    return pl.pallas_call(
        merge_kernel,
        in_specs=[VMEM] * 3,
        out_specs=VMEM,
        out_shape=like((pairs, two, 2 * side), F32),
        compiler_params=params(),
        cost_estimate=cost(1000, 100000),
    )(la, lb, got)


def half_kernel(count, at_ref, *refs):
    row_refs = refs[:count]
    piece = (row_refs[0].shape[0] - EXTRA) // 2
    pa_ref, pb_ref, v_ref, kt_ref, ma_ref, mb_ref, sent_ref, got_ref = refs[count : count + 8]
    kv_refs, dqs_ref, dqk_ref = refs[count + 8 : -2], refs[-2], refs[-1]
    side = ma_ref.shape[2]
    z = at_ref[Z]
    v = v_ref[...]
    tokens = v.shape[0]
    dk = jnp.zeros((tokens, PAIR), F32)
    dv = jnp.zeros((tokens, PAIR), F32)
    first = lax.broadcasted_iota(jnp.int32, (PAIR, side), 0) < HD
    halves = []
    for b, p_ref, m_ref in ((0, pa_ref, ma_ref), (1, pb_ref, mb_ref)):
        lse = log_add(sent_ref[0, :, span(1 - b, side)], got_ref[0, :, span(b, side)])
        w = jnp.exp(m_ref[0] - lse)
        wide = jnp.where(first, w[0:1], w[1:2]).T
        at = slice(b * count // 2, (b + 1) * count // 2)
        q = jnp.concatenate([r[:piece] for r in row_refs[at]], axis=0)
        g = jnp.concatenate([r[piece : 2 * piece] for r in row_refs[at]], axis=0)
        parts = [r[2 * piece :].astype(F32) for r in row_refs[at]]
        delta = jnp.concatenate([d[0:2] + d[2:4] + d[4:6] for d in parts], axis=1)
        qw = (q.astype(F32) * wide).astype(BF)
        gw = (g.astype(F32) * wide).astype(BF)
        parts = []
        for head in range(2):
            p = p_ref[head]
            dp = dot(v, own_lanes(g, head), 1, 1)
            t = (p.astype(F32) * (dp - delta[head : head + 1])).astype(BF)
            dv = dv + dot(p, own_lanes(gw, head), 1, 0)
            dk = dk + dot(t, own_lanes(qw, head), 1, 0)
            dq = dot(kt_ref[span(head, HD)], t, 1, 0)
            parts.append((dq * (w[head : head + 1] * SCALE)).astype(BF))
        halves.append(jnp.concatenate(parts, axis=0))
    dq = jnp.concatenate(halves, axis=1)

    @pl.when(pl.program_id(0) == 0)
    def _():
        dqs_ref[...] = flip_core(dq)

    @pl.when(pl.program_id(0) == 1)
    def _():
        dqk_ref[...] = dq

    both = jnp.concatenate([dk.astype(BF), dv.astype(BF)], axis=0)
    size = both.shape[0] // 4
    for ref, order in zip(kv_refs, ORDERS, strict=True):
        for n, k in enumerate(order):
            out = both[:size]
            for j in range(1, 4):
                out = jnp.where((z ^ k) == j, both[span(j, size)], out)
            ref[span(n, size)] = out


def half_of(at, own, pieces, pa, pb, vp, kt, ma, mb, sent, got):
    count = len(pieces)
    tokens = vp.shape[0]
    side = ma.shape[2]
    bit = lambda i, a: (i + 1 + a[CORE]) % 2
    pair = lambda i, a: 2 * (a[Y] if own else 1 - a[Y]) + bit(i, a)
    row_spec = pl.BlockSpec((pieces[0].shape[0], PAIR), lambda i, a: (0, pair(i, a)))
    p_spec = pl.BlockSpec((2, tokens, side), lambda i, a: (pair(i, a), 0, 0))
    stat_spec = lambda n: pl.BlockSpec((1, 2, n), lambda i, a: (pair(i, a), 0, 0))
    block = tokens
    return pl.pallas_call(
        functools.partial(half_kernel, count),
        grid_spec=pltpu.PrefetchScalarGridSpec(
            num_scalar_prefetch=1,
            grid=(2,),
            in_specs=[row_spec] * count
            + [
                p_spec,
                p_spec,
                pl.BlockSpec((tokens, PAIR), lambda i, a: (0, pair(i, a))),
                pl.BlockSpec((PAIR, tokens), lambda i, a: (pair(i, a), 0)),
                stat_spec(side),
                stat_spec(side),
                stat_spec(2 * side),
                stat_spec(2 * side),
            ],
            out_specs=[pl.BlockSpec((block, PAIR), lambda i, a: (0, bit(i, a)))] * 2
            + [pl.BlockSpec((PAIR, 2 * side), lambda i, a: (0, 0))] * 2,
        ),
        out_shape=[like((block, 2 * PAIR))] * 2 + [like((PAIR, 2 * side))] * 2,
        compiler_params=params(),
        cost_estimate=cost(16 * side * tokens * 2 * PAIR * 2, 8 * side * tokens * 2, 0),
    )(at, *pieces, pa, pb, vp, kt, ma, mb, sent, got)


def columns_kernel(count, high, at_ref, *refs):
    x_refs = refs[:count]
    keep_ref, core_ref, y_ref = refs[count : count + 3]
    w_refs, back_ref, send_ref, all_ref = refs[count + 3 : -3], refs[-3], refs[-2], refs[-1]
    side = keep_ref.shape[1] // 2
    far = jnp.concatenate([y_ref[:, side:], y_ref[:, :side]], axis=1)
    dq = (keep_ref[...].astype(F32) + core_ref[...].astype(F32) + far.astype(F32)).astype(BF)
    quarter = side // 2
    back_ref[...] = jnp.concatenate([dq[:, span(0, quarter)], dq[:, span(2, quarter)]], axis=1)
    send_ref[...] = jnp.concatenate([dq[:, span(1, quarter)], dq[:, span(3, quarter)]], axis=1)
    x = jnp.concatenate([r[...] for r in x_refs], axis=0)
    all_ref[...] = dot(dq, x, 1, 0)
    width = x.shape[1] // high
    for ref, order in zip(w_refs, ORDERS, strict=True):
        for n, k in enumerate(order):
            start = pl.multiple_of((at_ref[Z] ^ k) * width, PAIR)
            ref[span(n, ref.shape[0] // 2)] = all_ref[:, pl.ds(start, width)].astype(BF)


def columns_of(at, high, x_pieces, keep, core, y):
    count = len(x_pieces)
    piece, cols = x_pieces[0].shape
    width, rows = keep.shape
    return pl.pallas_call(
        functools.partial(columns_kernel, count, high),
        in_specs=[SMEM] + [VMEM] * (count + 3),
        out_specs=[VMEM] * 4,
        out_shape=[like((2 * width, cols // high))] * 2 + [like((width, rows // 2))] * 2,
        scratch_shapes=[pltpu.VMEM((width, cols), F32)],
        compiler_params=params(),
        cost_estimate=cost(2 * rows * cols * width, 2 * rows * cols),
    )(at, *x_pieces, keep, core, y)


def input_kernel(at_ref, back_ref, x_ref, y_ref, core_ref, wq_ref, out_ref, dq_ref):
    me, x = at_ref[SEQ], at_ref[X]
    size = back_ref.shape[0]

    def put(group, odd, block):
        row = pl.multiple_of((2 * group + (x ^ odd)) * size, PAIR)
        dq_ref[pl.ds(row, size), :] = block

    put(me, 0, back_ref[:, :size])
    put(me, 1, x_ref[:, :size])
    for odd in range(2):
        put(me ^ 2, odd, y_ref[span(odd, size), :size])
        put(me ^ 1, odd, core_ref[span(odd, size), :])
        put(me ^ 3, odd, core_ref[span(2 + odd, size), :])
    out_ref[...] = dot(dq_ref[...], wq_ref[...], 0, 1).astype(BF)


def input_of(at, back, x, y, core, wq):
    size, cols = back.shape[0], wq.shape[1]
    return pl.pallas_call(
        input_kernel,
        in_specs=[SMEM] + [VMEM] * 5,
        out_specs=VMEM,
        out_shape=like((size, cols)),
        scratch_shapes=[pltpu.VMEM((cols, size), BF)],
        compiler_params=params(),
        cost_estimate=cost(2 * size * cols * cols, 2 * cols * cols),
    )(at, back, x, y, core, wq)


def weight_near_kernel(own_ref, got_ref, keep_ref, send_ref):
    rows = keep_ref.shape[0]
    keep_ref[...] = own_ref[:rows].astype(F32) + got_ref[:rows].astype(F32)
    send_ref[...] = (own_ref[rows:].astype(F32) + got_ref[rows:].astype(F32)).astype(BF)


def weight_near(own, got):
    rows, cols = own.shape[0] // 2, own.shape[1]
    return pl.pallas_call(
        weight_near_kernel,
        in_specs=[VMEM] * 2,
        out_specs=[VMEM] * 2,
        out_shape=[like((rows, cols), F32), like((rows, cols))],
        compiler_params=params(),
        cost_estimate=cost(),
    )(own, got)


def weight_sum_kernel(at_ref, own_ref, got_ref, keep_ref, send_ref):
    total = own_ref[...] + got_ref[...].astype(F32)
    size = keep_ref.shape[1]
    a, b = total[:, :size], total[:, size:]
    low = at_ref[X] == 0
    keep_ref[...] = jnp.where(low, a, b)
    send_ref[...] = jnp.where(low, b, a).astype(BF)


def weight_sum(at, own, got):
    rows, cols = own.shape
    return pl.pallas_call(
        weight_sum_kernel,
        in_specs=[SMEM, VMEM, VMEM],
        out_specs=[VMEM] * 2,
        out_shape=[like((rows, cols // 2), F32), like((rows, cols // 2))],
        compiler_params=params(),
        cost_estimate=cost(),
    )(at, own, got)


def weight_out_kernel(at_ref, keep_ref, got_ref, out_ref):
    size = keep_ref.shape[0]
    a, b = keep_ref[...].T, got_ref[...].astype(F32).T
    low = at_ref[X] == 0
    out_ref[:, :size] = jnp.where(low, a, b)
    out_ref[:, size:] = jnp.where(low, b, a)


def weight_out(at, keep, got):
    size, rows = keep.shape
    return pl.pallas_call(
        weight_out_kernel,
        in_specs=[SMEM, VMEM, VMEM],
        out_specs=VMEM,
        out_shape=like((rows, 2 * size), F32),
        compiler_params=params(),
        cost_estimate=cost(1000, 300000),
    )(at, keep, got)


def tokens_kernel(at_ref, *refs):
    y, x, z = at_ref[Y], at_ref[X], at_ref[Z]
    key_ref, val_ref = refs[-2:]
    size = refs[0].shape[0] // 2
    for half in range(2):
        group = 2 * (y ^ (1 - half))
        keep, near, keep_x, near_x = refs[4 * half : 4 * half + 4]
        for i, k in enumerate(ORDERS[0] + ORDERS[1]):
            b = z ^ k
            row = pl.multiple_of((b % 2) * size, 16)
            own = (keep if i < 2 else near)[span(i % 2, size)]
            got = (keep_x if i < 2 else near_x)[span(i % 2, size)]
            for out_ref, which in ((key_ref, 0), (val_ref, 1)):

                @pl.when(b // 2 == which)
                def _():
                    for c in range(2):
                        for odd, block in ((0, own[:, span(c)]), (1, got[:, span(c)])):
                            col = pl.multiple_of((2 * (group + c) + (x ^ odd)) * PAIR, PAIR)
                            out_ref[pl.ds(row, size), pl.ds(col, PAIR)] = block


def tokens_out(at, tokens, cols, parts):
    return pl.pallas_call(
        tokens_kernel,
        in_specs=[SMEM] + [VMEM] * len(parts),
        out_specs=[VMEM] * 2,
        out_shape=[like((tokens, cols))] * 2,
        compiler_params=params(),
        cost_estimate=cost(),
    )(at, *parts)


def local_split(n_dp, n_seq, qx, queries, keys, values, attn_out, grad_out, wq):
    high = n_dp // 2
    dp, me = lax.axis_index("dp").astype(jnp.int32), lax.axis_index("seq").astype(jnp.int32)
    at = jnp.stack([dp % 2, me // 2, dp // 2, me % 2, me])
    over_x = lambda t: swap(t, "dp", n_dp, 1)
    over_y = lambda t: swap(t, "seq", n_seq, 2)
    over_core = lambda t: swap(t, "seq", n_seq, 1)
    over_z = lambda t, k: swap(t, "dp", n_dp, 2 * k)
    after = lambda t, *deps: lax.optimization_barrier((t, *deps))[0]

    def rows_of(own, from_x):
        from_y, from_xy = over_y(own), over_y(from_x)
        a = [own, over_core(own), from_x, over_core(from_x)]
        return a, from_y, from_xy

    def far_rows(from_y, from_xy):
        return [from_y, over_core(from_y), from_xy, over_core(from_xy)]

    own, send = pack(queries, grad_out, attn_out)
    kp, vp, kt = pack_tokens(at, keys, values)
    from_x = after(over_x(send), kp)
    ra, r_y, r_xy = rows_of(own, from_x)
    x_from_x = over_x(after(qx, own))
    pa, ma, la = side_of(ra, kp)
    rb = far_rows(r_y, after(r_xy, la, x_from_x))
    x_y = over_y(after(qx, r_xy))
    pb, mb, lb, sent = side_of(rb, kp, la)
    send = merge(la, lb, over_core(sent))
    got = over_y(send)
    x_xy = over_y(after(x_from_x, send))
    xa = [qx, over_core(after(qx, got)), x_from_x, over_core(after(x_from_x, got))]

    def half(own, pa):
        return half_of(at, own, ra + rb, pa, pb, vp, kt, ma, mb, send, got)

    def sum_near(keep, send, *deps):
        return add(after(keep, *deps), over_z(send, 1))

    def sum_far(near):
        return add_turned(near, over_z(near, 2))

    def spread(total):
        near = over_z(total, 1)
        return [total, near, over_x(total), over_x(near)]

    kv_keep, kv_send, dq_send, dq_keep = half(False, after(pa, x_from_x, x_y))
    first = (kv_keep, kv_send)
    far = add(dq_keep, over_core(dq_send))
    kv_keep, kv_send, dq_send, dq_keep = half(True, after(pa, far))
    far = over_y(far)
    first = sum_near(after(first[0], dq_keep), first[1])
    second = sum_near(kv_keep, kv_send, far)
    x_y, x_xy = after(x_y, dq_keep), after(x_xy, dq_keep)
    w_keep, w_send, back, back_s = columns_of(
        at, high, xa + far_rows(x_y, x_xy), dq_keep, over_core(dq_send), far
    )
    first, second = sum_far(first), sum_far(second)
    w_keep, w_send = weight_near(w_keep, over_z(w_send, 1))
    w_keep, w_send = weight_sum(at, w_keep, over_z(w_send, 2))
    w_got = over_x(w_send)

    from_x = over_x(back_s)
    size = back.shape[0]
    part = lambda i, n: (slice(None), slice(i * size, (i + n) * size))
    from_y = over_y(stack([back, from_x], [part(2, 2)] * 2))
    from_core = over_core(stack([back, from_x, from_y], [part(1, 1)] * 3))
    grad_input = input_of(at, back, from_x, from_y, from_core, wq)
    first = spread(first)
    second = spread(after(second, first[2]))
    grad_keys, grad_values = tokens_out(at, *keys.shape, first + second)
    grad_weight = weight_out(at, after(w_keep, grad_input, grad_keys), w_got)
    return (grad_input, grad_keys, grad_values, grad_weight)


def solution(mesh):
    n_dp, n_seq = mesh.shape["dp"], mesh.shape["seq"]

    def run(qx, queries, keys, *rest):
        pairs = queries.shape[1] == 2 * n_seq * PAIR and queries.shape[0] == n_dp * n_seq * PAIR
        split = n_seq == 4 and n_dp == 8 and pairs and (2 * keys.shape[0] // n_seq) % (16 * n_dp // 2) == 0
        return shard(local_split if split else local)(qx, queries, keys, *rest)

    def shard(f):
        return jax.shard_map(
            functools.partial(f, n_dp, n_seq),
            mesh=mesh,
            in_specs=(
                P(("dp", "seq"), None),
                P(("dp", "seq"), None),
                P("seq", None),
                P("seq", None),
                P(("dp", "seq"), None),
                P(("dp", "seq"), None),
                P(),
            ),
            out_specs=(P(("dp", "seq"), None), P("seq", None), P("seq", None), P("dp", "seq")),
            check_vma=False,
        )

    return run
```

```python
import functools
import math

import jax
import jax.numpy as jnp
from jax import lax
from jax.experimental import pallas as pl
from jax.experimental.pallas import tpu as pltpu
from jax.sharding import PartitionSpec as P

HD = 64
PAIR = 2 * HD
SCALE = 1.0 / math.sqrt(HD)
BF = jnp.bfloat16
F32 = jnp.float32
VMEM_LIMIT = 56 * 1024 * 1024


def dot(a, b, ca, cb):
    return lax.dot_general(a, b, (((ca,), (cb,)), ((), ())), preferred_element_type=F32)


def own_lanes(x, head):
    lane = lax.broadcasted_iota(jnp.int32, x.shape, 1)
    mine = lane < HD if head == 0 else lane >= HD
    return jnp.where(mine, x, jnp.zeros_like(x))


def delta_kernel(grad_ref, out_ref, delta_ref):
    prod = grad_ref[...].astype(F32) * out_ref[...].astype(F32)
    cols = prod.T
    heads = cols.shape[0] // HD
    for head in range(heads):
        part = jnp.sum(cols[head * HD : (head + 1) * HD], axis=0, keepdims=True)
        delta_ref[head // 2, head % 2] = part[0]


def delta_of(grad_out, attn_out):
    rows, cols = grad_out.shape
    return pl.pallas_call(
        delta_kernel,
        out_shape=jax.ShapeDtypeStruct((cols // PAIR, 2, rows), F32),
        compiler_params=pltpu.CompilerParams(vmem_limit_bytes=VMEM_LIMIT),
        cost_estimate=pl.CostEstimate(flops=4 * rows * cols, bytes_accessed=4 * rows * cols, transcendentals=0),
    )(grad_out, attn_out)


def probs_kernel(count, *refs):
    q_refs, k_ref = refs[:count], refs[count]
    p_ref, m_ref, lse_ref = refs[count + 1 :]
    q = jnp.concatenate([r[...] for r in q_refs], axis=0) * jnp.asarray(SCALE, BF)
    k = k_ref[...]
    for head in range(2):
        s = dot(own_lanes(k, head), q, 1, 1)
        top = jnp.max(s, axis=0, keepdims=True)
        p = jnp.exp(s - top)
        total = jnp.sum(p, axis=0, keepdims=True)
        p_ref[head] = p.astype(BF)
        m_ref[0, head] = top[0]
        lse_ref[0, head] = (top + jnp.log(total))[0]


def probs_of(q_pieces, keys):
    count = len(q_pieces)
    piece, cols = q_pieces[0].shape
    tokens = keys.shape[0]
    rows = piece * count
    pairs = cols // PAIR
    return pl.pallas_call(
        functools.partial(probs_kernel, count),
        grid=(pairs,),
        in_specs=[pl.BlockSpec((piece, PAIR), lambda i: (0, i))] * count
        + [pl.BlockSpec((tokens, PAIR), lambda i: (0, i))],
        out_specs=[
            pl.BlockSpec((2, tokens, rows), lambda i: (i, 0, 0)),
            pl.BlockSpec((1, 2, rows), lambda i: (i, 0, 0)),
            pl.BlockSpec((1, 2, rows), lambda i: (i, 0, 0)),
        ],
        out_shape=[
            jax.ShapeDtypeStruct((2 * pairs, tokens, rows), BF),
            jax.ShapeDtypeStruct((pairs, 2, rows), F32),
            jax.ShapeDtypeStruct((pairs, 2, rows), F32),
        ],
        compiler_params=pltpu.CompilerParams(vmem_limit_bytes=VMEM_LIMIT),
        cost_estimate=pl.CostEstimate(
            flops=2 * rows * tokens * cols,
            bytes_accessed=2 * rows * tokens * 2 * pairs,
            transcendentals=rows * tokens * 2 * pairs,
        ),
    )(*q_pieces, keys)


def grads_kernel(count, half_ref, *refs):
    q_refs, g_refs = refs[:count], refs[count : 2 * count]
    pa_ref, pb_ref, v_ref, kt_ref, w_ref, delta_ref, dkv_ref, dqt_ref = refs[2 * count :]
    rows = w_ref.shape[2]
    side = rows // 2
    w = w_ref[0]
    delta = delta_ref[0]
    v = v_ref[...]
    first = lax.broadcasted_iota(jnp.int32, (PAIR, rows), 0) < HD
    wide = jnp.where(first, w[0:1], w[1:2]).T
    q = jnp.concatenate([r[...] for r in q_refs], axis=0)
    g = jnp.concatenate([r[...] for r in g_refs], axis=0)
    qw = (q.astype(F32) * (wide * SCALE)).astype(BF)
    gw = (g.astype(F32) * wide).astype(BF)
    dk = jnp.zeros((v.shape[0], PAIR), F32)
    dv = jnp.zeros((v.shape[0], PAIR), F32)
    for half, p_ref in ((0, pa_ref), (1, pb_ref)):
        at = slice(half * side, (half + 1) * side)
        for head in range(2):
            p = p_ref[head]
            dp = dot(v, own_lanes(g[at], head), 1, 1)
            t = (p.astype(F32) * (dp - delta[head : head + 1, at])).astype(BF)
            dv = dv + dot(p, own_lanes(gw[at], head), 1, 0)
            dk = dk + dot(t, own_lanes(qw[at], head), 1, 0)
            dq = dot(kt_ref[head * HD : (head + 1) * HD], t, 1, 0)
            dq = dq * (w[head : head + 1, at] * SCALE)
            dqt_ref[head * HD : (head + 1) * HD, at] = dq.astype(BF)
    dkv_ref[0] = dk.astype(BF)
    dkv_ref[1] = dv.astype(BF)


def grads_of(half, q_pieces, g_pieces, pa, pb, values, keys_t, w, delta):
    count = len(q_pieces)
    piece, cols = q_pieces[0].shape
    tokens = values.shape[0]
    rows = piece * count
    steps = cols // PAIR // 2
    at = lambda i, h: h[0] * steps + i
    row_spec = pl.BlockSpec((piece, PAIR), lambda i, h: (0, at(i, h)))
    p_spec = pl.BlockSpec((2, tokens, rows // 2), lambda i, h: (at(i, h), 0, 0))
    stat_spec = pl.BlockSpec((1, 2, rows), lambda i, h: (at(i, h), 0, 0))
    return pl.pallas_call(
        functools.partial(grads_kernel, count),
        grid_spec=pltpu.PrefetchScalarGridSpec(
            num_scalar_prefetch=1,
            grid=(steps,),
            in_specs=[row_spec] * (2 * count)
            + [
                p_spec,
                p_spec,
                pl.BlockSpec((tokens, PAIR), lambda i, h: (0, at(i, h))),
                pl.BlockSpec((PAIR, tokens), lambda i, h: (at(i, h), 0)),
                stat_spec,
                stat_spec,
            ],
            out_specs=[
                pl.BlockSpec((2, tokens, PAIR), lambda i, h: (0, 0, i)),
                pl.BlockSpec((PAIR, rows), lambda i, h: (i, 0)),
            ],
        ),
        out_shape=[
            jax.ShapeDtypeStruct((2, tokens, cols // 2), BF),
            jax.ShapeDtypeStruct((cols // 2, rows), BF),
        ],
        compiler_params=pltpu.CompilerParams(vmem_limit_bytes=VMEM_LIMIT),
        cost_estimate=pl.CostEstimate(
            flops=4 * rows * tokens * cols,
            bytes_accessed=2 * rows * tokens * 2 * steps,
            transcendentals=0,
        ),
    )(half, *q_pieces, *g_pieces, pa, pb, values, keys_t, w, delta)


def weight_kernel(count, *refs):
    x = jnp.concatenate([r[...] for r in refs[:count]], axis=0)
    refs[count + 1][...] = dot(x, refs[count][...], 0, 1).astype(BF)


def weight_of(x_pieces, dq_cols):
    count = len(x_pieces)
    piece, cols = x_pieces[0].shape
    width, rows = dq_cols.shape
    step = min(cols, 256)
    return pl.pallas_call(
        functools.partial(weight_kernel, count),
        grid=(cols // step,),
        in_specs=[pl.BlockSpec((piece, step), lambda i: (0, i))] * count
        + [pl.BlockSpec((width, rows), lambda i: (0, 0))],
        out_specs=pl.BlockSpec((step, width), lambda i: (i, 0)),
        out_shape=jax.ShapeDtypeStruct((cols, width), BF),
        compiler_params=pltpu.CompilerParams(vmem_limit_bytes=VMEM_LIMIT),
        cost_estimate=pl.CostEstimate(
            flops=2 * rows * cols * width, bytes_accessed=2 * rows * cols, transcendentals=0
        ),
    )(*x_pieces, dq_cols)


def swap(x, axis, size, mask):
    return lax.ppermute(x, axis, [(i, i ^ mask) for i in range(size)])


def gather_pieces(x, axis, size):
    pieces = {0: x}
    bit = size // 2
    while bit:
        for k in list(pieces):
            pieces[k | bit] = swap(pieces[k], axis, size, bit)
        bit //= 2
    return [pieces[k] for k in range(size)]


def flip_pieces(x, count, bit):
    lead, piece = x.shape[:-1], x.shape[-1] // count
    y = x.reshape(lead + (count // (2 * bit), 2, bit * piece))
    return jnp.flip(y, axis=-2).reshape(x.shape)


def pick(blocks, index):
    return lax.dynamic_index_in_dim(blocks, index, 0, keepdims=False)


def exchange_sum(x, axis, size, stride, group, wide=False):
    me = (lax.axis_index(axis) // stride) % group
    total = pick(x, me).astype(F32)
    for k in range(1, group):
        total = total + swap(pick(x, me ^ k), axis, size, k * stride).astype(F32)
    return total if wide else total.astype(BF)


def exchange_gather(x, axis, size, stride, group):
    me = (lax.axis_index(axis) // stride) % group
    out = jnp.zeros((group,) + x.shape, x.dtype)
    for k in range(group):
        got = x if k == 0 else swap(x, axis, size, k * stride)
        out = lax.dynamic_update_index_in_dim(out, got, me ^ k, 0)
    return out


def local(n_dp, n_seq, qx, queries, keys, values, attn_out, grad_out, wq):
    low = max(n_dp // 4, 1)
    high = n_dp // low
    cols = queries.shape[1]
    me = lax.axis_index("seq")
    top = n_seq // 2
    q_pieces = gather_pieces(queries, "seq", n_seq)
    g_pieces = gather_pieces(grad_out, "seq", n_seq)
    x_pieces = gather_pieces(qx, "seq", n_seq)
    keys_t = keys.T
    delta = delta_of(grad_out, attn_out)
    pa, ma, la = probs_of(q_pieces[:top], keys)
    pb, mb, lb = probs_of(q_pieces[top:], keys)
    rows = 2 * la.shape[2]
    peak = jnp.concatenate([ma, mb], axis=2)
    lse = jnp.concatenate([la, lb], axis=2)
    bit = 1
    while bit < n_seq:
        got = swap(jnp.concatenate([lse, delta], axis=2), "seq", n_seq, bit)
        lse = jnp.logaddexp(lse, flip_pieces(got[:, :, :rows], n_seq, bit))
        delta = jnp.concatenate([delta, got[:, :, rows:]], axis=2)
        bit *= 2
    w = jnp.exp(peak - lse)

    mine = (me // top).astype(jnp.int32)
    shards, dqs = [], []
    for half in (1 - mine, mine):
        dkv, dqt = grads_of(half.reshape(1), q_pieces, g_pieces, pa, pb, values, keys_t, w, delta)
        tokens = dkv.shape[1]
        part = dkv.reshape(low, 2 * tokens // low, cols // 2)
        part = exchange_sum(part, "dp", n_dp, 1, low)
        part = part.reshape(high, part.shape[0] // high, cols // 2)
        shards.append(exchange_sum(part, "dp", n_dp, low, high))
        dqs.append(dqt)

    def narrow(dqt):
        blocks = dqt.reshape(top, dqt.shape[0] // top, rows)
        bit = 1
        base = me % top
        while bit < top:
            view = blocks.reshape((blocks.shape[0] // 2, 2) + blocks.shape[1:])
            own = (base // bit) % 2
            keep = lax.dynamic_index_in_dim(view, own, 1, keepdims=False)
            send = lax.dynamic_index_in_dim(view, 1 - own, 1, keepdims=False)
            got = swap(send, "seq", n_seq, bit)
            got = flip_pieces(got, n_seq, bit)
            blocks = (keep.astype(F32) + got.astype(F32)).astype(BF)
            bit *= 2
        return blocks[0]

    other, own = narrow(dqs[0]), narrow(dqs[1])
    got = flip_pieces(swap(other, "seq", n_seq, top), n_seq, top)
    dq_cols = (own.astype(F32) + got.astype(F32)).astype(BF)

    weight = weight_of(x_pieces, dq_cols)
    weight = weight.reshape(high, low, weight.shape[0] // n_dp, weight.shape[1])
    weight = exchange_sum(weight, "dp", n_dp, low, high)
    grad_weight = exchange_sum(weight, "dp", n_dp, 1, low, wide=True)

    piece = rows // n_seq
    width = cols // n_seq
    dq_rows = jnp.zeros((n_seq, width, piece), BF)
    for k in range(n_seq):
        block = dq_cols[:, k * piece : (k + 1) * piece]
        block = block if k == 0 else swap(block, "seq", n_seq, k)
        dq_rows = lax.dynamic_update_index_in_dim(dq_rows, block, me ^ k, 0)
    grad_input = dot(dq_rows.reshape(cols, piece), wq, 0, 1).astype(BF)

    halves = []
    for shard in shards:
        part = exchange_gather(shard, "dp", n_dp, low, high)
        part = part.reshape((-1,) + part.shape[2:])
        part = exchange_gather(part, "dp", n_dp, 1, low)
        halves.append(part.reshape(2, -1, cols // 2))
    other, own = halves
    left = jnp.where(mine == 0, own, other)
    right = jnp.where(mine == 0, other, own)
    both = jnp.concatenate([left, right], axis=2)
    return (grad_input, both[0], both[1], grad_weight)


def params(limit=24):
    return pltpu.CompilerParams(vmem_limit_bytes=limit * 1024 * 1024)


def cost(flops=0, nbytes=0, exps=0):
    return pl.CostEstimate(flops=1, bytes_accessed=1, transcendentals=0)


def like(shape, dtype=BF):
    return jax.ShapeDtypeStruct(shape, dtype)


SMEM = pl.BlockSpec(memory_space=pltpu.SMEM)
VMEM = pl.BlockSpec(memory_space=pltpu.VMEM)


def span(i, size=PAIR):
    return slice(i * size, (i + 1) * size)


def flip_core(x):
    n = x.shape[-1] // PAIR
    return jnp.concatenate([x[..., span(i ^ 1)] for i in range(n)], axis=-1)


def whole(shape):
    return pl.BlockSpec(shape, lambda i: (0,) * len(shape))


X, Y, Z, CORE, SEQ = range(5)
EXTRA = 16
ORDERS = ((0, 2), (1, 3))


def split_parts(d):
    high = d.astype(BF).astype(F32)
    mid = (d - high).astype(BF).astype(F32)
    return high, mid, d - high - mid


def pack_kernel(q_ref, g_ref, o_ref, keep_ref, send_ref):
    low = lax.axis_index("dp") % 2 == 0
    rows = q_ref.shape[0]
    pairs = keep_ref.shape[1] // PAIR
    for p in range(pairs):
        scale = jnp.asarray(SCALE, BF)
        a, b = q_ref[:, span(2 * p)] * scale, q_ref[:, span(2 * p + 1)] * scale
        keep_ref[:rows, span(p)] = jnp.where(low, a, b)
        send_ref[:rows, span(p)] = jnp.where(low, b, a)
        a, b = g_ref[:, span(2 * p)], g_ref[:, span(2 * p + 1)]
        keep_ref[rows : 2 * rows, span(p)] = jnp.where(low, a, b)
        send_ref[rows : 2 * rows, span(p)] = jnp.where(low, b, a)
    cols = (g_ref[...].astype(F32) * o_ref[...].astype(F32)).T
    for p in range(pairs):
        both = []
        for h in range(4):
            both.append(split_parts(jnp.sum(cols[span(4 * p + h, HD)], axis=0, keepdims=True)))
        pad = [jnp.zeros((EXTRA - 6, rows), F32)]
        a = jnp.concatenate([both[h][n] for n in range(3) for h in (0, 1)] + pad, axis=0).astype(BF)
        b = jnp.concatenate([both[h][n] for n in range(3) for h in (2, 3)] + pad, axis=0).astype(BF)
        keep_ref[2 * rows :, span(p)] = jnp.where(low, a, b)
        send_ref[2 * rows :, span(p)] = jnp.where(low, b, a)


def pack(queries, grad_out, attn_out):
    rows, cols = queries.shape
    steps = 2
    block = pl.BlockSpec((rows, cols // steps), lambda i: (0, i))
    total = 2 * rows + EXTRA
    half = pl.BlockSpec((total, cols // 2 // steps), lambda i: (0, i))
    return pl.pallas_call(
        pack_kernel,
        grid=(steps,),
        in_specs=[block] * 3,
        out_specs=[half] * 2,
        out_shape=[like((total, cols // 2))] * 2,
        compiler_params=params(60),
        cost_estimate=cost(),
    )(queries, grad_out, attn_out)


def pack_tokens_kernel(at_ref, k_ref, v_ref, kp_ref, vp_ref, kt_ref):
    low = at_ref[X] == 0
    for p in range(kp_ref.shape[1] // PAIR):
        k = jnp.where(low, k_ref[:, span(2 * p)], k_ref[:, span(2 * p + 1)])
        kp_ref[:, span(p)] = k
        kt_ref[span(p)] = k.T
        vp_ref[:, span(p)] = jnp.where(low, v_ref[:, span(2 * p)], v_ref[:, span(2 * p + 1)])


def pack_tokens(at, keys, values):
    tokens, cols = keys.shape
    steps = 2
    block = pl.BlockSpec((tokens, cols // steps), lambda i: (0, i))
    half = pl.BlockSpec((tokens, cols // 2 // steps), lambda i: (0, i))
    return pl.pallas_call(
        pack_tokens_kernel,
        grid=(steps,),
        in_specs=[SMEM, block, block],
        out_specs=[half, half, pl.BlockSpec((cols // 2 // steps, tokens), lambda i: (i, 0))],
        out_shape=[like((tokens, cols // 2))] * 2 + [like((cols // 2, tokens))],
        compiler_params=params(),
        cost_estimate=cost(),
    )(at, keys, values)


def add_kernel(*refs):
    total = refs[0][...].astype(F32)
    for r in refs[1:-1]:
        total = total + r[...].astype(F32)
    refs[-1][...] = total.astype(BF)


def add(*parts):
    return pl.pallas_call(
        add_kernel,
        in_specs=[VMEM] * len(parts),
        out_specs=VMEM,
        out_shape=like(parts[0].shape),
        compiler_params=params(),
        cost_estimate=cost(),
    )(*parts)


def add_turned_kernel(own_ref, got_ref, out_ref):
    rows = own_ref.shape[0] // 2
    for n in range(2):
        total = own_ref[span(n, rows)].astype(F32) + got_ref[span(1 - n, rows)].astype(F32)
        out_ref[span(n, rows)] = total.astype(BF)


def add_turned(own, got):
    return pl.pallas_call(
        add_turned_kernel,
        in_specs=[VMEM] * 2,
        out_specs=VMEM,
        out_shape=like(own.shape),
        compiler_params=params(),
        cost_estimate=cost(),
    )(own, got)


def stack_kernel(cuts, *refs):
    out_ref, row = refs[-1], 0
    for r, cut in zip(refs[:-1], cuts, strict=True):
        block = r[...] if cut is None else r[cut]
        out_ref[row : row + block.shape[0], :] = block
        row += block.shape[0]


def stack(parts, cuts=None):
    cuts = cuts or [None] * len(parts)
    shapes = [jax.eval_shape(lambda t, c=c: t if c is None else t[c], t).shape for t, c in zip(parts, cuts, strict=True)]
    rows, width = sum(t[0] for t in shapes), shapes[0][1]
    return pl.pallas_call(
        functools.partial(stack_kernel, cuts),
        in_specs=[VMEM] * len(parts),
        out_specs=VMEM,
        out_shape=like((rows, width)),
        compiler_params=params(),
        cost_estimate=cost(),
    )(*parts)


def side_kernel(count, step, last, *refs):
    q_refs, k_ref = refs[:count], refs[count]
    if last:
        la_ref, p_ref, m_ref, lse_ref, send_ref = refs[count + 1 :]
    else:
        p_ref, m_ref, lse_ref = refs[count + 1 :]
    for j in range(step):
        q = jnp.concatenate([r[:, span(j)] for r in q_refs], axis=0)
        k = k_ref[:, span(j)]
        for head in range(2):
            s = dot(own_lanes(k, head), q, 1, 1)
            top = jnp.max(s, axis=0, keepdims=True)
            p = jnp.exp(s - top)
            total = jnp.sum(p, axis=0, keepdims=True)
            p_ref[2 * j + head] = p.astype(BF)
            m_ref[j, head] = top[0]
            lse_ref[j, head] = (top + jnp.log(total))[0]
    if last:
        send_ref[...] = jnp.concatenate([flip_core(la_ref[...]), flip_core(lse_ref[...])], axis=-1)


def side_of(pieces, keys, extra=None, step=2):
    count = len(pieces)
    cols = pieces[0].shape[1]
    tokens = keys.shape[0]
    piece = (pieces[0].shape[0] - EXTRA) // 2
    rows, pairs = piece * count, cols // PAIR
    stat_spec = lambda n: pl.BlockSpec((step, 2, n), lambda i: (i, 0, 0))
    in_specs = [pl.BlockSpec((piece, step * PAIR), lambda i: (0, i))] * count
    in_specs += [pl.BlockSpec((tokens, step * PAIR), lambda i: (0, i))]
    out_specs = [pl.BlockSpec((2 * step, tokens, rows), lambda i: (i, 0, 0)), stat_spec(rows), stat_spec(rows)]
    out_shape = [like((2 * pairs, tokens, rows)), like((pairs, 2, rows), F32), like((pairs, 2, rows), F32)]
    args = [*pieces, keys]
    if extra is not None:
        in_specs += [stat_spec(rows)]
        out_specs += [stat_spec(2 * rows)]
        out_shape += [like((pairs, 2, 2 * rows), F32)]
        args += [extra]
    return pl.pallas_call(
        functools.partial(side_kernel, count, step, extra is not None),
        grid=(pairs // step,),
        in_specs=in_specs,
        out_specs=out_specs,
        out_shape=out_shape,
        compiler_params=params(),
        cost_estimate=cost(2 * rows * tokens * cols, 4 * rows * tokens * pairs, 2 * rows * tokens * pairs),
    )(*args)


def log_add(a, b):
    top = jnp.maximum(a, b)
    return top + jnp.log(jnp.exp(a - top) + jnp.exp(b - top))


def merge_kernel(la_ref, lb_ref, got_ref, send_ref):
    side = la_ref.shape[2]
    send_ref[:, :, :side] = log_add(lb_ref[...], got_ref[:, :, side:])
    send_ref[:, :, side:] = log_add(la_ref[...], got_ref[:, :, :side])


def merge(la, lb, got):
    pairs, two, side = la.shape
    return pl.pallas_call(
        merge_kernel,
        in_specs=[VMEM] * 3,
        out_specs=VMEM,
        out_shape=like((pairs, two, 2 * side), F32),
        compiler_params=params(),
        cost_estimate=cost(1000, 100000),
    )(la, lb, got)


def half_kernel(count, at_ref, *refs):
    row_refs = refs[:count]
    piece = (row_refs[0].shape[0] - EXTRA) // 2
    pa_ref, pb_ref, v_ref, kt_ref, ma_ref, mb_ref, sent_ref, got_ref = refs[count : count + 8]
    kv_refs, dqs_ref, dqk_ref = refs[count + 8 : -2], refs[-2], refs[-1]
    side = ma_ref.shape[2]
    z = at_ref[Z]
    v = v_ref[...]
    tokens = v.shape[0]
    dk = jnp.zeros((tokens, PAIR), F32)
    dv = jnp.zeros((tokens, PAIR), F32)
    first = lax.broadcasted_iota(jnp.int32, (PAIR, side), 0) < HD
    halves = []
    for b, p_ref, m_ref in ((0, pa_ref, ma_ref), (1, pb_ref, mb_ref)):
        lse = log_add(sent_ref[0, :, span(1 - b, side)], got_ref[0, :, span(b, side)])
        w = jnp.exp(m_ref[0] - lse)
        wide = jnp.where(first, w[0:1], w[1:2]).T
        at = slice(b * count // 2, (b + 1) * count // 2)
        q = jnp.concatenate([r[:piece] for r in row_refs[at]], axis=0)
        g = jnp.concatenate([r[piece : 2 * piece] for r in row_refs[at]], axis=0)
        parts = [r[2 * piece :].astype(F32) for r in row_refs[at]]
        delta = jnp.concatenate([d[0:2] + d[2:4] + d[4:6] for d in parts], axis=1)
        qw = (q.astype(F32) * wide).astype(BF)
        gw = (g.astype(F32) * wide).astype(BF)
        parts = []
        for head in range(2):
            p = p_ref[head]
            dp = dot(v, own_lanes(g, head), 1, 1)
            t = (p.astype(F32) * (dp - delta[head : head + 1])).astype(BF)
            dv = dv + dot(p, own_lanes(gw, head), 1, 0)
            dk = dk + dot(t, own_lanes(qw, head), 1, 0)
            dq = dot(kt_ref[span(head, HD)], t, 1, 0)
            parts.append((dq * (w[head : head + 1] * SCALE)).astype(BF))
        halves.append(jnp.concatenate(parts, axis=0))
    dq = jnp.concatenate(halves, axis=1)

    @pl.when(pl.program_id(0) == 0)
    def _():
        dqs_ref[...] = flip_core(dq)

    @pl.when(pl.program_id(0) == 1)
    def _():
        dqk_ref[...] = dq

    both = jnp.concatenate([dk.astype(BF), dv.astype(BF)], axis=0)
    size = both.shape[0] // 4
    for ref, order in zip(kv_refs, ORDERS, strict=True):
        for n, k in enumerate(order):
            out = both[:size]
            for j in range(1, 4):
                out = jnp.where((z ^ k) == j, both[span(j, size)], out)
            ref[span(n, size)] = out


def half_of(at, own, pieces, pa, pb, vp, kt, ma, mb, sent, got):
    count = len(pieces)
    tokens = vp.shape[0]
    side = ma.shape[2]
    bit = lambda i, a: (i + 1 + a[CORE]) % 2
    pair = lambda i, a: 2 * (a[Y] if own else 1 - a[Y]) + bit(i, a)
    row_spec = pl.BlockSpec((pieces[0].shape[0], PAIR), lambda i, a: (0, pair(i, a)))
    p_spec = pl.BlockSpec((2, tokens, side), lambda i, a: (pair(i, a), 0, 0))
    stat_spec = lambda n: pl.BlockSpec((1, 2, n), lambda i, a: (pair(i, a), 0, 0))
    block = tokens
    return pl.pallas_call(
        functools.partial(half_kernel, count),
        grid_spec=pltpu.PrefetchScalarGridSpec(
            num_scalar_prefetch=1,
            grid=(2,),
            in_specs=[row_spec] * count
            + [
                p_spec,
                p_spec,
                pl.BlockSpec((tokens, PAIR), lambda i, a: (0, pair(i, a))),
                pl.BlockSpec((PAIR, tokens), lambda i, a: (pair(i, a), 0)),
                stat_spec(side),
                stat_spec(side),
                stat_spec(2 * side),
                stat_spec(2 * side),
            ],
            out_specs=[pl.BlockSpec((block, PAIR), lambda i, a: (0, bit(i, a)))] * 2
            + [pl.BlockSpec((PAIR, 2 * side), lambda i, a: (0, 0))] * 2,
        ),
        out_shape=[like((block, 2 * PAIR))] * 2 + [like((PAIR, 2 * side))] * 2,
        compiler_params=params(),
        cost_estimate=cost(16 * side * tokens * 2 * PAIR * 2, 8 * side * tokens * 2, 0),
    )(at, *pieces, pa, pb, vp, kt, ma, mb, sent, got)


def columns_kernel(count, high, at_ref, *refs):
    x_refs = refs[:count]
    keep_ref, core_ref, y_ref = refs[count : count + 3]
    w_refs, back_ref, send_ref, all_ref = refs[count + 3 : -3], refs[-3], refs[-2], refs[-1]
    side = keep_ref.shape[1] // 2
    far = jnp.concatenate([y_ref[:, side:], y_ref[:, :side]], axis=1)
    dq = (keep_ref[...].astype(F32) + core_ref[...].astype(F32) + far.astype(F32)).astype(BF)
    quarter = side // 2
    back_ref[...] = jnp.concatenate([dq[:, span(0, quarter)], dq[:, span(2, quarter)]], axis=1)
    send_ref[...] = jnp.concatenate([dq[:, span(1, quarter)], dq[:, span(3, quarter)]], axis=1)
    x = jnp.concatenate([r[...] for r in x_refs], axis=0)
    all_ref[...] = dot(dq, x, 1, 0)
    width = x.shape[1] // high
    for ref, order in zip(w_refs, ORDERS, strict=True):
        for n, k in enumerate(order):
            start = pl.multiple_of((at_ref[Z] ^ k) * width, PAIR)
            ref[span(n, ref.shape[0] // 2)] = all_ref[:, pl.ds(start, width)].astype(BF)


def columns_of(at, high, x_pieces, keep, core, y):
    count = len(x_pieces)
    piece, cols = x_pieces[0].shape
    width, rows = keep.shape
    return pl.pallas_call(
        functools.partial(columns_kernel, count, high),
        in_specs=[SMEM] + [VMEM] * (count + 3),
        out_specs=[VMEM] * 4,
        out_shape=[like((2 * width, cols // high))] * 2 + [like((width, rows // 2))] * 2,
        scratch_shapes=[pltpu.VMEM((width, cols), F32)],
        compiler_params=params(),
        cost_estimate=cost(2 * rows * cols * width, 2 * rows * cols),
    )(at, *x_pieces, keep, core, y)


def input_kernel(at_ref, back_ref, x_ref, y_ref, core_ref, wq_ref, out_ref, dq_ref):
    me, x = at_ref[SEQ], at_ref[X]
    size = back_ref.shape[0]

    def put(group, odd, block):
        row = pl.multiple_of((2 * group + (x ^ odd)) * size, PAIR)
        dq_ref[pl.ds(row, size), :] = block

    put(me, 0, back_ref[:, :size])
    put(me, 1, x_ref[:, :size])
    for odd in range(2):
        put(me ^ 2, odd, y_ref[span(odd, size), :size])
        put(me ^ 1, odd, core_ref[span(odd, size), :])
        put(me ^ 3, odd, core_ref[span(2 + odd, size), :])
    out_ref[...] = dot(dq_ref[...], wq_ref[...], 0, 1).astype(BF)


def input_of(at, back, x, y, core, wq):
    size, cols = back.shape[0], wq.shape[1]
    return pl.pallas_call(
        input_kernel,
        in_specs=[SMEM] + [VMEM] * 5,
        out_specs=VMEM,
        out_shape=like((size, cols)),
        scratch_shapes=[pltpu.VMEM((cols, size), BF)],
        compiler_params=params(),
        cost_estimate=cost(2 * size * cols * cols, 2 * cols * cols),
    )(at, back, x, y, core, wq)


def weight_near_kernel(own_ref, got_ref, keep_ref, send_ref):
    rows = keep_ref.shape[0]
    keep_ref[...] = own_ref[:rows].astype(F32) + got_ref[:rows].astype(F32)
    send_ref[...] = (own_ref[rows:].astype(F32) + got_ref[rows:].astype(F32)).astype(BF)


def weight_near(own, got):
    rows, cols = own.shape[0] // 2, own.shape[1]
    return pl.pallas_call(
        weight_near_kernel,
        in_specs=[VMEM] * 2,
        out_specs=[VMEM] * 2,
        out_shape=[like((rows, cols), F32), like((rows, cols))],
        compiler_params=params(),
        cost_estimate=cost(),
    )(own, got)


def weight_sum_kernel(at_ref, own_ref, got_ref, keep_ref, send_ref):
    total = own_ref[...] + got_ref[...].astype(F32)
    size = keep_ref.shape[1]
    a, b = total[:, :size], total[:, size:]
    low = at_ref[X] == 0
    keep_ref[...] = jnp.where(low, a, b)
    send_ref[...] = jnp.where(low, b, a).astype(BF)


def weight_sum(at, own, got):
    rows, cols = own.shape
    return pl.pallas_call(
        weight_sum_kernel,
        in_specs=[SMEM, VMEM, VMEM],
        out_specs=[VMEM] * 2,
        out_shape=[like((rows, cols // 2), F32), like((rows, cols // 2))],
        compiler_params=params(),
        cost_estimate=cost(),
    )(at, own, got)


def weight_out_kernel(at_ref, keep_ref, got_ref, out_ref):
    size = keep_ref.shape[0]
    a, b = keep_ref[...].T, got_ref[...].astype(F32).T
    low = at_ref[X] == 0
    out_ref[:, :size] = jnp.where(low, a, b)
    out_ref[:, size:] = jnp.where(low, b, a)


def weight_out(at, keep, got):
    size, rows = keep.shape
    return pl.pallas_call(
        weight_out_kernel,
        in_specs=[SMEM, VMEM, VMEM],
        out_specs=VMEM,
        out_shape=like((rows, 2 * size), F32),
        compiler_params=params(),
        cost_estimate=cost(1000, 300000),
    )(at, keep, got)


def tokens_kernel(at_ref, *refs):
    y, x, z = at_ref[Y], at_ref[X], at_ref[Z]
    key_ref, val_ref = refs[-2:]
    size = refs[0].shape[0] // 2
    for half in range(2):
        group = 2 * (y ^ (1 - half))
        keep, near, keep_x, near_x = refs[4 * half : 4 * half + 4]
        for i, k in enumerate(ORDERS[0] + ORDERS[1]):
            b = z ^ k
            row = pl.multiple_of((b % 2) * size, 16)
            own = (keep if i < 2 else near)[span(i % 2, size)]
            got = (keep_x if i < 2 else near_x)[span(i % 2, size)]
            for out_ref, which in ((key_ref, 0), (val_ref, 1)):

                @pl.when(b // 2 == which)
                def _():
                    for c in range(2):
                        for odd, block in ((0, own[:, span(c)]), (1, got[:, span(c)])):
                            col = pl.multiple_of((2 * (group + c) + (x ^ odd)) * PAIR, PAIR)
                            out_ref[pl.ds(row, size), pl.ds(col, PAIR)] = block


def tokens_out(at, tokens, cols, parts):
    return pl.pallas_call(
        tokens_kernel,
        in_specs=[SMEM] + [VMEM] * len(parts),
        out_specs=[VMEM] * 2,
        out_shape=[like((tokens, cols))] * 2,
        compiler_params=params(),
        cost_estimate=cost(),
    )(at, *parts)


def local_split(n_dp, n_seq, qx, queries, keys, values, attn_out, grad_out, wq):
    high = n_dp // 2
    dp, me = lax.axis_index("dp").astype(jnp.int32), lax.axis_index("seq").astype(jnp.int32)
    at = jnp.stack([dp % 2, me // 2, dp // 2, me % 2, me])
    over_x = lambda t: swap(t, "dp", n_dp, 1)
    over_y = lambda t: swap(t, "seq", n_seq, 2)
    over_core = lambda t: swap(t, "seq", n_seq, 1)
    over_z = lambda t, k: swap(t, "dp", n_dp, 2 * k)
    after = lambda t, *deps: lax.optimization_barrier((t, *deps))[0]

    def rows_of(own, from_x):
        from_y, from_xy = over_y(own), over_y(from_x)
        a = [own, over_core(own), from_x, over_core(from_x)]
        return a, from_y, from_xy

    def far_rows(from_y, from_xy):
        return [from_y, over_core(from_y), from_xy, over_core(from_xy)]

    own, send = pack(queries, grad_out, attn_out)
    kp, vp, kt = pack_tokens(at, keys, values)
    from_x = after(over_x(send), kp)
    ra, r_y, r_xy = rows_of(own, from_x)
    pa, ma, la = side_of(ra, kp)
    rb = far_rows(r_y, after(r_xy, la))
    x_y = over_y(after(qx, r_xy))
    pb, mb, lb, sent = side_of(rb, kp, la)
    x_from_x = over_x(after(qx, lb))
    send = merge(la, lb, over_core(sent))
    got = over_y(send)
    x_xy = over_y(after(x_from_x, send))
    xa = [qx, over_core(after(qx, got)), x_from_x, over_core(after(x_from_x, got))]

    def half(own, pa):
        return half_of(at, own, ra + rb, pa, pb, vp, kt, ma, mb, send, got)

    def sum_near(keep, send, *deps):
        return add(after(keep, *deps), over_z(send, 1))

    def sum_far(near):
        return add_turned(near, over_z(near, 2))

    def spread(total):
        near = over_z(total, 1)
        return [total, near, over_x(total), over_x(near)]

    kv_keep, kv_send, dq_send, dq_keep = half(False, after(pa, x_y))
    first = (kv_keep, kv_send)
    far = add(dq_keep, over_core(after(dq_send, x_from_x)))
    kv_keep, kv_send, dq_send, dq_keep = half(True, after(pa, far))
    far = over_y(far)
    first = sum_near(after(first[0], dq_keep), first[1])
    second = sum_near(kv_keep, kv_send, far)
    x_y, x_xy = after(x_y, dq_keep), after(x_xy, dq_keep)
    w_keep, w_send, back, back_s = columns_of(
        at, high, xa + far_rows(x_y, x_xy), dq_keep, over_core(dq_send), far
    )
    first, second = sum_far(first), sum_far(second)
    w_keep, w_send = weight_near(w_keep, over_z(w_send, 1))
    w_got = over_z(w_send, 2)

    from_x = over_x(back_s)
    size = back.shape[0]
    part = lambda i, n: (slice(None), slice(i * size, (i + n) * size))
    from_y = over_y(stack([back, from_x], [part(2, 2)] * 2))
    from_core = over_core(stack([back, from_x, from_y], [part(1, 1)] * 3))
    grad_input = input_of(at, back, from_x, from_y, from_core, wq)
    w_keep, w_send = weight_sum(at, after(w_keep, grad_input), w_got)
    w_got = over_x(w_send)
    first = spread(first)
    second = spread(after(second, first[2]))
    grad_keys, grad_values = tokens_out(at, *keys.shape, first + second)
    grad_weight = weight_out(at, after(w_keep, grad_keys), w_got)
    return (grad_input, grad_keys, grad_values, grad_weight)


def solution(mesh):
    n_dp, n_seq = mesh.shape["dp"], mesh.shape["seq"]

    def run(qx, queries, keys, *rest):
        pairs = queries.shape[1] == 2 * n_seq * PAIR and queries.shape[0] == n_dp * n_seq * PAIR
        split = n_seq == 4 and n_dp == 8 and pairs and (2 * keys.shape[0] // n_seq) % (16 * n_dp // 2) == 0
        return shard(local_split if split else local)(qx, queries, keys, *rest)

    def shard(f):
        return jax.shard_map(
            functools.partial(f, n_dp, n_seq),
            mesh=mesh,
            in_specs=(
                P(("dp", "seq"), None),
                P(("dp", "seq"), None),
                P("seq", None),
                P("seq", None),
                P(("dp", "seq"), None),
                P(("dp", "seq"), None),
                P(),
            ),
            out_specs=(P(("dp", "seq"), None), P("seq", None), P("seq", None), P("dp", "seq")),
            check_vma=False,
        )

    return run
```

```python
import functools
import math

import jax
import jax.numpy as jnp
from jax import lax
from jax.experimental import pallas as pl
from jax.experimental.pallas import tpu as pltpu
from jax.sharding import PartitionSpec as P

HD = 64
PAIR = 2 * HD
SCALE = 1.0 / math.sqrt(HD)
BF = jnp.bfloat16
F32 = jnp.float32
VMEM_LIMIT = 56 * 1024 * 1024


def dot(a, b, ca, cb):
    return lax.dot_general(a, b, (((ca,), (cb,)), ((), ())), preferred_element_type=F32)


def own_lanes(x, head):
    lane = lax.broadcasted_iota(jnp.int32, x.shape, 1)
    mine = lane < HD if head == 0 else lane >= HD
    return jnp.where(mine, x, jnp.zeros_like(x))


def delta_kernel(grad_ref, out_ref, delta_ref):
    prod = grad_ref[...].astype(F32) * out_ref[...].astype(F32)
    cols = prod.T
    heads = cols.shape[0] // HD
    for head in range(heads):
        part = jnp.sum(cols[head * HD : (head + 1) * HD], axis=0, keepdims=True)
        delta_ref[head // 2, head % 2] = part[0]


def delta_of(grad_out, attn_out):
    rows, cols = grad_out.shape
    return pl.pallas_call(
        delta_kernel,
        out_shape=jax.ShapeDtypeStruct((cols // PAIR, 2, rows), F32),
        compiler_params=pltpu.CompilerParams(vmem_limit_bytes=VMEM_LIMIT),
        cost_estimate=pl.CostEstimate(flops=4 * rows * cols, bytes_accessed=4 * rows * cols, transcendentals=0),
    )(grad_out, attn_out)


def probs_kernel(count, *refs):
    q_refs, k_ref = refs[:count], refs[count]
    p_ref, m_ref, lse_ref = refs[count + 1 :]
    q = jnp.concatenate([r[...] for r in q_refs], axis=0) * jnp.asarray(SCALE, BF)
    k = k_ref[...]
    for head in range(2):
        s = dot(own_lanes(k, head), q, 1, 1)
        top = jnp.max(s, axis=0, keepdims=True)
        p = jnp.exp(s - top)
        total = jnp.sum(p, axis=0, keepdims=True)
        p_ref[head] = p.astype(BF)
        m_ref[0, head] = top[0]
        lse_ref[0, head] = (top + jnp.log(total))[0]


def probs_of(q_pieces, keys):
    count = len(q_pieces)
    piece, cols = q_pieces[0].shape
    tokens = keys.shape[0]
    rows = piece * count
    pairs = cols // PAIR
    return pl.pallas_call(
        functools.partial(probs_kernel, count),
        grid=(pairs,),
        in_specs=[pl.BlockSpec((piece, PAIR), lambda i: (0, i))] * count
        + [pl.BlockSpec((tokens, PAIR), lambda i: (0, i))],
        out_specs=[
            pl.BlockSpec((2, tokens, rows), lambda i: (i, 0, 0)),
            pl.BlockSpec((1, 2, rows), lambda i: (i, 0, 0)),
            pl.BlockSpec((1, 2, rows), lambda i: (i, 0, 0)),
        ],
        out_shape=[
            jax.ShapeDtypeStruct((2 * pairs, tokens, rows), BF),
            jax.ShapeDtypeStruct((pairs, 2, rows), F32),
            jax.ShapeDtypeStruct((pairs, 2, rows), F32),
        ],
        compiler_params=pltpu.CompilerParams(vmem_limit_bytes=VMEM_LIMIT),
        cost_estimate=pl.CostEstimate(
            flops=2 * rows * tokens * cols,
            bytes_accessed=2 * rows * tokens * 2 * pairs,
            transcendentals=rows * tokens * 2 * pairs,
        ),
    )(*q_pieces, keys)


def grads_kernel(count, half_ref, *refs):
    q_refs, g_refs = refs[:count], refs[count : 2 * count]
    pa_ref, pb_ref, v_ref, kt_ref, w_ref, delta_ref, dkv_ref, dqt_ref = refs[2 * count :]
    rows = w_ref.shape[2]
    side = rows // 2
    w = w_ref[0]
    delta = delta_ref[0]
    v = v_ref[...]
    first = lax.broadcasted_iota(jnp.int32, (PAIR, rows), 0) < HD
    wide = jnp.where(first, w[0:1], w[1:2]).T
    q = jnp.concatenate([r[...] for r in q_refs], axis=0)
    g = jnp.concatenate([r[...] for r in g_refs], axis=0)
    qw = (q.astype(F32) * (wide * SCALE)).astype(BF)
    gw = (g.astype(F32) * wide).astype(BF)
    dk = jnp.zeros((v.shape[0], PAIR), F32)
    dv = jnp.zeros((v.shape[0], PAIR), F32)
    for half, p_ref in ((0, pa_ref), (1, pb_ref)):
        at = slice(half * side, (half + 1) * side)
        for head in range(2):
            p = p_ref[head]
            dp = dot(v, own_lanes(g[at], head), 1, 1)
            t = (p.astype(F32) * (dp - delta[head : head + 1, at])).astype(BF)
            dv = dv + dot(p, own_lanes(gw[at], head), 1, 0)
            dk = dk + dot(t, own_lanes(qw[at], head), 1, 0)
            dq = dot(kt_ref[head * HD : (head + 1) * HD], t, 1, 0)
            dq = dq * (w[head : head + 1, at] * SCALE)
            dqt_ref[head * HD : (head + 1) * HD, at] = dq.astype(BF)
    dkv_ref[0] = dk.astype(BF)
    dkv_ref[1] = dv.astype(BF)


def grads_of(half, q_pieces, g_pieces, pa, pb, values, keys_t, w, delta):
    count = len(q_pieces)
    piece, cols = q_pieces[0].shape
    tokens = values.shape[0]
    rows = piece * count
    steps = cols // PAIR // 2
    at = lambda i, h: h[0] * steps + i
    row_spec = pl.BlockSpec((piece, PAIR), lambda i, h: (0, at(i, h)))
    p_spec = pl.BlockSpec((2, tokens, rows // 2), lambda i, h: (at(i, h), 0, 0))
    stat_spec = pl.BlockSpec((1, 2, rows), lambda i, h: (at(i, h), 0, 0))
    return pl.pallas_call(
        functools.partial(grads_kernel, count),
        grid_spec=pltpu.PrefetchScalarGridSpec(
            num_scalar_prefetch=1,
            grid=(steps,),
            in_specs=[row_spec] * (2 * count)
            + [
                p_spec,
                p_spec,
                pl.BlockSpec((tokens, PAIR), lambda i, h: (0, at(i, h))),
                pl.BlockSpec((PAIR, tokens), lambda i, h: (at(i, h), 0)),
                stat_spec,
                stat_spec,
            ],
            out_specs=[
                pl.BlockSpec((2, tokens, PAIR), lambda i, h: (0, 0, i)),
                pl.BlockSpec((PAIR, rows), lambda i, h: (i, 0)),
            ],
        ),
        out_shape=[
            jax.ShapeDtypeStruct((2, tokens, cols // 2), BF),
            jax.ShapeDtypeStruct((cols // 2, rows), BF),
        ],
        compiler_params=pltpu.CompilerParams(vmem_limit_bytes=VMEM_LIMIT),
        cost_estimate=pl.CostEstimate(
            flops=4 * rows * tokens * cols,
            bytes_accessed=2 * rows * tokens * 2 * steps,
            transcendentals=0,
        ),
    )(half, *q_pieces, *g_pieces, pa, pb, values, keys_t, w, delta)


def weight_kernel(count, *refs):
    x = jnp.concatenate([r[...] for r in refs[:count]], axis=0)
    refs[count + 1][...] = dot(x, refs[count][...], 0, 1).astype(BF)


def weight_of(x_pieces, dq_cols):
    count = len(x_pieces)
    piece, cols = x_pieces[0].shape
    width, rows = dq_cols.shape
    step = min(cols, 256)
    return pl.pallas_call(
        functools.partial(weight_kernel, count),
        grid=(cols // step,),
        in_specs=[pl.BlockSpec((piece, step), lambda i: (0, i))] * count
        + [pl.BlockSpec((width, rows), lambda i: (0, 0))],
        out_specs=pl.BlockSpec((step, width), lambda i: (i, 0)),
        out_shape=jax.ShapeDtypeStruct((cols, width), BF),
        compiler_params=pltpu.CompilerParams(vmem_limit_bytes=VMEM_LIMIT),
        cost_estimate=pl.CostEstimate(
            flops=2 * rows * cols * width, bytes_accessed=2 * rows * cols, transcendentals=0
        ),
    )(*x_pieces, dq_cols)


def swap(x, axis, size, mask):
    return lax.ppermute(x, axis, [(i, i ^ mask) for i in range(size)])


def gather_pieces(x, axis, size):
    pieces = {0: x}
    bit = size // 2
    while bit:
        for k in list(pieces):
            pieces[k | bit] = swap(pieces[k], axis, size, bit)
        bit //= 2
    return [pieces[k] for k in range(size)]


def flip_pieces(x, count, bit):
    lead, piece = x.shape[:-1], x.shape[-1] // count
    y = x.reshape(lead + (count // (2 * bit), 2, bit * piece))
    return jnp.flip(y, axis=-2).reshape(x.shape)


def pick(blocks, index):
    return lax.dynamic_index_in_dim(blocks, index, 0, keepdims=False)


def exchange_sum(x, axis, size, stride, group, wide=False):
    me = (lax.axis_index(axis) // stride) % group
    total = pick(x, me).astype(F32)
    for k in range(1, group):
        total = total + swap(pick(x, me ^ k), axis, size, k * stride).astype(F32)
    return total if wide else total.astype(BF)


def exchange_gather(x, axis, size, stride, group):
    me = (lax.axis_index(axis) // stride) % group
    out = jnp.zeros((group,) + x.shape, x.dtype)
    for k in range(group):
        got = x if k == 0 else swap(x, axis, size, k * stride)
        out = lax.dynamic_update_index_in_dim(out, got, me ^ k, 0)
    return out


def local(n_dp, n_seq, qx, queries, keys, values, attn_out, grad_out, wq):
    low = max(n_dp // 4, 1)
    high = n_dp // low
    cols = queries.shape[1]
    me = lax.axis_index("seq")
    top = n_seq // 2
    q_pieces = gather_pieces(queries, "seq", n_seq)
    g_pieces = gather_pieces(grad_out, "seq", n_seq)
    x_pieces = gather_pieces(qx, "seq", n_seq)
    keys_t = keys.T
    delta = delta_of(grad_out, attn_out)
    pa, ma, la = probs_of(q_pieces[:top], keys)
    pb, mb, lb = probs_of(q_pieces[top:], keys)
    rows = 2 * la.shape[2]
    peak = jnp.concatenate([ma, mb], axis=2)
    lse = jnp.concatenate([la, lb], axis=2)
    bit = 1
    while bit < n_seq:
        got = swap(jnp.concatenate([lse, delta], axis=2), "seq", n_seq, bit)
        lse = jnp.logaddexp(lse, flip_pieces(got[:, :, :rows], n_seq, bit))
        delta = jnp.concatenate([delta, got[:, :, rows:]], axis=2)
        bit *= 2
    w = jnp.exp(peak - lse)

    mine = (me // top).astype(jnp.int32)
    shards, dqs = [], []
    for half in (1 - mine, mine):
        dkv, dqt = grads_of(half.reshape(1), q_pieces, g_pieces, pa, pb, values, keys_t, w, delta)
        tokens = dkv.shape[1]
        part = dkv.reshape(low, 2 * tokens // low, cols // 2)
        part = exchange_sum(part, "dp", n_dp, 1, low)
        part = part.reshape(high, part.shape[0] // high, cols // 2)
        shards.append(exchange_sum(part, "dp", n_dp, low, high))
        dqs.append(dqt)

    def narrow(dqt):
        blocks = dqt.reshape(top, dqt.shape[0] // top, rows)
        bit = 1
        base = me % top
        while bit < top:
            view = blocks.reshape((blocks.shape[0] // 2, 2) + blocks.shape[1:])
            own = (base // bit) % 2
            keep = lax.dynamic_index_in_dim(view, own, 1, keepdims=False)
            send = lax.dynamic_index_in_dim(view, 1 - own, 1, keepdims=False)
            got = swap(send, "seq", n_seq, bit)
            got = flip_pieces(got, n_seq, bit)
            blocks = (keep.astype(F32) + got.astype(F32)).astype(BF)
            bit *= 2
        return blocks[0]

    other, own = narrow(dqs[0]), narrow(dqs[1])
    got = flip_pieces(swap(other, "seq", n_seq, top), n_seq, top)
    dq_cols = (own.astype(F32) + got.astype(F32)).astype(BF)

    weight = weight_of(x_pieces, dq_cols)
    weight = weight.reshape(high, low, weight.shape[0] // n_dp, weight.shape[1])
    weight = exchange_sum(weight, "dp", n_dp, low, high)
    grad_weight = exchange_sum(weight, "dp", n_dp, 1, low, wide=True)

    piece = rows // n_seq
    width = cols // n_seq
    dq_rows = jnp.zeros((n_seq, width, piece), BF)
    for k in range(n_seq):
        block = dq_cols[:, k * piece : (k + 1) * piece]
        block = block if k == 0 else swap(block, "seq", n_seq, k)
        dq_rows = lax.dynamic_update_index_in_dim(dq_rows, block, me ^ k, 0)
    grad_input = dot(dq_rows.reshape(cols, piece), wq, 0, 1).astype(BF)

    halves = []
    for shard in shards:
        part = exchange_gather(shard, "dp", n_dp, low, high)
        part = part.reshape((-1,) + part.shape[2:])
        part = exchange_gather(part, "dp", n_dp, 1, low)
        halves.append(part.reshape(2, -1, cols // 2))
    other, own = halves
    left = jnp.where(mine == 0, own, other)
    right = jnp.where(mine == 0, other, own)
    both = jnp.concatenate([left, right], axis=2)
    return (grad_input, both[0], both[1], grad_weight)


def params(limit=24):
    return pltpu.CompilerParams(vmem_limit_bytes=limit * 1024 * 1024)


def cost(flops=0, nbytes=0, exps=0):
    return pl.CostEstimate(flops=1, bytes_accessed=1, transcendentals=0)


def like(shape, dtype=BF):
    return jax.ShapeDtypeStruct(shape, dtype)


SMEM = pl.BlockSpec(memory_space=pltpu.SMEM)
VMEM = pl.BlockSpec(memory_space=pltpu.VMEM)


def span(i, size=PAIR):
    return slice(i * size, (i + 1) * size)


def flip_core(x):
    n = x.shape[-1] // PAIR
    return jnp.concatenate([x[..., span(i ^ 1)] for i in range(n)], axis=-1)


def whole(shape):
    return pl.BlockSpec(shape, lambda i: (0,) * len(shape))


X, Y, Z, CORE, SEQ = range(5)
EXTRA = 16
ORDERS = ((0, 2), (1, 3))


def split_parts(d):
    high = d.astype(BF).astype(F32)
    mid = (d - high).astype(BF).astype(F32)
    return high, mid, d - high - mid


def pack_kernel(q_ref, g_ref, o_ref, keep_ref, send_ref):
    low = lax.axis_index("dp") % 2 == 0
    rows = q_ref.shape[0]
    pairs = keep_ref.shape[1] // PAIR
    for p in range(pairs):
        scale = jnp.asarray(SCALE, BF)
        a, b = q_ref[:, span(2 * p)] * scale, q_ref[:, span(2 * p + 1)] * scale
        keep_ref[:rows, span(p)] = jnp.where(low, a, b)
        send_ref[:rows, span(p)] = jnp.where(low, b, a)
        a, b = g_ref[:, span(2 * p)], g_ref[:, span(2 * p + 1)]
        keep_ref[rows : 2 * rows, span(p)] = jnp.where(low, a, b)
        send_ref[rows : 2 * rows, span(p)] = jnp.where(low, b, a)
    cols = (g_ref[...].astype(F32) * o_ref[...].astype(F32)).T
    for p in range(pairs):
        both = []
        for h in range(4):
            both.append(split_parts(jnp.sum(cols[span(4 * p + h, HD)], axis=0, keepdims=True)))
        pad = [jnp.zeros((EXTRA - 6, rows), F32)]
        a = jnp.concatenate([both[h][n] for n in range(3) for h in (0, 1)] + pad, axis=0).astype(BF)
        b = jnp.concatenate([both[h][n] for n in range(3) for h in (2, 3)] + pad, axis=0).astype(BF)
        keep_ref[2 * rows :, span(p)] = jnp.where(low, a, b)
        send_ref[2 * rows :, span(p)] = jnp.where(low, b, a)


def pack(queries, grad_out, attn_out):
    rows, cols = queries.shape
    steps = 2
    block = pl.BlockSpec((rows, cols // steps), lambda i: (0, i))
    total = 2 * rows + EXTRA
    half = pl.BlockSpec((total, cols // 2 // steps), lambda i: (0, i))
    return pl.pallas_call(
        pack_kernel,
        grid=(steps,),
        in_specs=[block] * 3,
        out_specs=[half] * 2,
        out_shape=[like((total, cols // 2))] * 2,
        compiler_params=params(60),
        cost_estimate=cost(),
    )(queries, grad_out, attn_out)


def pack_tokens_kernel(at_ref, k_ref, v_ref, kp_ref, vp_ref, kt_ref):
    low = at_ref[X] == 0
    for p in range(kp_ref.shape[1] // PAIR):
        k = jnp.where(low, k_ref[:, span(2 * p)], k_ref[:, span(2 * p + 1)])
        kp_ref[:, span(p)] = k
        kt_ref[span(p)] = k.T
        vp_ref[:, span(p)] = jnp.where(low, v_ref[:, span(2 * p)], v_ref[:, span(2 * p + 1)])


def pack_tokens(at, keys, values):
    tokens, cols = keys.shape
    steps = 2
    block = pl.BlockSpec((tokens, cols // steps), lambda i: (0, i))
    half = pl.BlockSpec((tokens, cols // 2 // steps), lambda i: (0, i))
    return pl.pallas_call(
        pack_tokens_kernel,
        grid=(steps,),
        in_specs=[SMEM, block, block],
        out_specs=[half, half, pl.BlockSpec((cols // 2 // steps, tokens), lambda i: (i, 0))],
        out_shape=[like((tokens, cols // 2))] * 2 + [like((cols // 2, tokens))],
        compiler_params=params(),
        cost_estimate=cost(),
    )(at, keys, values)


def add_kernel(*refs):
    total = refs[0][...].astype(F32)
    for r in refs[1:-1]:
        total = total + r[...].astype(F32)
    refs[-1][...] = total.astype(BF)


def add(*parts):
    return pl.pallas_call(
        add_kernel,
        in_specs=[VMEM] * len(parts),
        out_specs=VMEM,
        out_shape=like(parts[0].shape),
        compiler_params=params(),
        cost_estimate=cost(),
    )(*parts)


def add_turned_kernel(own_ref, got_ref, out_ref):
    rows = own_ref.shape[0] // 2
    for n in range(2):
        total = own_ref[span(n, rows)].astype(F32) + got_ref[span(1 - n, rows)].astype(F32)
        out_ref[span(n, rows)] = total.astype(BF)


def add_turned(own, got):
    return pl.pallas_call(
        add_turned_kernel,
        in_specs=[VMEM] * 2,
        out_specs=VMEM,
        out_shape=like(own.shape),
        compiler_params=params(),
        cost_estimate=cost(),
    )(own, got)


def stack_kernel(cuts, *refs):
    out_ref, row = refs[-1], 0
    for r, cut in zip(refs[:-1], cuts, strict=True):
        block = r[...] if cut is None else r[cut]
        out_ref[row : row + block.shape[0], :] = block
        row += block.shape[0]


def stack(parts, cuts=None):
    cuts = cuts or [None] * len(parts)
    shapes = [jax.eval_shape(lambda t, c=c: t if c is None else t[c], t).shape for t, c in zip(parts, cuts, strict=True)]
    rows, width = sum(t[0] for t in shapes), shapes[0][1]
    return pl.pallas_call(
        functools.partial(stack_kernel, cuts),
        in_specs=[VMEM] * len(parts),
        out_specs=VMEM,
        out_shape=like((rows, width)),
        compiler_params=params(),
        cost_estimate=cost(),
    )(*parts)


def side_kernel(count, step, last, *refs):
    q_refs, k_ref = refs[:count], refs[count]
    if last:
        la_ref, p_ref, m_ref, lse_ref, send_ref = refs[count + 1 :]
    else:
        p_ref, m_ref, lse_ref = refs[count + 1 :]
    for j in range(step):
        q = jnp.concatenate([r[: (r.shape[0] - EXTRA) // 2, span(j)] for r in q_refs], axis=0)
        k = k_ref[:, span(j)]
        for head in range(2):
            s = dot(own_lanes(k, head), q, 1, 1)
            top = jnp.max(s, axis=0, keepdims=True)
            p = jnp.exp(s - top)
            total = jnp.sum(p, axis=0, keepdims=True)
            p_ref[2 * j + head] = p.astype(BF)
            m_ref[j, head] = top[0]
            lse_ref[j, head] = (top + jnp.log(total))[0]
    if last:
        send_ref[...] = jnp.concatenate([flip_core(la_ref[...]), flip_core(lse_ref[...])], axis=-1)


def side_of(pieces, keys, extra=None):
    count = len(pieces)
    cols = pieces[0].shape[1]
    tokens = keys.shape[0]
    piece = (pieces[0].shape[0] - EXTRA) // 2
    rows, pairs = piece * count, cols // PAIR
    in_specs, out_specs = [VMEM] * (count + 1), [VMEM] * 3
    out_shape = [like((2 * pairs, tokens, rows)), like((pairs, 2, rows), F32), like((pairs, 2, rows), F32)]
    args = [*pieces, keys]
    if extra is not None:
        in_specs += [VMEM]
        out_specs += [VMEM]
        out_shape += [like((pairs, 2, 2 * rows), F32)]
        args += [extra]
    return pl.pallas_call(
        functools.partial(side_kernel, count, pairs, extra is not None),
        in_specs=in_specs,
        out_specs=out_specs,
        out_shape=out_shape,
        compiler_params=params(),
        cost_estimate=cost(2 * rows * tokens * cols, 4 * rows * tokens * pairs, 2 * rows * tokens * pairs),
    )(*args)


def log_add(a, b):
    top = jnp.maximum(a, b)
    return top + jnp.log(jnp.exp(a - top) + jnp.exp(b - top))


def merge_kernel(la_ref, lb_ref, got_ref, send_ref):
    side = la_ref.shape[2]
    send_ref[:, :, :side] = log_add(lb_ref[...], got_ref[:, :, side:])
    send_ref[:, :, side:] = log_add(la_ref[...], got_ref[:, :, :side])


def merge(la, lb, got):
    pairs, two, side = la.shape
    return pl.pallas_call(
        merge_kernel,
        in_specs=[VMEM] * 3,
        out_specs=VMEM,
        out_shape=like((pairs, two, 2 * side), F32),
        compiler_params=params(),
        cost_estimate=cost(1000, 100000),
    )(la, lb, got)


def half_kernel(count, own, at_ref, *refs):
    row_refs = refs[:count]
    piece = (row_refs[0].shape[0] - EXTRA) // 2
    pa_ref, pb_ref, v_ref, kt_ref, ma_ref, mb_ref, sent_ref, got_ref = refs[count : count + 8]
    kv_refs, dqs_ref, dqk_ref = refs[count + 8 : -2], refs[-2], refs[-1]
    side = ma_ref.shape[2]
    z = at_ref[Z]
    first = lax.broadcasted_iota(jnp.int32, (PAIR, side), 0) < HD
    for i in range(2):
        bit = (i + 1 + at_ref[CORE]) % 2
        pair = 2 * (at_ref[Y] if own else 1 - at_ref[Y]) + bit
        lanes = pl.ds(pl.multiple_of(pair * PAIR, PAIR), PAIR)
        v = v_ref[:, lanes]
        tokens = v.shape[0]
        dk = jnp.zeros((tokens, PAIR), F32)
        dv = jnp.zeros((tokens, PAIR), F32)
        halves = []
        for b, p_ref, m_ref in ((0, pa_ref, ma_ref), (1, pb_ref, mb_ref)):
            lse = log_add(sent_ref[pair, :, span(1 - b, side)], got_ref[pair, :, span(b, side)])
            w = jnp.exp(m_ref[pair] - lse)
            wide = jnp.where(first, w[0:1], w[1:2]).T
            at = slice(b * count // 2, (b + 1) * count // 2)
            rows = [r[:, lanes] for r in row_refs[at]]
            q = jnp.concatenate([r[:piece] for r in rows], axis=0)
            g = jnp.concatenate([r[piece : 2 * piece] for r in rows], axis=0)
            parts = [r[2 * piece :].astype(F32) for r in rows]
            delta = jnp.concatenate([d[0:2] + d[2:4] + d[4:6] for d in parts], axis=1)
            qw = (q.astype(F32) * wide).astype(BF)
            gw = (g.astype(F32) * wide).astype(BF)
            parts = []
            for head in range(2):
                p = p_ref[2 * pair + head]
                dp = dot(v, own_lanes(g, head), 1, 1)
                t = (p.astype(F32) * (dp - delta[head : head + 1])).astype(BF)
                dv = dv + dot(p, own_lanes(gw, head), 1, 0)
                dk = dk + dot(t, own_lanes(qw, head), 1, 0)
                dq = dot(kt_ref[pl.ds(pl.multiple_of(pair * PAIR, PAIR) + head * HD, HD), :], t, 1, 0)
                parts.append((dq * (w[head : head + 1] * SCALE)).astype(BF))
            halves.append(jnp.concatenate(parts, axis=0))
        dq = jnp.concatenate(halves, axis=1)
        if i == 0:
            dqs_ref[...] = flip_core(dq)
        else:
            dqk_ref[...] = dq
        both = jnp.concatenate([dk.astype(BF), dv.astype(BF)], axis=0)
        size = both.shape[0] // 4
        out_lanes = pl.ds(pl.multiple_of(bit * PAIR, PAIR), PAIR)
        for ref, order in zip(kv_refs, ORDERS, strict=True):
            for n, k in enumerate(order):
                out = both[:size]
                for j in range(1, 4):
                    out = jnp.where((z ^ k) == j, both[span(j, size)], out)
                ref[span(n, size), out_lanes] = out


def half_of(at, own, pieces, pa, pb, vp, kt, ma, mb, sent, got):
    count = len(pieces)
    tokens, side = vp.shape[0], ma.shape[2]
    return pl.pallas_call(
        functools.partial(half_kernel, count, own),
        in_specs=[SMEM] + [VMEM] * (count + 8),
        out_specs=[VMEM] * 4,
        out_shape=[like((tokens, 2 * PAIR))] * 2 + [like((PAIR, 2 * side))] * 2,
        compiler_params=params(),
        cost_estimate=cost(),
    )(at, *pieces, pa, pb, vp, kt, ma, mb, sent, got)


def columns_kernel(count, high, at_ref, *refs):
    x_refs = refs[:count]
    keep_ref, core_ref, y_ref = refs[count : count + 3]
    w_refs, back_ref, send_ref, all_ref = refs[count + 3 : -3], refs[-3], refs[-2], refs[-1]
    side = keep_ref.shape[1] // 2
    far = jnp.concatenate([y_ref[:, side:], y_ref[:, :side]], axis=1)
    dq = (keep_ref[...].astype(F32) + core_ref[...].astype(F32) + far.astype(F32)).astype(BF)
    quarter = side // 2
    back_ref[...] = jnp.concatenate([dq[:, span(0, quarter)], dq[:, span(2, quarter)]], axis=1)
    send_ref[...] = jnp.concatenate([dq[:, span(1, quarter)], dq[:, span(3, quarter)]], axis=1)
    x = jnp.concatenate([r[...] for r in x_refs], axis=0)
    all_ref[...] = dot(dq, x, 1, 0)
    width = x.shape[1] // high
    for ref, order in zip(w_refs, ORDERS, strict=True):
        for n, k in enumerate(order):
            start = pl.multiple_of((at_ref[Z] ^ k) * width, PAIR)
            ref[span(n, ref.shape[0] // 2)] = all_ref[:, pl.ds(start, width)].astype(BF)


def columns_of(at, high, x_pieces, keep, core, y):
    count = len(x_pieces)
    piece, cols = x_pieces[0].shape
    width, rows = keep.shape
    return pl.pallas_call(
        functools.partial(columns_kernel, count, high),
        in_specs=[SMEM] + [VMEM] * (count + 3),
        out_specs=[VMEM] * 4,
        out_shape=[like((2 * width, cols // high))] * 2 + [like((width, rows // 2))] * 2,
        scratch_shapes=[pltpu.VMEM((width, cols), F32)],
        compiler_params=params(),
        cost_estimate=cost(2 * rows * cols * width, 2 * rows * cols),
    )(at, *x_pieces, keep, core, y)


def input_kernel(at_ref, back_ref, x_ref, y_ref, core_ref, wq_ref, out_ref, dq_ref):
    me, x = at_ref[SEQ], at_ref[X]
    size = back_ref.shape[0]

    def put(group, odd, block):
        row = pl.multiple_of((2 * group + (x ^ odd)) * size, PAIR)
        dq_ref[pl.ds(row, size), :] = block

    put(me, 0, back_ref[:, :size])
    put(me, 1, x_ref[:, :size])
    for odd in range(2):
        put(me ^ 2, odd, y_ref[span(odd, size), :size])
        put(me ^ 1, odd, core_ref[span(odd, size), :])
        put(me ^ 3, odd, core_ref[span(2 + odd, size), :])
    out_ref[...] = dot(dq_ref[...], wq_ref[...], 0, 1).astype(BF)


def input_of(at, back, x, y, core, wq):
    size, cols = back.shape[0], wq.shape[1]
    return pl.pallas_call(
        input_kernel,
        in_specs=[SMEM] + [VMEM] * 5,
        out_specs=VMEM,
        out_shape=like((size, cols)),
        scratch_shapes=[pltpu.VMEM((cols, size), BF)],
        compiler_params=params(),
        cost_estimate=cost(2 * size * cols * cols, 2 * cols * cols),
    )(at, back, x, y, core, wq)


def weight_near_kernel(own_ref, got_ref, keep_ref, send_ref):
    rows = keep_ref.shape[0]
    keep_ref[...] = own_ref[:rows].astype(F32) + got_ref[:rows].astype(F32)
    send_ref[...] = (own_ref[rows:].astype(F32) + got_ref[rows:].astype(F32)).astype(BF)


def weight_near(own, got):
    rows, cols = own.shape[0] // 2, own.shape[1]
    return pl.pallas_call(
        weight_near_kernel,
        in_specs=[VMEM] * 2,
        out_specs=[VMEM] * 2,
        out_shape=[like((rows, cols), F32), like((rows, cols))],
        compiler_params=params(),
        cost_estimate=cost(),
    )(own, got)


def weight_sum_kernel(at_ref, own_ref, got_ref, keep_ref, send_ref):
    total = own_ref[...] + got_ref[...].astype(F32)
    size = keep_ref.shape[1]
    a, b = total[:, :size], total[:, size:]
    low = at_ref[X] == 0
    keep_ref[...] = jnp.where(low, a, b)
    send_ref[...] = jnp.where(low, b, a).astype(BF)


def weight_sum(at, own, got):
    rows, cols = own.shape
    return pl.pallas_call(
        weight_sum_kernel,
        in_specs=[SMEM, VMEM, VMEM],
        out_specs=[VMEM] * 2,
        out_shape=[like((rows, cols // 2), F32), like((rows, cols // 2))],
        compiler_params=params(),
        cost_estimate=cost(),
    )(at, own, got)


def weight_out_kernel(at_ref, keep_ref, got_ref, out_ref):
    size = keep_ref.shape[0]
    a, b = keep_ref[...].T, got_ref[...].astype(F32).T
    low = at_ref[X] == 0
    out_ref[:, :size] = jnp.where(low, a, b)
    out_ref[:, size:] = jnp.where(low, b, a)


def weight_out(at, keep, got):
    size, rows = keep.shape
    return pl.pallas_call(
        weight_out_kernel,
        in_specs=[SMEM, VMEM, VMEM],
        out_specs=VMEM,
        out_shape=like((rows, 2 * size), F32),
        compiler_params=params(),
        cost_estimate=cost(1000, 300000),
    )(at, keep, got)


def tokens_kernel(at_ref, *refs):
    y, x, z = at_ref[Y], at_ref[X], at_ref[Z]
    key_ref, val_ref = refs[-2:]
    size = refs[0].shape[0] // 2
    for half in range(2):
        group = 2 * (y ^ (1 - half))
        keep, near, keep_x, near_x = refs[4 * half : 4 * half + 4]
        for i, k in enumerate(ORDERS[0] + ORDERS[1]):
            b = z ^ k
            row = pl.multiple_of((b % 2) * size, 16)
            own = (keep if i < 2 else near)[span(i % 2, size)]
            got = (keep_x if i < 2 else near_x)[span(i % 2, size)]
            for out_ref, which in ((key_ref, 0), (val_ref, 1)):

                @pl.when(b // 2 == which)
                def _():
                    for c in range(2):
                        for odd, block in ((0, own[:, span(c)]), (1, got[:, span(c)])):
                            col = pl.multiple_of((2 * (group + c) + (x ^ odd)) * PAIR, PAIR)
                            out_ref[pl.ds(row, size), pl.ds(col, PAIR)] = block


def tokens_out(at, tokens, cols, parts):
    return pl.pallas_call(
        tokens_kernel,
        in_specs=[SMEM] + [VMEM] * len(parts),
        out_specs=[VMEM] * 2,
        out_shape=[like((tokens, cols))] * 2,
        compiler_params=params(),
        cost_estimate=cost(),
    )(at, *parts)


def local_split(n_dp, n_seq, qx, queries, keys, values, attn_out, grad_out, wq):
    high = n_dp // 2
    dp, me = lax.axis_index("dp").astype(jnp.int32), lax.axis_index("seq").astype(jnp.int32)
    at = jnp.stack([dp % 2, me // 2, dp // 2, me % 2, me])
    over_x = lambda t: swap(t, "dp", n_dp, 1)
    over_y = lambda t: swap(t, "seq", n_seq, 2)
    over_core = lambda t: swap(t, "seq", n_seq, 1)
    over_z = lambda t, k: swap(t, "dp", n_dp, 2 * k)
    after = lambda t, *deps: lax.optimization_barrier((t, *deps))[0]

    def rows_of(own, from_x):
        from_y, from_xy = over_y(own), over_y(from_x)
        a = [own, over_core(own), from_x, over_core(from_x)]
        return a, from_y, from_xy

    def far_rows(from_y, from_xy):
        return [from_y, over_core(from_y), from_xy, over_core(from_xy)]

    own, send = pack(queries, grad_out, attn_out)
    kp, vp, kt = pack_tokens(at, keys, values)
    from_x = after(over_x(send), kp)
    ra, r_y, r_xy = rows_of(own, from_x)
    pa, ma, la = side_of(ra, kp)
    rb = far_rows(r_y, after(r_xy, la))
    x_y = over_y(after(qx, r_xy))
    pb, mb, lb, sent = side_of(rb, kp, la)
    x_from_x = over_x(after(qx, lb))
    send = merge(la, lb, over_core(sent))
    got = over_y(send)
    x_xy = over_y(after(x_from_x, send))
    xa = [qx, over_core(after(qx, got)), x_from_x, over_core(after(x_from_x, got))]

    def half(own, pa):
        return half_of(at, own, ra + rb, pa, pb, vp, kt, ma, mb, send, got)

    def sum_near(keep, send, *deps):
        return add(after(keep, *deps), over_z(send, 1))

    def sum_far(near):
        return add_turned(near, over_z(near, 2))

    def spread(total):
        near = over_z(total, 1)
        return [total, near, over_x(total), over_x(near)]

    kv_keep, kv_send, dq_send, dq_keep = half(False, after(pa, x_y))
    first = (kv_keep, kv_send)
    far = add(dq_keep, over_core(after(dq_send, x_from_x)))
    kv_keep, kv_send, dq_send, dq_keep = half(True, after(pa, far))
    far = over_y(far)
    first = sum_near(after(first[0], dq_keep), first[1])
    second = sum_near(kv_keep, kv_send, far)
    x_y, x_xy = after(x_y, dq_keep), after(x_xy, dq_keep)
    w_keep, w_send, back, back_s = columns_of(
        at, high, xa + far_rows(x_y, x_xy), dq_keep, over_core(dq_send), far
    )
    first, second = sum_far(first), sum_far(second)
    w_keep, w_send = weight_near(w_keep, over_z(w_send, 1))
    w_got = over_z(w_send, 2)

    from_x = over_x(back_s)
    size = back.shape[0]
    part = lambda i, n: (slice(None), slice(i * size, (i + n) * size))
    from_y = over_y(stack([back, from_x], [part(2, 2)] * 2))
    from_core = over_core(stack([back, from_x, from_y], [part(1, 1)] * 3))
    grad_input = input_of(at, back, from_x, from_y, from_core, wq)
    w_keep, w_send = weight_sum(at, after(w_keep, grad_input), w_got)
    w_got = over_x(w_send)
    first = spread(first)
    second = spread(after(second, first[2]))
    grad_keys, grad_values = tokens_out(at, *keys.shape, first + second)
    grad_weight = weight_out(at, after(w_keep, grad_keys), w_got)
    return (grad_input, grad_keys, grad_values, grad_weight)


def solution(mesh):
    n_dp, n_seq = mesh.shape["dp"], mesh.shape["seq"]

    def run(qx, queries, keys, *rest):
        pairs = queries.shape[1] == 2 * n_seq * PAIR and queries.shape[0] == n_dp * n_seq * PAIR
        split = n_seq == 4 and n_dp == 8 and pairs and (2 * keys.shape[0] // n_seq) % (16 * n_dp // 2) == 0
        return shard(local_split if split else local)(qx, queries, keys, *rest)

    def shard(f):
        return jax.shard_map(
            functools.partial(f, n_dp, n_seq),
            mesh=mesh,
            in_specs=(
                P(("dp", "seq"), None),
                P(("dp", "seq"), None),
                P("seq", None),
                P("seq", None),
                P(("dp", "seq"), None),
                P(("dp", "seq"), None),
                P(),
            ),
            out_specs=(P(("dp", "seq"), None), P("seq", None), P("seq", None), P("dp", "seq")),
            check_vma=False,
        )

    return run
```
